32 devices in a mesh: lo: 8 (over z, y), hi: 4 (over x, core).
Axes of the slice: x: 2, y: 2, z: 4, core: 2. Of those that a mesh axis runs over, the one named last changes fastest.
Arguments:
- contribution: float32 [4, 8, 1024, 1024], P('hi', 'lo'), as said below
- pivot_one: float32 [4, 8, 384, 768], P('hi', 'lo'), as said below
- rows_one: float32 [4, 8, 768, 2304], P('hi', 'lo'), as said below
- pivot_two: float32 [4, 8, 192, 768], P('hi', 'lo'), as said below
- rows_two: float32 [4, 8, 384, 2304], P('hi', 'lo'), as said below
- map_one: int32 [4, 8, 8], replicated, may hold values from 0 to 17, as said below
- map_two: int32 [4, 4, 12], replicated, may hold values from 0 to 17, as said below
- fill_one: int32 [4, 4, 12, 6], replicated, may hold values 0 or 1
- fill_two: int32 [2, 4, 12, 6], replicated, may hold values 0 or 1
- live_one: int32 [4, 4], replicated, may hold values from 3 to 6, as said below
- live_two: int32 [2, 4], replicated, may hold values from 3 to 6, as said below
Outputs:
- lower_one: float32 [4, 8, 384, 768], P('hi', 'lo')
- panel_one: float32 [4, 8, 768, 768], P('hi', 'lo')
- lower_two: float32 [4, 8, 192, 768], P('hi', 'lo')
- panel_two: float32 [4, 8, 384, 768], P('hi', 'lo')
- schur_two: float32 [4, 8, 384, 1536], P('hi', 'lo')
The draws below stay inside these ranges and needn't reach their ends.
Inputs may be any that keep to these rules, and one draw needn't show every extreme that they name: `contribution`: symmetric and negative semidefinite: minus a Gram matrix, divided by 1024. `pivot_one`: with rows_one, the rows of a symmetric matrix of each front with a dominant diagonal. `rows_one`: with pivot_one, the rows of a symmetric matrix of each front with a dominant diagonal. `pivot_two`: with rows_two, the rows of a symmetric matrix of each front with a dominant diagonal. `rows_two`: with pivot_two, the rows of a symmetric matrix of each front with a dominant diagonal. `map_one`: each device's list names 8 distinct tiles. `map_two`: each front's list names 12 distinct tiles. `live_one`: both ends reached in every draw. `live_two`: both ends reached in every draw.
All inputs are finite; a program needn't handle non-finite values.
Results may differ from the reference program's by a relative error of at most 0.0003.
Values sent between devices are 32-bit elements; how exact they have to be, the bound alone decides.
No kernel may reach another device: no remote copies, remote signals or barrier semaphores. Data moves between devices by JAX's collectives and lax.ppermute only.
A program may use at most 192 MiB of HBM per device.

```python
import math
import jax
import jax.numpy as jnp
from jax import lax

TILE = 128
CT = 8
P1T = 6
U1T = 12
P2T = 6
U2T = 12
N_LO = 8
N_HI = 4


def base_normal(key, shape):
    return jax.random.normal(key, shape, jnp.float32)


def front_blocks(key, tag, count_hi, count_lo, pivot_size, rest_size):
    sub_keys = jax.random.split(jax.random.fold_in(key, tag), 3)
    entry_scale = 1.0 / math.sqrt(pivot_size + rest_size)
    upper_part = base_normal(sub_keys[0], (count_hi, count_lo, pivot_size, pivot_size))
    pivot_part = (upper_part + jnp.swapaxes(upper_part, -1, -2)) * (entry_scale / math.sqrt(2.0)) + 12.0 * jnp.eye(pivot_size, dtype=jnp.float32)
    coupling = base_normal(sub_keys[1], (count_hi, count_lo, rest_size, pivot_size)) * entry_scale
    trailing_part = base_normal(sub_keys[2], (count_hi, count_lo, rest_size, rest_size))
    trailing_part = (trailing_part + jnp.swapaxes(trailing_part, -1, -2)) * (entry_scale / math.sqrt(2.0)) + 12.0 * jnp.eye(rest_size, dtype=jnp.float32)
    return (pivot_part, jnp.concatenate([coupling, trailing_part], axis=-1))


def split_one(fronts):
    row_count = fronts.shape[2]
    grouped = fronts.reshape(N_HI, N_LO // 2, 2, row_count // 2, fronts.shape[3])
    return grouped.transpose(0, 2, 1, 3, 4).reshape(N_HI, N_LO, row_count // 2, fronts.shape[3])


def split_two(fronts):
    row_count = fronts.shape[2]
    grouped = fronts.reshape(N_HI // 2, N_LO // 2, 2, 2, row_count // 4, fronts.shape[3])
    return grouped.transpose(2, 0, 3, 1, 4, 5).reshape(N_HI, N_LO, row_count // 4, fronts.shape[3])


def draw_contribution(key, part):
    order_size = CT * TILE
    factor_part = base_normal(jax.random.fold_in(key, 11), (N_HI, N_LO, order_size, order_size))
    return -jnp.einsum('hlik,hljk->hlij', factor_part, factor_part) / order_size


def draw_pivot_one(key, part):
    pivot_part, rows_part = front_blocks(key, 21, N_HI, N_LO // 2, P1T * TILE, U1T * TILE)
    return split_one(pivot_part)


def draw_rows_one(key, part):
    pivot_part, rows_part = front_blocks(key, 21, N_HI, N_LO // 2, P1T * TILE, U1T * TILE)
    return split_one(rows_part)


def draw_pivot_two(key, part):
    pivot_part, rows_part = front_blocks(key, 22, N_HI // 2, N_LO // 2, P2T * TILE, U2T * TILE)
    return split_two(pivot_part)


def draw_rows_two(key, part):
    pivot_part, rows_part = front_blocks(key, 22, N_HI // 2, N_LO // 2, P2T * TILE, U2T * TILE)
    return split_two(rows_part)


def draw_map_one(key, part):
    sub_keys = jax.random.split(jax.random.fold_in(key, 31), N_HI * N_LO)
    chosen = jax.vmap(lambda single: jax.random.permutation(single, P1T + U1T)[:CT])(sub_keys)
    return chosen.reshape(N_HI, N_LO, CT).astype(jnp.int32)


def draw_map_two(key, part):
    sub_keys = jax.random.split(jax.random.fold_in(key, 32), N_HI * (N_LO // 2))
    chosen = jax.vmap(lambda single: jax.random.permutation(single, P2T + U2T)[:U1T])(sub_keys)
    return chosen.reshape(N_HI, N_LO // 2, U1T).astype(jnp.int32)


def draw_live_one(key, part):
    counts = jax.random.randint(jax.random.fold_in(key, 41), (N_HI, N_LO // 2), P1T // 2, P1T + 1)
    counts = counts.at[0, 0].set(P1T).at[0, 1].set(P1T // 2)
    return counts.astype(jnp.int32)


def draw_live_two(key, part):
    counts = jax.random.randint(jax.random.fold_in(key, 42), (N_HI // 2, N_LO // 2), P2T // 2, P2T + 1)
    counts = counts.at[0, 0].set(P2T).at[0, 1].set(P2T // 2)
    return counts.astype(jnp.int32)


def plant(array, own_key, smallest, top_value):
    longest = array.shape.index(max(array.shape))
    spots = []
    for shift in (0, 1):
        where = [jax.random.randint(jax.random.fold_in(own_key, axis), (), 0, length) for axis, length in enumerate(array.shape)]
        where[longest] = (where[longest] + shift) % array.shape[longest]
        spots.append(tuple(where))
    return array.at[spots[0]].set(smallest).at[spots[1]].set(top_value)


def setup_inputs(seed: int = 0) -> dict:
    key_of = jax.random.split(jax.random.key(seed), 12)
    contribution = draw_contribution(jax.random.fold_in(key_of[11], 71), 0)
    pivot_one = draw_pivot_one(jax.random.fold_in(key_of[11], 71), 0)
    rows_one = draw_rows_one(jax.random.fold_in(key_of[11], 71), 0)
    pivot_two = draw_pivot_two(jax.random.fold_in(key_of[11], 71), 0)
    rows_two = draw_rows_two(jax.random.fold_in(key_of[11], 71), 0)
    map_one = draw_map_one(jax.random.fold_in(key_of[11], 71), 0)
    map_two = draw_map_two(jax.random.fold_in(key_of[11], 71), 0)
    fill_one = plant((jax.random.randint(key_of[7], (N_HI, N_LO // 2, U1T, P1T), 0, 3) < 2).astype(jnp.int32), jax.random.fold_in(key_of[7], 1), 0, 1)
    fill_two = plant((jax.random.randint(key_of[8], (N_HI // 2, N_LO // 2, U2T, P2T), 0, 3) < 2).astype(jnp.int32), jax.random.fold_in(key_of[8], 1), 0, 1)
    live_one = draw_live_one(jax.random.fold_in(key_of[11], 71), 0)
    live_two = draw_live_two(jax.random.fold_in(key_of[11], 71), 0)
    return {"contribution": contribution, "pivot_one": pivot_one, "rows_one": rows_one, "pivot_two": pivot_two, "rows_two": rows_two, "map_one": map_one, "map_two": map_two, "fill_one": fill_one, "fill_two": fill_two, "live_one": live_one, "live_two": live_two}


HIGHEST_MODE = lax.Precision.HIGHEST

def spread(source_block, row_map, col_map, row_first, row_tiles, col_tiles):
    row_count = row_map.shape[0]
    col_count = col_map.shape[0]
    tile_size = source_block.shape[1] // col_count
    targets = row_first + jnp.arange(row_tiles, dtype=jnp.int32)
    row_onehot = (row_map[:, None] == targets[None, :]).astype(jnp.float32)
    col_onehot = (col_map[:, None] == jnp.arange(col_tiles, dtype=jnp.int32)[None, :]).astype(jnp.float32)
    blocks = source_block.reshape(row_count, tile_size, col_count, tile_size)
    placed = jnp.einsum('ia,ixky->axky', row_onehot, blocks, precision=HIGHEST_MODE)
    placed = jnp.einsum('axky,kb->axby', placed, col_onehot, precision=HIGHEST_MODE)
    return placed.reshape(row_tiles * tile_size, col_tiles * tile_size)

def factor(pivot_block, coupling, live_tiles):
    kept = (jnp.arange(pivot_block.shape[0]) // TILE < live_tiles).astype(pivot_block.dtype)
    pivot_block = pivot_block * kept[:, None] * kept[None, :] + jnp.diag(1.0 - kept)
    coupling = coupling * kept[None, :]
    factor_lower = jnp.linalg.cholesky(pivot_block)
    panel_part = lax.linalg.triangular_solve(factor_lower, coupling, left_side=False, lower=True, transpose_a=True)
    return (factor_lower, panel_part)

def expand_fill(fill_tiles):
    return jnp.repeat(jnp.repeat(fill_tiles, TILE, axis=0), TILE, axis=1).astype(jnp.float32)

def to_fronts(values_in):
    grouped = values_in.reshape((2, N_HI // 2, 2, N_LO // 2) + values_in.shape[2:])
    axes_order = (1, 3, 0, 2) + tuple(range(4, grouped.ndim))
    return grouped.transpose(axes_order)

def table_fronts(table_in):
    grouped = table_in.reshape((2, N_HI // 2) + table_in.shape[1:])
    return jnp.moveaxis(grouped, 0, 2)

def to_devices(stacked):
    grouped = stacked.reshape((N_HI // 2, N_LO // 2) + stacked.shape[1:])
    axes_order = (2, 0, 3, 1) + tuple(range(4, grouped.ndim))
    return grouped.transpose(axes_order).reshape((N_HI, N_LO) + grouped.shape[4:])

def one_quad(quad_items):
    blocks, maps_first, maps_second, pivots_first, rows_first, fills_first, lives_first, pivots_second, rows_second, fill_second, live_second = quad_items
    pivot_size = P1T * TILE
    rest_size = U1T * TILE
    second_size = P2T * TILE
    second_rest = U2T * TILE
    lowers = []
    panels = []
    schurs = []
    for which_side in range(2):
        pivot_block = pivots_first[which_side].reshape(pivot_size, pivot_size)
        front_rows = rows_first[which_side].reshape(rest_size, pivot_size + rest_size)
        coupling = front_rows[:, :pivot_size] * expand_fill(fills_first[which_side])
        trailing = front_rows[:, pivot_size:]
        for which_half in range(2):
            child_block = blocks[which_side, which_half]
            child_map = maps_first[which_side, which_half]
            pivot_block = pivot_block + spread(child_block, child_map, child_map, 0, P1T, P1T)
            placed_rows = spread(child_block, child_map, child_map, P1T, U1T, P1T + U1T)
            coupling = coupling + placed_rows[:, :pivot_size]
            trailing = trailing + placed_rows[:, pivot_size:]
        factor_lower, panel_part = factor(pivot_block, coupling, lives_first[which_side])
        schurs.append(trailing - jnp.dot(panel_part, panel_part.T, precision=HIGHEST_MODE))
        lowers.append(factor_lower.reshape(2, pivot_size // 2, pivot_size))
        panels.append(panel_part.reshape(2, rest_size // 2, pivot_size))
    pivot_block = pivots_second.reshape(second_size, second_size)
    front_rows = rows_second.reshape(second_rest, second_size + second_rest)
    coupling = front_rows[:, :second_size] * expand_fill(fill_second)
    trailing = front_rows[:, second_size:]
    for which_side in range(2):
        child_map = maps_second[which_side]
        pivot_block = pivot_block + spread(schurs[which_side], child_map, child_map, 0, P2T, P2T)
        placed_rows = spread(schurs[which_side], child_map, child_map, P2T, U2T, P2T + U2T)
        coupling = coupling + placed_rows[:, :second_size]
        trailing = trailing + placed_rows[:, second_size:]
    lower_full, panel_full = factor(pivot_block, coupling, live_second)
    schur_full = trailing - jnp.dot(panel_full, panel_full.T, precision=HIGHEST_MODE)
    return (jnp.stack(lowers), jnp.stack(panels), lower_full.reshape(2, 2, second_size // 4, second_size), panel_full.reshape(2, 2, second_rest // 4, second_size), schur_full.reshape(2, 2, second_rest // 4, second_rest))

def reference(contribution, pivot_one, rows_one, pivot_two, rows_two, map_one, map_two, fill_one, fill_two, live_one, live_two):
    quad_items = (to_fronts(contribution), to_fronts(map_one), table_fronts(map_two), to_fronts(pivot_one), to_fronts(rows_one), table_fronts(fill_one), table_fronts(live_one), to_fronts(pivot_two), to_fronts(rows_two), fill_two, live_two)
    flat_items = jax.tree.map(lambda member: member.reshape((-1,) + member.shape[2:]), quad_items)
    quad_results = lax.map(one_quad, flat_items)
    lower_first, panel_first, lower_second, panel_second, schur_second = quad_results
    return (to_devices(lower_first), to_devices(panel_first), to_devices(lower_second), to_devices(panel_second), to_devices(schur_second))
```

```python
import jax
import jax.numpy as jnp
import numpy as np
from jax import lax
from jax.experimental import pallas as pl
from jax.experimental.pallas import tpu as pltpu
from jax.sharding import PartitionSpec as P

TILE = 128
HALF = TILE // 2
CT = 8
P1T = 6
U1T = 12
P2T = 6
U2T = 12
ROWS = 8

HALF_U = U1T // 2
QUARTER = U2T // 4
PIVOT = P1T * TILE
SECOND = P2T * TILE

TRI_C = [(a, b) for a in range(CT) for b in range(a + 1)]
TRI_U = [(a, b) for a in range(HALF_U) for b in range(a + 1)]
TRI_P = [(a, b) for a in range(P1T // 2) for b in range(a + 1)]
N_OFF = (P1T // 2) ** 2
N_PIV = P1T * P1T
N_COUP = HALF_U * P1T
N_TRI = len(TRI_U)
N_CROSS = HALF_U * HALF_U
S_COUP = N_PIV
S_OWN = S_COUP + N_COUP
S_FAR = S_OWN + N_TRI
S_CROSS = S_FAR + N_COUP
S_OTH = S_CROSS + N_CROSS
N_FRONT = S_OTH + N_TRI
G_COUP = P2T * P2T
G_TRAIL = G_COUP + U2T * P2T
G_NONE = G_TRAIL + QUARTER * U2T

NT = (((1,), (1,)), ((), ()))
NN = (((1,), (0,)), ((), ()))
F32 = jnp.float32


def split(x):
    high = x.astype(jnp.bfloat16)
    return high, (x - high.astype(F32)).astype(jnp.bfloat16)


def dot3(a, b, dims):
    def one(p, q):
        return lax.dot_general(p, q, dims, preferred_element_type=F32)

    return one(a[0], b[0]) + (one(a[0], b[1]) + one(a[1], b[0]))


def mul(a, b, dims):
    return dot3(split(a), split(b), dims)


def factor_half(block, width):
    groups = HALF // ROWS
    sub = lax.broadcasted_iota(jnp.int32, (ROWS, TILE), 0)
    lane = lax.broadcasted_iota(jnp.int32, (ROWS, TILE), 1)

    def full(x):
        return jnp.broadcast_to(x, (ROWS, TILE))

    wide = jnp.concatenate([block, jnp.zeros((HALF, HALF), F32)], axis=1)
    a = [
        jnp.where(lane == sub + ROWS * g + HALF, 1.0, wide[ROWS * g : ROWS * g + ROWS])
        for g in range(groups)
    ]
    rows = [None] * HALF
    for j in range(0, HALF, width):
        gj, o = j // ROWS, j % ROWS
        cols = {g: [full(a[g][:, j + i : j + i + 1]) for i in range(width)] for g in range(gj, groups)}
        s = [
            [full(cols[gj][k][o + i : o + i + 1, :]) if k <= i else None for k in range(width)]
            for i in range(width)
        ]
        u = [full(a[gj][o + i : o + i + 1, :]) for i in range(width)]
        inv = [None] * width
        low = [[None] * width for _ in range(width)]
        for k in range(width):
            inv[k] = 1.0 / s[k][k]
            for i in range(k + 1, width):
                low[i][k] = s[i][k] * inv[k]
            for i in range(k + 1, width):
                for q in range(k + 1, i + 1):
                    s[i][q] = s[i][q] - low[i][k] * s[q][k]
        for i in range(width):
            for k in range(i):
                u[i] = u[i] - low[i][k] * u[k]
            rows[j + i] = u[i] * lax.rsqrt(s[i][i])
        scaled = [u[i] * inv[i] for i in range(width)]
        for g in range(gj if o + width < ROWS else gj + 1, groups):
            c = cols[g]
            for i in range(width):
                for k in range(i):
                    c[i] = c[i] - c[k] * low[i][k]
            for i in range(width):
                a[g] = a[g] - c[i] * scaled[i]
    out = []
    for g in range(groups):
        v = rows[ROWS * g]
        for i in range(1, ROWS):
            v = jnp.where(sub == i, rows[ROWS * g + i], v)
        out.append(v)
    both = jnp.concatenate(out, axis=0)
    return both[:, :HALF], both[:, HALF:]


def factor(a, low, inv, tiles, width):
    d = a[0:TILE, 0:TILE]
    zero = jnp.zeros((HALF, HALF), F32)
    ri = lax.broadcasted_iota(jnp.int32, (HALF, HALF), 0)
    ci = lax.broadcasted_iota(jnp.int32, (HALF, HALF), 1)
    for k in range(tiles):
        k0, k1, k2 = k * TILE, (k + 1) * TILE, (k + 2) * TILE
        u1, w1 = factor_half(d[:HALF, :HALF], width)
        l21 = mul(d[HALF:, :HALF], w1, NT)
        u2, w2 = factor_half(d[HALF:, HALF:] - mul(l21, l21, NT), width)
        w21 = -mul(w2, mul(l21, w1, NN), NN)
        w = jnp.concatenate([jnp.concatenate([w1, zero], 1), jnp.concatenate([w21, w2], 1)], 0)
        ws = split(w)
        inv[k0:k1, k0:k1] = w
        if k + 1 < tiles:
            p = dot3(split(a[k1:k2, k0:k1]), ws, NT)
            low[k1:k2, k0:k1] = p
            ps = split(p)
            d = a[k1:k2, k1:k2] - dot3(ps, ps, NT)
        l1 = jnp.where(ri >= ci, u1.T, 0.0)
        l2 = jnp.where(ri >= ci, u2.T, 0.0)
        low[k0:k1, k0:k1] = jnp.concatenate(
            [jnp.concatenate([l1, zero], 1), jnp.concatenate([l21, l2], 1)], 0
        )
        if k + 2 < tiles:
            low[k2:, k0:k1] = dot3(split(a[k2:, k0:k1]), ws, NT)
            for j in range(k + 1, tiles):
                j0 = j * TILE
                top = max(j0, k2)
                a[top:, j0 : j0 + TILE] = a[top:, j0 : j0 + TILE] - mul(
                    low[top:, k0:k1], low[j0 : j0 + TILE, k0:k1], NT
                )
        if k > 0:
            x = mul(low[k0:k1, 0:k0], inv[0:k0, 0:k0], NN)
            inv[k0:k1, 0:k0] = -dot3(ws, split(x), NN)
        if k + 1 < tiles:
            rest = jnp.zeros((TILE, (tiles - k - 1) * TILE), F32)
            low[k0:k1, k1:] = rest
            inv[k0:k1, k1:] = rest


def padded(a, tile_of, live, tiles):
    ri = lax.broadcasted_iota(jnp.int32, (TILE, TILE), 0)
    ci = lax.broadcasted_iota(jnp.int32, (TILE, TILE), 1)
    eye = jnp.where(ri == ci, 1.0, 0.0)
    for i in range(tiles):
        kept = (jnp.int32(i) < live).astype(F32)
        for j in range(i + 1):
            value = tile_of(i, j) * kept
            if i == j:
                value = value + eye * (1.0 - kept)
            a[i * TILE : (i + 1) * TILE, j * TILE : (j + 1) * TILE] = value


def copy_all(pairs, sems):
    copies = [pltpu.make_async_copy(src, dst, sems.at[n]) for n, (src, dst) in enumerate(pairs)]
    for c in copies:
        c.start()
    for c in copies:
        c.wait()


def tile_at(ref, row, col):
    return ref.at[
        pl.ds(pl.multiple_of(row * TILE, TILE), TILE), pl.ds(pl.multiple_of(col * TILE, TILE), TILE)
    ]


def pack_first(tab, block, pivot, out, sems):
    side = tab[CT]
    pairs = []
    for n, (a, b) in enumerate(TRI_C):
        pairs.append((tile_at(block, tab[a], tab[b]), out.at[n]))
    for n, (a, b) in enumerate(TRI_P):
        pairs.append((tile_at(pivot, a, side * (P1T // 2) + b), out.at[len(TRI_C) + n]))
    copy_all(pairs, sems)


def pack_rest(tab, block, pivot, rows, second, coup, own, kept, cross, off, coup_two, sems):
    side = tab[CT]
    order = CT + 1
    local = order + CT
    pairs = []
    for r in range(HALF_U):
        row = tab[local + r] - side * HALF_U
        for c in range(P1T):
            pairs.append((tile_at(rows, row, c), coup.at[r * P1T + c]))
    for n, (a, b) in enumerate(TRI_U):
        row = tab[local + a] - side * HALF_U
        pairs.append((tile_at(rows, row, P1T + tab[local + b]), own.at[n]))
    for n, (a, b) in enumerate(TRI_C):
        pairs.append((tile_at(block, tab[order + a], tab[order + b]), kept.at[n]))
    for i in range(HALF_U):
        row = tab[local + i] - side * HALF_U
        for k in range(HALF_U):
            pairs.append(
                (tile_at(rows, row, P1T + tab[local + HALF_U + k]), cross.at[i * HALF_U + k])
            )
    for i in range(P1T // 2):
        for k in range(P1T // 2):
            pairs.append(
                (tile_at(pivot, i, (1 - side) * (P1T // 2) + k), off.at[i * (P1T // 2) + k])
            )
    for n, (i, k) in enumerate(TRI_P):
        pairs.append((tile_at(pivot, i, side * (P1T // 2) + k), off.at[N_OFF + n]))
    for r in range(QUARTER):
        for c in range(P2T):
            pairs.append((tile_at(second, r, c), coup_two.at[r * P2T + c]))
    copy_all(pairs, sems)


T_SIDE = 0
T_LIVE = 1
T_LOCAL = 2
T_FILL = T_LOCAL + U1T
T_SLOT = T_FILL + U1T * P1T
T_SLOT_FAR = T_SLOT + len(TRI_C)


def panel_rows(tile_of, count, live, inv, put):
    parts = split(inv)
    for r in range(0, count, 2):
        block = jnp.concatenate(
            [
                jnp.concatenate([tile_of(r + i, c) for c in range(P1T)], axis=1)
                for i in range(2)
            ],
            axis=0,
        )
        lane = lax.broadcasted_iota(jnp.int32, block.shape, 1)
        block = jnp.where(lane < live * TILE, block, 0.0)
        put(r, dot3(split(block), parts, NT))


def first_kernel(
    tab, mine, theirs, coup, own, cross, off,
    lower_out, inv_out, panel_out, rows_out, own_out, far_out,
    front, a, low, sem,
):
    side = tab[T_SIDE]
    live = tab[T_LIVE]
    half = P1T // 2
    front[0:N_PIV] = jnp.zeros((N_PIV, TILE, TILE), F32)
    for n, (i, k) in enumerate(TRI_P):
        front[(side * half + i) * P1T + side * half + k] = off[N_OFF + n]
        front[((1 - side) * half + i) * P1T + (1 - side) * half + k] = theirs[len(TRI_C) + n]
    for i in range(half):
        for k in range(half):

            @pl.when(side == 0)
            def _():
                front[(half + k) * P1T + i] = off[i * half + k].T

            @pl.when(side != 0)
            def _():
                front[(half + i) * P1T + k] = off[i * half + k]

    def scale(n, carry):
        front[S_COUP + n] = coup[n] * tab[T_FILL + n].astype(F32)
        front[S_FAR + n] = jnp.zeros((TILE, TILE), F32)
        front[S_CROSS + n] = cross[n]
        return carry

    lax.fori_loop(0, N_COUP, scale, 0)

    def copy(n, carry):
        front[S_OWN + n] = own[n]
        front[S_OTH + n] = jnp.zeros((TILE, TILE), F32)
        return carry

    lax.fori_loop(0, N_TRI, copy, 0)

    def extend(n, carry):
        here = tab[T_SLOT + n]
        front[here] = front[here] + mine[n]
        there = tab[T_SLOT_FAR + n]
        front[there] = front[there] + theirs[n]
        return carry

    lax.fori_loop(0, len(TRI_C), extend, 0)
    leave = pltpu.make_async_copy(front.at[pl.ds(S_FAR, N_FRONT - S_FAR)], far_out, sem)
    leave.start()
    padded(a, lambda i, j: front[i * P1T + j], live, P1T)
    factor(a, low, inv_out, P1T, 4)
    lower_out[...] = low[pl.ds(pl.multiple_of(side * (PIVOT // 2), TILE), PIVOT // 2), :]

    def put(r, rows):
        panel_out[r * TILE : (r + 2) * TILE, :] = rows
        for i in range(2):
            place = tab[T_LOCAL + r + i] - side * HALF_U
            rows_out[pl.ds(pl.multiple_of(place * TILE, TILE), TILE), :] = rows[
                i * TILE : (i + 1) * TILE
            ]

    panel_rows(lambda r, c: front[S_COUP + r * P1T + c], HALF_U, live, inv_out[...], put)
    for i in range(HALF_U):
        left = split(panel_out[i * TILE : (i + 1) * TILE, :])
        product = dot3(left, split(panel_out[0 : (i + 1) * TILE, :]), NT)
        for k in range(i + 1):
            n = i * (i + 1) // 2 + k
            own_out[n] = front[S_OWN + n] - product[:, k * TILE : (k + 1) * TILE]
    leave.wait()


def second_kernel(tab, far, coup, inv, panel, cross_out, oth_out, panel_far):
    live = tab[T_LIVE]

    def tile_of(r, c):
        n = r * P1T + c
        return far[n] + coup[n] * tab[T_FILL + N_COUP + n].astype(F32)

    def put(r, rows):
        panel_far[r * TILE : (r + 2) * TILE, :] = rows

    panel_rows(tile_of, HALF_U, live, inv[...], put)
    right = split(panel_far[...])
    for i in range(0, HALF_U, 2):
        product = dot3(split(panel[i * TILE : (i + 2) * TILE, :]), right, NT)
        for q in range(2):
            for k in range(HALF_U):
                n = (i + q) * HALF_U + k
                cross_out[n] = (
                    far[N_COUP + n]
                    - product[q * TILE : (q + 1) * TILE, k * TILE : (k + 1) * TILE]
                )
    for i in range(HALF_U):
        left = split(panel_far[i * TILE : (i + 1) * TILE, :])
        product = dot3(left, split(panel_far[0 : (i + 1) * TILE, :]), NT)
        for k in range(i + 1):
            n = i * (i + 1) // 2 + k
            oth_out[n] = far[N_COUP + N_CROSS + n] - product[:, k * TILE : (k + 1) * TILE]


Q_LIVE = 0
Q_MINE = 1
Q_FILL = 5
Q_DIRECT = Q_FILL + U2T * P2T
N_S1 = 2 * N_TRI + N_CROSS
Q_TURNED = Q_DIRECT + 2 * N_S1


def third_kernel(
    tab, own0, cross0, oth0, own1, cross1, oth1, piv0, piv1, piv2, piv3, second,
    lower_out, inv_out, g_out,
    g, a, low, sem,
):
    units = SECOND // 4 // HALF
    for s, piv in enumerate((piv0, piv1, piv2, piv3)):
        for i in range(units):
            unit = tab[Q_MINE + s] * units + i
            row = unit // 2
            start = pl.multiple_of((unit % 2) * HALF, HALF)
            for c in range(P2T):
                g[row * P2T + c, pl.ds(start, HALF), :] = piv[
                    i * HALF : (i + 1) * HALF, c * TILE : (c + 1) * TILE
                ]

    def clear(n, carry):
        g[G_COUP + n] = jnp.zeros((TILE, TILE), F32)
        return carry

    lax.fori_loop(0, U2T * P2T, clear, 0)
    for r in range(QUARTER):
        for c in range(U2T):
            g[G_TRAIL + r * U2T + c] = second[
                r * TILE : (r + 1) * TILE, SECOND + c * TILE : SECOND + (c + 1) * TILE
            ]
    first = 0
    for ref in (own0, cross0, oth0, own1, cross1, oth1):

        def extend(n, carry, ref=ref, first=first):
            direct = tab[Q_DIRECT + first + n]
            turned = tab[Q_TURNED + first + n]
            g[direct] = g[direct] + ref[n]

            @pl.when(turned != G_NONE)
            def _():
                g[turned] = g[turned] + ref[n].T

            return carry

        lax.fori_loop(0, ref.shape[0], extend, 0)
        first += ref.shape[0]
    leave = pltpu.make_async_copy(g.at[pl.ds(G_COUP, G_NONE - G_COUP)], g_out, sem)
    leave.start()
    padded(a, lambda i, j: g[i * P2T + j], tab[Q_LIVE], P2T)
    factor(a, low, inv_out, P2T, 8)
    start = tab[Q_MINE] * (SECOND // 4)
    lower_out[...] = low[pl.ds(pl.multiple_of(start, HALF), SECOND // 4), :]
    leave.wait()


def last_kernel(tab, g, inv, coup0, coup1, coup2, coup3, panel_out, schur_out, panels):
    live = tab[Q_LIVE]
    parts = split(inv[...])
    for s, coup in enumerate((coup0, coup1, coup2, coup3)):
        quarter = tab[Q_MINE + s]
        rows = []
        for r in range(QUARTER):
            row = quarter * QUARTER + r
            rows.append(
                jnp.concatenate(
                    [
                        g[row * P2T + c]
                        + coup[r * P2T + c] * tab[Q_FILL + row * P2T + c].astype(F32)
                        for c in range(P2T)
                    ],
                    axis=1,
                )
            )
        block = jnp.concatenate(rows, axis=0)
        lane = lax.broadcasted_iota(jnp.int32, block.shape, 1)
        block = jnp.where(lane < live * TILE, block, 0.0)
        panel = dot3(split(block), parts, NT)
        panels[quarter] = panel
        if s == 0:
            panel_out[...] = panel
    left = split(panel_out[...])
    wide = QUARTER * TILE
    for q in range(4):
        product = dot3(left, split(panels[q]), NT)
        for r in range(QUARTER):
            for c in range(QUARTER):
                col = q * QUARTER + c
                schur_out[r * TILE : (r + 1) * TILE, col * TILE : (col + 1) * TILE] = (
                    g[G_TRAIL - G_COUP + r * U2T + col]
                    - product[r * TILE : (r + 1) * TILE, c * TILE : (c + 1) * TILE]
                )


def swap(array, axis):
    size = lax.axis_size(axis)
    return lax.ppermute(array, axis, [(i, i ^ (size // 2)) for i in range(size)])


def tiles(count):
    return jax.ShapeDtypeStruct((count, TILE, TILE), F32)


def dense(rows, cols):
    return jax.ShapeDtypeStruct((rows, cols), F32)


SMEM = pl.BlockSpec(memory_space=pltpu.SMEM)
VMEM = pl.BlockSpec(memory_space=pltpu.VMEM)
HBM = pl.BlockSpec(memory_space=pl.ANY)
LIMIT = 56 << 20


def cost(flops, count):
    return pl.CostEstimate(flops=flops, bytes_accessed=count * TILE * TILE * 4, transcendentals=0)


def tri(i, k):
    return i * (i + 1) // 2 + k


def local_order(second_map, side):
    unit = jnp.arange(U1T, dtype=jnp.int32)
    rank = second_map + jnp.where(unit // HALF_U == side, 0, P2T + U2T)
    place = jnp.sum((rank[None, :] < rank[:, None]).astype(jnp.int32), axis=1)
    hit = (place[None, :] == unit[:, None]).astype(jnp.int32)
    return place, hit


def place_of(child_map, place):
    unit = jnp.arange(U1T, dtype=jnp.int32)
    hit = (child_map[:, None] - P1T == unit[None, :]).astype(jnp.int32)
    return jnp.where(child_map < P1T, child_map, P1T + jnp.sum(hit * place[None, :], axis=1))


def sort_by(key):
    spot = jnp.sum((key[None, :] < key[:, None]).astype(jnp.int32), axis=1)
    hit = (spot[None, :] == jnp.arange(CT, dtype=jnp.int32)[:, None]).astype(jnp.int32)
    order = jnp.sum(hit * jnp.arange(CT, dtype=jnp.int32)[None, :], axis=1)
    return order, jnp.sum(hit * key[None, :], axis=1)


def turned_key(key):
    return jnp.where(key < P1T, key, P1T + (key - P1T + HALF_U) % U1T)


def slots(keys):
    row = keys[np.array([a for a, b in TRI_C])]
    col = keys[np.array([b for a, b in TRI_C])]
    own = P1T + HALF_U
    pivot = row * P1T + col
    coup = jnp.where(row >= own, S_COUP + (row - own) * P1T, S_FAR + (row - P1T) * P1T) + col
    near = S_OWN + tri(row - own, col - own)
    cross = S_CROSS + (row - own) * HALF_U + col - P1T
    other = S_OTH + tri(row - P1T, col - P1T)
    rest = jnp.where(row < own, other, jnp.where(col < own, cross, near))
    return jnp.where(row < P1T, pivot, jnp.where(col < P1T, coup, rest))


PAIRS = (
    TRI_U
    + [(i, HALF_U + k) for i in range(HALF_U) for k in range(HALF_U)]
    + [(HALF_U + i, HALF_U + k) for i, k in TRI_U]
)


def targets(goal, quarter):
    row = goal[np.array([a for a, b in PAIRS])]
    col = goal[np.array([b for a, b in PAIRS])]

    def index(r, c):
        mine = (r - P2T) // QUARTER == quarter
        coup = G_COUP + (r - P2T) * P2T + c
        trail = G_TRAIL + (r - P2T - quarter * QUARTER) * U2T + c - P2T
        rest = jnp.where(c < P2T, coup, jnp.where(mine, trail, G_NONE))
        return jnp.where(r < P2T, jnp.where((c < P2T) & (r >= c), r * P2T + c, G_NONE), rest)

    direct = index(row, col)
    return direct, jnp.where(row == col, G_NONE, index(col, row))


def body(
    contribution,
    pivot_one,
    rows_one,
    pivot_two,
    rows_two,
    map_one,
    map_two,
    fill_one,
    fill_two,
    live_one,
    live_two,
):
    size_lo = lax.axis_size("lo")
    size_hi = lax.axis_size("hi")
    half_lo = size_lo // 2
    half_hi = size_hi // 2
    index_lo = lax.axis_index("lo")
    index_hi = lax.axis_index("hi")
    side_lo = index_lo // half_lo
    side_hi = index_hi // half_hi
    front_lo = index_lo % half_lo
    front_hi = index_hi % half_hi
    far_lo = (index_lo + half_lo) % size_lo
    far_hi = (index_hi + half_hi) % size_hi
    block, pivot, rows = contribution[0, 0], pivot_one[0, 0], rows_one[0, 0]
    pivot_second, rows_second = pivot_two[0, 0], rows_two[0, 0]
    params = pltpu.CompilerParams(vmem_limit_bytes=LIMIT)

    second_map = map_two[index_hi, front_lo]
    place, hit = local_order(second_map, side_lo)
    key = place_of(map_one[index_hi, index_lo], place)
    order_sent, _ = sort_by(key)
    tab_first = jnp.concatenate([order_sent, side_lo[None]]).astype(jnp.int32)
    n_first = len(TRI_C) + len(TRI_P)
    sent = pl.pallas_call(
        pack_first,
        out_shape=tiles(n_first),
        in_specs=[SMEM, HBM, HBM],
        out_specs=HBM,
        scratch_shapes=[pltpu.SemaphoreType.DMA((n_first,))],
        name="pack_first",
        compiler_params=params,
        cost_estimate=cost(0, 2 * n_first),
    )(tab_first, block, pivot)
    got_first = swap(sent, "lo")

    unit = jnp.arange(U1T, dtype=jnp.int32)
    local = jnp.sum(hit * unit[None, :], axis=1)
    order_kept, keys = sort_by(turned_key(key))
    tab_rest = jnp.concatenate([tab_first, order_kept, local]).astype(jnp.int32)
    shapes = [tiles(N_COUP), tiles(N_TRI), tiles(len(TRI_C)), tiles(N_CROSS), tiles(N_OFF + len(TRI_P)), tiles(QUARTER * P2T)]
    n_rest = sum(s.shape[0] for s in shapes)
    coup, own, kept, cross, off, coup_two = pl.pallas_call(
        pack_rest,
        out_shape=shapes,
        in_specs=[SMEM, HBM, HBM, HBM, HBM],
        out_specs=[HBM] * len(shapes),
        scratch_shapes=[pltpu.SemaphoreType.DMA((n_rest,))],
        name="pack_rest",
        compiler_params=params,
        cost_estimate=cost(0, 2 * n_rest),
    )(tab_rest, block, pivot, rows, rows_second)
    got_coup = swap(coup, "lo")
    got_own = swap(own, "lo")
    got_pivot = swap(pivot_second, "lo")
    got_two = swap(coup_two, "lo")

    far_key = place_of(map_one[index_hi, far_lo], place)
    _, far_keys = sort_by(turned_key(far_key))
    live_first = live_one[index_hi, front_lo]
    fill_first = jnp.sum(hit[:, :, None] * fill_one[index_hi, front_lo][None, :, :], axis=1)
    tab_one = jnp.concatenate(
        [side_lo[None], live_first[None], local, fill_first.reshape(-1), slots(keys), slots(far_keys)]
    ).astype(jnp.int32)
    mega = 2 * TILE**3
    half_rows = HALF_U * TILE
    lower_one, inv_one, panel_own, panel_one, s_own, far_part = pl.pallas_call(
        first_kernel,
        out_shape=[
            dense(PIVOT // 2, PIVOT), dense(PIVOT, PIVOT), dense(half_rows, PIVOT),
            dense(half_rows, PIVOT), tiles(N_TRI), tiles(N_FRONT - S_FAR),
        ],
        in_specs=[SMEM] + [VMEM] * 6,
        out_specs=[VMEM] * 5 + [HBM],
        scratch_shapes=[
            pltpu.VMEM((N_FRONT, TILE, TILE), F32),
            pltpu.VMEM((PIVOT, PIVOT), F32),
            pltpu.VMEM((PIVOT, PIVOT), F32),
            pltpu.SemaphoreType.DMA,
        ],
        name="first_front_own",
        compiler_params=params,
        cost_estimate=cost(4000 * mega, 2 * N_FRONT),
    )(tab_one, kept, got_first, coup, own, cross, off)
    s_own_far = swap(s_own, "hi")
    pivot_hi, got_pivot_hi = swap(pivot_second, "hi"), swap(got_pivot, "hi")
    two_hi = swap(coup_two, "hi")

    s_cross, s_part = pl.pallas_call(
        second_kernel,
        out_shape=[tiles(N_CROSS), tiles(N_TRI)],
        in_specs=[SMEM] + [VMEM] * 4,
        out_specs=[VMEM] * 2,
        scratch_shapes=[pltpu.VMEM((half_rows, PIVOT), F32)],
        name="first_front_other",
        compiler_params=params,
        cost_estimate=cost(1500 * mega, 300),
    )(tab_one, far_part, got_coup, inv_one, panel_own)
    s_cross_far = swap(s_cross, "hi")
    s_oth = s_part + got_own
    s_oth_far = swap(s_oth, "hi")
    two_both = swap(got_two, "hi")

    quarter = 2 * side_hi + side_lo
    _, hit_far = local_order(map_two[far_hi, front_lo], side_lo)
    goal = jnp.sum(hit * second_map[None, :], axis=1)
    goal_far = jnp.sum(hit_far * map_two[far_hi, front_lo][None, :], axis=1)
    direct, turned = targets(goal, quarter)
    direct_far, turned_far = targets(goal_far, quarter)
    fill_second = fill_two[front_hi, front_lo].reshape(-1)
    quarters = jnp.stack(
        [quarter, 2 * side_hi + 1 - side_lo, 2 * (1 - side_hi) + side_lo, 2 * (1 - side_hi) + 1 - side_lo]
    )
    tab_two = jnp.concatenate(
        [
            live_two[front_hi, front_lo][None], quarters, fill_second,
            direct, direct_far, turned, turned_far,
        ]
    ).astype(jnp.int32)
    lower_two, inv_two, gathered = pl.pallas_call(
        third_kernel,
        out_shape=[dense(SECOND // 4, SECOND), dense(SECOND, SECOND), tiles(G_NONE - G_COUP)],
        in_specs=[SMEM] + [VMEM] * 11,
        out_specs=[VMEM] * 2 + [HBM],
        scratch_shapes=[
            pltpu.VMEM((G_NONE + 1, TILE, TILE), F32),
            pltpu.VMEM((SECOND, SECOND), F32),
            pltpu.VMEM((SECOND, SECOND), F32),
            pltpu.SemaphoreType.DMA,
        ],
        name="second_front_pivot",
        compiler_params=params,
        cost_estimate=cost(4000 * mega, 2 * G_NONE),
    )(
        tab_two, s_own, s_cross, s_oth, s_own_far, s_cross_far, s_oth_far,
        pivot_second, got_pivot, pivot_hi, got_pivot_hi, rows_second,
    )
    quarter_rows = QUARTER * TILE
    panel_two, schur_two = pl.pallas_call(
        last_kernel,
        out_shape=[dense(quarter_rows, SECOND), dense(quarter_rows, U2T * TILE)],
        in_specs=[SMEM] + [VMEM] * 6,
        out_specs=[VMEM] * 2,
        scratch_shapes=[pltpu.VMEM((4, quarter_rows, SECOND), F32)],
        name="second_front_rows",
        compiler_params=params,
        cost_estimate=cost(1000 * mega, 300),
    )(tab_two, gathered, inv_two, coup_two, got_two, two_hi, two_both)
    return (
        lower_one[None, None],
        panel_one[None, None],
        lower_two[None, None],
        panel_two[None, None],
        schur_two[None, None],
    )


def solution(mesh):
    split_both = P("hi", "lo", None, None)
    return jax.shard_map(
        body,
        mesh=mesh,
        in_specs=(split_both,) * 5 + (P(),) * 6,
        out_specs=(split_both,) * 5,
        check_vma=False,
    )
```

```python
import jax
import jax.numpy as jnp
import numpy as np
from jax import lax
from jax.experimental import pallas as pl
from jax.experimental.pallas import tpu as pltpu
from jax.sharding import PartitionSpec as P

TILE = 128
HALF = TILE // 2
CT = 8
P1T = 6
U1T = 12
P2T = 6
U2T = 12
ROWS = 8

HALF_U = U1T // 2
QUARTER = U2T // 4
PIVOT = P1T * TILE
SECOND = P2T * TILE

TRI_C = [(a, b) for a in range(CT) for b in range(a + 1)]
TRI_U = [(a, b) for a in range(HALF_U) for b in range(a + 1)]
TRI_P = [(a, b) for a in range(P1T // 2) for b in range(a + 1)]
BELOW_C = [(a, b) for a, b in TRI_C if a != b]
BELOW_U = [(a, b) for a, b in TRI_U if a != b]
BELOW_P = [(a, b) for a, b in TRI_P if a != b]
DIAG_FIRST = CT + P1T // 2
N_FIRST = len(BELOW_C) + len(BELOW_P) + (DIAG_FIRST + 1) // 2
N_OWN = len(BELOW_U) + (HALF_U + 1) // 2
UNITS = SECOND // HALF
OWN_UNITS = UNITS // 4
REACH = UNITS // 2 + 1
N_UNIT = OWN_UNITS * REACH
N_WIDE = (N_UNIT + 1) // 2
N_TWO = QUARTER * P2T
N_TWO_A = N_TWO // 2
N_OFF = (P1T // 2) ** 2
N_PIV = P1T * P1T
N_COUP = HALF_U * P1T
N_TRI = len(TRI_U)
N_CROSS = HALF_U * HALF_U
N_CROSS_A = N_CROSS // 2
S_COUP = N_PIV
S_OWN = S_COUP + N_COUP
S_FAR = S_OWN + N_TRI
S_CROSS = S_FAR + N_COUP
S_OTH = S_CROSS + N_CROSS
N_FRONT = S_OTH + N_TRI
G_COUP = P2T * P2T
G_TRAIL = G_COUP + U2T * P2T
G_NONE = G_TRAIL + QUARTER * U2T

NT = (((1,), (1,)), ((), ()))
NN = (((1,), (0,)), ((), ()))
F32 = jnp.float32


def split(x):
    high = x.astype(jnp.bfloat16)
    return high, (x - high.astype(F32)).astype(jnp.bfloat16)


def dot3(a, b, dims):
    def one(p, q):
        return lax.dot_general(p, q, dims, preferred_element_type=F32)

    return one(a[0], b[0]) + (one(a[0], b[1]) + one(a[1], b[0]))


def times_inverse(block, parts):
    wide = 2 * TILE
    size = parts[0].shape[0]
    block = split(block)
    return jnp.concatenate(
        [
            dot3([p[:, : c + wide] for p in block], [q[c : c + wide, : c + wide] for q in parts], NT)
            for c in range(0, size, wide)
        ],
        axis=1,
    )


def mul(a, b, dims):
    return dot3(split(a), split(b), dims)


def factor_half(block, width):
    groups = HALF // ROWS
    sub = lax.broadcasted_iota(jnp.int32, (ROWS, TILE), 0)
    lane = lax.broadcasted_iota(jnp.int32, (ROWS, TILE), 1)

    def full(x):
        return jnp.broadcast_to(x, (ROWS, TILE))

    wide = jnp.concatenate([block, jnp.zeros((HALF, HALF), F32)], axis=1)
    a = [
        jnp.where(lane == sub + ROWS * g + HALF, 1.0, wide[ROWS * g : ROWS * g + ROWS])
        for g in range(groups)
    ]
    rows = [None] * HALF
    for j in range(0, HALF, width):
        gj, o = j // ROWS, j % ROWS
        cols = {g: [full(a[g][:, j + i : j + i + 1]) for i in range(width)] for g in range(gj, groups)}
        s = [
            [full(cols[gj][k][o + i : o + i + 1, :]) if k <= i else None for k in range(width)]
            for i in range(width)
        ]
        u = [full(a[gj][o + i : o + i + 1, :]) for i in range(width)]
        inv = [None] * width
        low = [[None] * width for _ in range(width)]
        for k in range(width):
            inv[k] = 1.0 / s[k][k]
            for i in range(k + 1, width):
                low[i][k] = s[i][k] * inv[k]
            for i in range(k + 1, width):
                for q in range(k + 1, i + 1):
                    s[i][q] = s[i][q] - low[i][k] * s[q][k]
        for i in range(width):
            for k in range(i):
                u[i] = u[i] - low[i][k] * u[k]
            rows[j + i] = u[i] * lax.rsqrt(s[i][i])
        scaled = [u[i] * inv[i] for i in range(width)]
        for g in range(gj if o + width < ROWS else gj + 1, groups):
            c = cols[g]
            for i in range(width):
                for k in range(i):
                    c[i] = c[i] - c[k] * low[i][k]
            for i in range(width):
                a[g] = a[g] - c[i] * scaled[i]
    out = []
    for g in range(groups):
        v = rows[ROWS * g]
        for i in range(1, ROWS):
            v = jnp.where(sub == i, rows[ROWS * g + i], v)
        out.append(v)
    both = jnp.concatenate(out, axis=0)
    return both[:, :HALF], both[:, HALF:]


def factor(a, low, inv, tiles, width, start=0, stop=None):
    stop = tiles if stop is None else stop
    d = a[start * TILE : (start + 1) * TILE, start * TILE : (start + 1) * TILE]
    zero = jnp.zeros((HALF, HALF), F32)
    ri = lax.broadcasted_iota(jnp.int32, (HALF, HALF), 0)
    ci = lax.broadcasted_iota(jnp.int32, (HALF, HALF), 1)
    for k in range(start, stop):
        k0, k1, k2 = k * TILE, (k + 1) * TILE, (k + 2) * TILE
        u1, w1 = factor_half(d[:HALF, :HALF], width)
        l21 = mul(d[HALF:, :HALF], w1, NT)
        u2, w2 = factor_half(d[HALF:, HALF:] - mul(l21, l21, NT), width)
        w21 = -mul(w2, mul(l21, w1, NN), NN)
        w = jnp.concatenate([jnp.concatenate([w1, zero], 1), jnp.concatenate([w21, w2], 1)], 0)
        ws = split(w)
        inv[k0:k1, k0:k1] = w
        if k + 1 < tiles:
            p = dot3(split(a[k1:k2, k0:k1]), ws, NT)
            low[k1:k2, k0:k1] = p
            ps = split(p)
            d = a[k1:k2, k1:k2] - dot3(ps, ps, NT)
        l1 = jnp.where(ri >= ci, u1.T, 0.0)
        l2 = jnp.where(ri >= ci, u2.T, 0.0)
        low[k0:k1, k0:k1] = jnp.concatenate(
            [jnp.concatenate([l1, zero], 1), jnp.concatenate([l21, l2], 1)], 0
        )
        if k + 2 < tiles:
            low[k2:, k0:k1] = dot3(split(a[k2:, k0:k1]), ws, NT)
            for j in range(k + 1, tiles):
                j0 = j * TILE
                top = max(j0, k2)
                a[top:, j0 : j0 + TILE] = a[top:, j0 : j0 + TILE] - mul(
                    low[top:, k0:k1], low[j0 : j0 + TILE, k0:k1], NT
                )
        if k > 0:
            x = mul(low[k0:k1, 0:k0], inv[0:k0, 0:k0], NN)
            inv[k0:k1, 0:k0] = -dot3(ws, split(x), NN)
        if k + 1 < tiles:
            rest = jnp.zeros((TILE, (tiles - k - 1) * TILE), F32)
            low[k0:k1, k1:] = rest
            inv[k0:k1, k1:] = rest
    if stop < tiles:
        a[k1:k2, k1:k2] = d


def padded(a, tile_of, live, tiles):
    ri = lax.broadcasted_iota(jnp.int32, (TILE, TILE), 0)
    ci = lax.broadcasted_iota(jnp.int32, (TILE, TILE), 1)
    eye = jnp.where(ri == ci, 1.0, 0.0)
    for i in range(tiles):
        kept = (jnp.int32(i) < live).astype(F32)
        for j in range(i + 1):
            value = tile_of(i, j) * kept
            if i == j:
                value = value + eye * (1.0 - kept)
            a[i * TILE : (i + 1) * TILE, j * TILE : (j + 1) * TILE] = value


def copy_all(pairs, sems):
    copies = [pltpu.make_async_copy(src, dst, sems.at[n]) for n, (src, dst) in enumerate(pairs)]
    for c in copies:
        c.start()
    for c in copies:
        c.wait()


def tile_at(ref, row, col):
    return ref.at[
        pl.ds(pl.multiple_of(row * TILE, TILE), TILE), pl.ds(pl.multiple_of(col * TILE, TILE), TILE)
    ]


def square_index():
    return (
        lax.broadcasted_iota(jnp.int32, (TILE, TILE), 0),
        lax.broadcasted_iota(jnp.int32, (TILE, TILE), 1),
    )


def put_pairs(tiles_in, out, first):
    r, c = square_index()
    diagonals = []
    for n in range(0, len(tiles_in), 2):
        mixed = tiles_in[n]
        if n + 1 < len(tiles_in):
            mixed = jnp.where(r >= c, mixed, tiles_in[n + 1])
            diagonals.append(jnp.sum(jnp.where(r == c, tiles_in[n + 1], 0.0), axis=0, keepdims=True))
        out[pl.ds((first + n // 2) * TILE, TILE), :] = mixed
    diagonals += [jnp.zeros((1, TILE), F32)] * (ROWS - len(diagonals))
    out[pl.ds((first + (len(tiles_in) + 1) // 2) * TILE, ROWS), :] = jnp.concatenate(diagonals, axis=0)


def get_pairs(ref, first, count):
    r, c = square_index()
    base = (first + (count + 1) // 2) * TILE
    out = []
    for n in range(0, count, 2):
        mixed = ref[(first + n // 2) * TILE : (first + n // 2 + 1) * TILE, :]
        if n + 1 == count:
            out.append(mixed)
            continue
        other = mixed.T
        out.append(jnp.where(r >= c, mixed, other))
        diagonal = ref[base + n // 2 : base + n // 2 + 1, :]
        out.append(jnp.where(r == c, diagonal, jnp.where(r < c, mixed, other)))
    return out


def message_tile(ref, n):
    return ref[pl.ds(pl.multiple_of(n * TILE, TILE), TILE), :]


def pack_first(tab, block, pivot, out, square, sems):
    side = tab[CT]
    pairs = []
    for n, (a, b) in enumerate(BELOW_C):
        pairs.append((tile_at(block, tab[a], tab[b]), out.at[pl.ds(n * TILE, TILE)]))
    first = len(BELOW_C)
    for n, (a, b) in enumerate(BELOW_P):
        pairs.append(
            (tile_at(pivot, a, side * (P1T // 2) + b), out.at[pl.ds((first + n) * TILE, TILE)])
        )
    for a in range(CT):
        pairs.append((tile_at(block, tab[a], tab[a]), square.at[a]))
    for a in range(P1T // 2):
        pairs.append((tile_at(pivot, a, side * (P1T // 2) + a), square.at[CT + a]))
    copy_all(pairs, sems)
    put_pairs([square[n] for n in range(DIAG_FIRST)], out, first + len(BELOW_P))


def pack_rest(
    tab, block, pivot, rows, pivot_second, second,
    coup, own, kept, cross, off, own_sent, coup_two, two_sent_a, two_sent_b, units, units_sent,
    strips, sems,
):
    side = tab[CT]
    order = CT + 1
    local = order + CT
    quarter = tab[local + U1T]
    pairs = []
    for r in range(HALF_U):
        row = tab[local + r] - side * HALF_U
        for c in range(P1T):
            pairs.append((tile_at(rows, row, c), coup.at[r * P1T + c]))
    for n, (a, b) in enumerate(TRI_U):
        row = tab[local + a] - side * HALF_U
        pairs.append((tile_at(rows, row, P1T + tab[local + b]), own.at[n]))
    for n, (a, b) in enumerate(TRI_C):
        pairs.append((tile_at(block, tab[order + a], tab[order + b]), kept.at[n]))
    for i in range(HALF_U):
        row = tab[local + i] - side * HALF_U
        for k in range(HALF_U):
            pairs.append(
                (tile_at(rows, row, P1T + tab[local + HALF_U + k]), cross.at[i * HALF_U + k])
            )
    for i in range(P1T // 2):
        for k in range(P1T // 2):
            pairs.append(
                (tile_at(pivot, i, (1 - side) * (P1T // 2) + k), off.at[i * (P1T // 2) + k])
            )
    for n, (i, k) in enumerate(TRI_P):
        pairs.append((tile_at(pivot, i, side * (P1T // 2) + k), off.at[N_OFF + n]))
    for r in range(QUARTER):
        for c in range(P2T):
            n = r * P2T + c
            sent = two_sent_a.at[n] if n < N_TWO_A else two_sent_b.at[n - N_TWO_A]
            pairs.append((tile_at(second, r, c), coup_two.at[n]))
            pairs.append((tile_at(second, r, c), sent))
    far = []
    for i in range(OWN_UNITS):
        for d in range(REACH):
            col = (quarter * OWN_UNITS + i - d + UNITS) % UNITS
            far.append(col % 2)
            source = pivot_second.at[
                pl.ds(i * HALF, HALF), pl.ds(pl.multiple_of(col // 2 * TILE, TILE), TILE)
            ]
            pairs.append((source, strips.at[i * REACH + d]))
    copy_all(pairs, sems)
    lane = lax.broadcasted_iota(jnp.int32, (HALF, TILE), 1)

    def placed(n, half):
        strip = strips[n]
        return jnp.where(far[n] == half, strip, pltpu.roll(strip, HALF, 1))

    for n in range(N_WIDE):
        strip = placed(2 * n, 0)
        if 2 * n + 1 < N_UNIT:
            strip = jnp.where(lane < HALF, strip, placed(2 * n + 1, 1))
        units[n * HALF : (n + 1) * HALF, :] = strip
        units_sent[n * HALF : (n + 1) * HALF, :] = strip
    put_own([own[n] for n in range(N_TRI)], own_sent)


def after(array, *others):
    def kernel(*refs):
        pass

    return pl.pallas_call(
        kernel,
        out_shape=jax.ShapeDtypeStruct(array.shape, array.dtype),
        in_specs=[HBM] * (1 + len(others)),
        out_specs=HBM,
        input_output_aliases={0: 0},
        name="after",
        cost_estimate=CHEAP,
    )(array, *others)


T_SIDE = 0
T_LIVE = 1
T_LOCAL = 2
T_FILL = T_LOCAL + U1T
T_SLOT = T_FILL + U1T * P1T
T_SLOT_FAR = T_SLOT + CT * CT


def panel_rows(tile_of, count, live, inv, put):
    parts = split(inv)
    for r in range(0, count, 2):
        block = jnp.concatenate(
            [
                jnp.concatenate([tile_of(r + i, c) for c in range(P1T)], axis=1)
                for i in range(2)
            ],
            axis=0,
        )
        lane = lax.broadcasted_iota(jnp.int32, block.shape, 1)
        block = jnp.where(lane < live * TILE, block, 0.0)
        put(r, times_inverse(block, parts))


def first_kernel(
    tab, mine, theirs, coup, own, cross, off,
    lower_out, inv_out, panel_out, rows_out, own_out, far_out,
    front, a, low, sem,
):
    side = tab[T_SIDE]
    live = tab[T_LIVE]
    half = P1T // 2
    square = get_pairs(theirs, len(BELOW_C) + len(BELOW_P), DIAG_FIRST)
    front[0:N_PIV] = jnp.zeros((N_PIV, TILE, TILE), F32)
    for n, (i, k) in enumerate(TRI_P):
        front[(side * half + i) * P1T + side * half + k] = off[N_OFF + n]
        if i == k:
            tile = square[CT + i]
        else:
            tile = message_tile(theirs, len(BELOW_C) + BELOW_P.index((i, k)))
        front[((1 - side) * half + i) * P1T + (1 - side) * half + k] = tile
    for i in range(half):
        for k in range(half):

            @pl.when(side == 0)
            def _():
                front[(half + k) * P1T + i] = off[i * half + k].T

            @pl.when(side != 0)
            def _():
                front[(half + i) * P1T + k] = off[i * half + k]

    def scale(n, carry):
        front[S_COUP + n] = coup[n] * tab[T_FILL + n].astype(F32)
        front[S_FAR + n] = jnp.zeros((TILE, TILE), F32)
        front[S_CROSS + n] = cross[n]
        return carry

    lax.fori_loop(0, N_COUP, scale, 0)

    def copy(n, carry):
        front[S_OWN + n] = own[n]
        front[S_OTH + n] = jnp.zeros((TILE, TILE), F32)
        return carry

    lax.fori_loop(0, N_TRI, copy, 0)
    for i in range(CT):

        def extend(k, carry, i=i):
            here = tab[T_SLOT + i * CT + k]
            front[here] = front[here] + mine[tri(i, 0) + k]
            return carry

        lax.fori_loop(0, i + 1, extend, 0)

        def extend_far(k, carry, i=i):
            there = tab[T_SLOT_FAR + i * CT + k]
            front[there] = front[there] + message_tile(theirs, i * (i - 1) // 2 + k)
            return carry

        lax.fori_loop(0, i, extend_far, 0)
        there = tab[T_SLOT_FAR + i * CT + i]
        front[there] = front[there] + square[i]
    leave = pltpu.make_async_copy(front.at[pl.ds(S_FAR, N_FRONT - S_FAR)], far_out, sem)
    leave.start()
    padded(a, lambda i, j: front[i * P1T + j], live, P1T)
    factor(a, low, inv_out, P1T, 4)
    lower_out[...] = low[pl.ds(pl.multiple_of(side * (PIVOT // 2), TILE), PIVOT // 2), :]

    def put(r, rows):
        panel_out[r * TILE : (r + 2) * TILE, :] = rows
        for i in range(2):
            place = tab[T_LOCAL + r + i] - side * HALF_U
            rows_out[pl.ds(pl.multiple_of(place * TILE, TILE), TILE), :] = rows[
                i * TILE : (i + 1) * TILE
            ]

    panel_rows(lambda r, c: front[S_COUP + r * P1T + c], HALF_U, live, inv_out[...], put)
    for i in range(HALF_U):
        left = split(panel_out[i * TILE : (i + 1) * TILE, :])
        product = dot3(left, split(panel_out[0 : (i + 1) * TILE, :]), NT)
        for k in range(i + 1):
            own_out[tri(i, k)] = front[S_OWN + tri(i, k)] - product[:, k * TILE : (k + 1) * TILE]
    leave.wait()


def second_kernel(tab, far, coup, inv, panel, cross_a, cross_b, oth_out, panel_far):
    live = tab[T_LIVE]

    def tile_of(r, c):
        n = r * P1T + c
        return far[n] + coup[n] * tab[T_FILL + N_COUP + n].astype(F32)

    def put(r, rows):
        panel_far[r * TILE : (r + 2) * TILE, :] = rows

    panel_rows(tile_of, HALF_U, live, inv[...], put)
    right = split(panel_far[...])
    for i in range(0, HALF_U, 2):
        product = dot3(split(panel[i * TILE : (i + 2) * TILE, :]), right, NT)
        for q in range(2):
            for k in range(HALF_U):
                n = (i + q) * HALF_U + k
                out, first = (cross_a, 0) if n < N_CROSS_A else (cross_b, N_CROSS_A)
                out[n - first] = (
                    far[N_COUP + n]
                    - product[q * TILE : (q + 1) * TILE, k * TILE : (k + 1) * TILE]
                )
    for i in range(HALF_U):
        left = split(panel_far[i * TILE : (i + 1) * TILE, :])
        product = dot3(left, split(panel_far[0 : (i + 1) * TILE, :]), NT)
        for k in range(i + 1):
            oth_out[tri(i, k)] = (
                far[N_COUP + N_CROSS + tri(i, k)] - product[:, k * TILE : (k + 1) * TILE]
            )


def add_kernel(part, got, out, sent):
    square = get_pairs(got, len(BELOW_U), HALF_U)
    for n, (i, k) in enumerate(BELOW_U):
        out[tri(i, k)] = part[tri(i, k)] + message_tile(got, n)
    for i in range(HALF_U):
        out[tri(i, i)] = part[tri(i, i)] + square[i]
    put_own([out[n] for n in range(N_TRI)], sent)


def put_own(block, out):
    for n, (a, b) in enumerate(BELOW_U):
        out[n * TILE : (n + 1) * TILE, :] = block[tri(a, b)]
    put_pairs([block[tri(a, a)] for a in range(HALF_U)], out, len(BELOW_U))


def get_own(ref, out):
    for n, (i, k) in enumerate(BELOW_U):
        out[tri(i, k)] = message_tile(ref, n)
    for i, tile in enumerate(get_pairs(ref, len(BELOW_U), HALF_U)):
        out[tri(i, i)] = tile


Q_LIVE = 0
Q_MINE = 1
Q_FILL = 5
Q_DIRECT = Q_FILL + U2T * P2T
Q_TURNED = Q_DIRECT + 2 * U1T * U1T


def extend_cross(tab, refs, g, front, low, high):
    for q, ref in enumerate(refs):
        extend_two(tab, ref, g, front, q * HALF_U // 2, HALF_U, False, low, high, HALF_U // 2)


def extend_two(tab, ref, g, front, rows, cols, triangle, low, high, count=HALF_U):
    for i in range(count):

        def one(k, carry, i=i):
            at = front * U1T * U1T + (rows + i) * U1T + cols + k
            n = (tri(i, 0) if triangle else i * HALF_U) + k
            direct = tab[Q_DIRECT + at]
            turned = tab[Q_TURNED + at]

            @pl.when((direct >= low) & (direct < high))
            def _():
                g[direct - low] = g[direct - low] + ref[n]

            @pl.when((turned >= low) & (turned < high))
            def _():
                g[turned - low] = g[turned - low] + ref[n].T

            return carry

        lax.fori_loop(0, i + 1 if triangle else HALF_U, one, 0)


def add_units(tab, g, units, s):
    lane = lax.broadcasted_iota(jnp.int32, (HALF, TILE), 1)
    for i in range(OWN_UNITS):
        row = tab[Q_MINE + s] * OWN_UNITS + i
        for d in range(REACH):
            n = i * REACH + d
            col = (row - d + UNITS) % UNITS
            strip = units[n // 2 * HALF : (n // 2 + 1) * HALF, :]
            here = n % 2

            def add(r, c, block):
                slot = r // 2 * P2T + c // 2
                start = pl.multiple_of(r % 2 * HALF, HALF)
                old = g[slot, pl.ds(start, HALF), :]
                g[slot, pl.ds(start, HALF), :] = old + jnp.where(lane // HALF == c % 2, block, 0.0)

            @pl.when((col <= row) & ((d < REACH - 1) | (row >= UNITS // 2)))
            def _():
                add(row, col, jnp.where(col % 2 == here, strip, pltpu.roll(strip, HALF, 1)))

            if d < REACH - 1 and d > 0:

                @pl.when(col > row)
                def _():
                    turned = strip.T[here * HALF : (here + 1) * HALF, :]
                    add(col, row, jnp.concatenate([turned, turned], axis=1))


def third_kernel(tab, own0, cross0_a, cross0_b, own1, units0, units2, second, g):
    def clear(n, carry):
        g[n] = jnp.zeros((TILE, TILE), F32)
        return carry

    lax.fori_loop(0, G_TRAIL, clear, 0)
    for r in range(QUARTER):
        for c in range(U2T):
            g[G_TRAIL + r * U2T + c] = second[
                r * TILE : (r + 1) * TILE, SECOND + c * TILE : SECOND + (c + 1) * TILE
            ]
    add_units(tab, g, units0, 0)
    add_units(tab, g, units2, 2)
    extend_two(tab, own0, g, 0, 0, 0, True, 0, G_NONE)
    extend_cross(tab, (cross0_a, cross0_b), g, 0, 0, G_NONE)
    extend_two(tab, own1, g, 1, 0, 0, True, 0, G_NONE)


def more_kernel(tab, part, cross1_a, cross1_b, oth0, units1, g, sem):
    enter = pltpu.make_async_copy(part, g, sem)
    enter.start()
    enter.wait()
    add_units(tab, g, units1, 1)
    extend_cross(tab, (cross1_a, cross1_b), g, 1, 0, G_NONE)
    extend_two(tab, oth0, g, 0, HALF_U, HALF_U, True, 0, G_NONE)


def pivot_kernel(tab, part, oth1, units3, a, low, inv_out, g, other, sem):
    enter = pltpu.make_async_copy(part.at[pl.ds(0, G_COUP)], g, sem)
    enter.start()
    get_own(oth1, other)
    enter.wait()
    add_units(tab, g, units3, 3)
    extend_two(tab, other, g, 1, HALF_U, HALF_U, True, 0, G_COUP)
    padded(a, lambda i, j: g[i * P2T + j], tab[Q_LIVE], P2T)
    factor(a, low, inv_out, P2T, 8, 0, P2T // 2)


def pivot_rest_kernel(tab, a_in, low_in, inv_in, lower_out, inv_out, a, low):
    done = P2T // 2 * TILE
    a[done:, done:] = a_in[done:, done:]
    low[:, :done] = low_in[:, :done]
    low[:done, done:] = jnp.zeros((done, SECOND - done), F32)
    inv_out[:done, :] = inv_in[:done, :]
    factor(a, low, inv_out, P2T, 8, P2T // 2)
    start = tab[Q_MINE] * (SECOND // 4)
    lower_out[...] = low[pl.ds(pl.multiple_of(start, HALF), SECOND // 4), :]


def quarter_rows_of(tab, g, quarter):
    return jnp.concatenate(
        [
            jnp.concatenate([g[(quarter * QUARTER + r) * P2T + c] for c in range(P2T)], axis=1)
            for r in range(QUARTER)
        ],
        axis=0,
    )


def halves(first, second):
    return lambda n: first[n] if n < N_TWO_A else second[n - N_TWO_A]


def quarter_panel(tab, block, coup, parts, quarter):
    rows = []
    for r in range(QUARTER):
        fill = Q_FILL + (quarter * QUARTER + r) * P2T
        rows.append(
            jnp.concatenate(
                [coup(r * P2T + c) * tab[fill + c].astype(F32) for c in range(P2T)], axis=1
            )
        )
    block = block + jnp.concatenate(rows, axis=0)
    lane = lax.broadcasted_iota(jnp.int32, block.shape, 1)
    block = jnp.where(lane < tab[Q_LIVE] * TILE, block, 0.0)
    return times_inverse(block, parts)


WIDE = QUARTER * TILE


def rows_kernel(
    tab, part, oth1, inv, coup0, coup1_a, coup1_b, coup2,
    panel_out, schur_out, rest_out,
    g, other, panels, sem,
):
    enter = pltpu.make_async_copy(part.at[pl.ds(G_COUP, G_NONE - G_COUP)], g, sem)
    enter.start()
    get_own(oth1, other)
    enter.wait()
    extend_two(tab, other, g, 1, HALF_U, HALF_U, True, G_COUP, G_NONE)
    parts = split(inv[...])
    rest_out[...] = quarter_rows_of(tab, g, tab[Q_MINE + 3])
    whole = [lambda n, ref=ref: ref[n] for ref in (coup0, coup2)]
    for s, coup in enumerate((whole[0], halves(coup1_a, coup1_b), whole[1])):
        quarter = tab[Q_MINE + s]
        panel = quarter_panel(tab, quarter_rows_of(tab, g, quarter), coup, parts, quarter)
        panels[s] = panel
        if s == 0:
            panel_out[...] = panel
    left = split(panel_out[...])
    for s in range(4):
        quarter = tab[Q_MINE + s]
        if s < 3:
            product = dot3(left, split(panels[s]), NT)
        for r in range(QUARTER):
            for c in range(QUARTER):
                tile = g[G_TRAIL - G_COUP + r * U2T + quarter * QUARTER + c]
                if s < 3:
                    tile = tile - product[r * TILE : (r + 1) * TILE, c * TILE : (c + 1) * TILE]
                col = pl.multiple_of((quarter * QUARTER + c) * TILE, TILE)
                schur_out[r * TILE : (r + 1) * TILE, pl.ds(col, TILE)] = tile


def last_kernel(tab, schur, rest, panel, inv, coup_a, coup_b, out, block, sem):
    quarter = tab[Q_MINE + 3]
    col = pl.ds(pl.multiple_of(quarter * WIDE, TILE), WIDE)
    enter = pltpu.make_async_copy(schur.at[:, col], block, sem)
    enter.start()
    other = quarter_panel(tab, rest[...], halves(coup_a, coup_b), split(inv[...]), quarter)
    product = dot3(split(panel[...]), split(other), NT)
    enter.wait()
    block[...] = block[...] - product
    leave = pltpu.make_async_copy(block, out.at[:, col], sem)
    leave.start()
    leave.wait()


def swap(array, axis):
    size = lax.axis_size(axis)
    return lax.ppermute(array, axis, [(i, i ^ (size // 2)) for i in range(size)])


def tiles(count):
    return jax.ShapeDtypeStruct((count, TILE, TILE), F32)


def dense(rows, cols):
    return jax.ShapeDtypeStruct((rows, cols), F32)


SMEM = pl.BlockSpec(memory_space=pltpu.SMEM)
VMEM = pl.BlockSpec(memory_space=pltpu.VMEM)
HBM = pl.BlockSpec(memory_space=pl.ANY)
LIMIT = 60 << 20
CHEAP = pl.CostEstimate(flops=1, bytes_accessed=1, transcendentals=0)


def call(kernel, name, out_shape, in_specs, out_specs, scratch=(), waits=(), limit=LIMIT, **options):
    count = len(in_specs)

    def body(*refs):
        kernel(*refs[:count], *refs[count + len(waits) :])

    run = pl.pallas_call(
        body,
        out_shape=out_shape,
        in_specs=in_specs + [HBM] * len(waits),
        out_specs=out_specs,
        scratch_shapes=list(scratch),
        name=name,
        compiler_params=pltpu.CompilerParams(vmem_limit_bytes=limit),
        cost_estimate=CHEAP,
        **options,
    )
    return lambda *args: run(*args, *waits)


def tri(i, k):
    return i * (i + 1) // 2 + k


def local_order(second_map, side):
    unit = jnp.arange(U1T, dtype=jnp.int32)
    rank = second_map + jnp.where(unit // HALF_U == side, 0, P2T + U2T)
    place = jnp.sum((rank[None, :] < rank[:, None]).astype(jnp.int32), axis=1)
    hit = (place[None, :] == unit[:, None]).astype(jnp.int32)
    return place, hit


def place_of(child_map, place):
    unit = jnp.arange(U1T, dtype=jnp.int32)
    hit = (child_map[:, None] - P1T == unit[None, :]).astype(jnp.int32)
    return jnp.where(child_map < P1T, child_map, P1T + jnp.sum(hit * place[None, :], axis=1))


def sort_by(key):
    spot = jnp.sum((key[None, :] < key[:, None]).astype(jnp.int32), axis=1)
    hit = (spot[None, :] == jnp.arange(CT, dtype=jnp.int32)[:, None]).astype(jnp.int32)
    order = jnp.sum(hit * jnp.arange(CT, dtype=jnp.int32)[None, :], axis=1)
    return order, jnp.sum(hit * key[None, :], axis=1)


def turned_key(key):
    return jnp.where(key < P1T, key, P1T + (key - P1T + HALF_U) % U1T)


def slots(keys):
    row = keys[:, None]
    col = keys[None, :]
    own = P1T + HALF_U
    pivot = row * P1T + col
    coup = jnp.where(row >= own, S_COUP + (row - own) * P1T, S_FAR + (row - P1T) * P1T) + col
    near = S_OWN + tri(row - own, col - own)
    cross = S_CROSS + (row - own) * HALF_U + col - P1T
    other = S_OTH + tri(row - P1T, col - P1T)
    rest = jnp.where(row < own, other, jnp.where(col < own, cross, near))
    return jnp.where(row < P1T, pivot, jnp.where(col < P1T, coup, rest)).reshape(-1)


def targets(goal, quarter):
    row = goal[:, None]
    col = goal[None, :]

    def index(r, c):
        mine = (r - P2T) // QUARTER == quarter
        coup = G_COUP + (r - P2T) * P2T + c
        trail = G_TRAIL + (r - P2T - quarter * QUARTER) * U2T + c - P2T
        rest = jnp.where(c < P2T, coup, jnp.where(mine, trail, G_NONE))
        return jnp.where(r < P2T, jnp.where((c < P2T) & (r >= c), r * P2T + c, G_NONE), rest)

    direct = index(row, col)
    turned = jnp.where(row == col, G_NONE, index(col, row))
    return direct.reshape(-1), turned.reshape(-1)


def body(
    contribution,
    pivot_one,
    rows_one,
    pivot_two,
    rows_two,
    map_one,
    map_two,
    fill_one,
    fill_two,
    live_one,
    live_two,
):
    size_lo = lax.axis_size("lo")
    size_hi = lax.axis_size("hi")
    half_lo = size_lo // 2
    half_hi = size_hi // 2
    index_lo = lax.axis_index("lo")
    index_hi = lax.axis_index("hi")
    side_lo = index_lo // half_lo
    side_hi = index_hi // half_hi
    front_lo = index_lo % half_lo
    front_hi = index_hi % half_hi
    far_lo = (index_lo + half_lo) % size_lo
    far_hi = (index_hi + half_hi) % size_hi
    quarter = 2 * side_hi + side_lo
    block, pivot, rows = contribution[0, 0], pivot_one[0, 0], rows_one[0, 0]
    pivot_second, rows_second = pivot_two[0, 0], rows_two[0, 0]

    second_map = map_two[index_hi, front_lo]
    place, hit = local_order(second_map, side_lo)
    key = place_of(map_one[index_hi, index_lo], place)
    order_sent, _ = sort_by(key)
    tab_first = jnp.concatenate([order_sent, side_lo[None]]).astype(jnp.int32)
    sent = call(
        pack_first,
        "pack_first",
        dense(N_FIRST * TILE + ROWS, TILE),
        [SMEM, HBM, HBM],
        VMEM,
        [
            pltpu.VMEM((DIAG_FIRST, TILE, TILE), F32),
            pltpu.SemaphoreType.DMA((len(TRI_C) + len(TRI_P),)),
        ],
    )(tab_first, block, pivot)
    got_first = swap(sent, "lo")

    unit = jnp.arange(U1T, dtype=jnp.int32)
    local = jnp.sum(hit * unit[None, :], axis=1)
    order_kept, keys = sort_by(turned_key(key))
    tab_rest = jnp.concatenate([tab_first, order_kept, local, quarter[None]]).astype(jnp.int32)
    shapes = [
        tiles(N_COUP), tiles(N_TRI), tiles(len(TRI_C)), tiles(N_CROSS), tiles(N_OFF + len(TRI_P)),
        dense(N_OWN * TILE + ROWS, TILE), tiles(N_TWO), tiles(N_TWO_A), tiles(N_TWO - N_TWO_A),
        dense(N_WIDE * HALF, TILE), dense(N_WIDE * HALF, TILE),
    ]
    n_rest = N_COUP + N_TRI + len(TRI_C) + N_CROSS + N_OFF + len(TRI_P) + 2 * N_TWO + N_UNIT
    coup, own, kept, cross, off, own_sent, two, two_a, two_b, units, units_sent = call(
        pack_rest,
        "pack_rest",
        shapes,
        [SMEM] + [HBM] * 5,
        [VMEM] * len(shapes),
        [pltpu.VMEM((N_UNIT, HALF, TILE), F32), pltpu.SemaphoreType.DMA((n_rest,))],
        waits=(sent,),
    )(tab_rest, block, pivot, rows, pivot_second, rows_second)
    two_hi = swap(two, "hi")
    units_hi = swap(units, "hi")
    far_key = place_of(map_one[index_hi, far_lo], place)
    _, far_keys = sort_by(turned_key(far_key))
    live_first = live_one[index_hi, front_lo]
    fill_first = jnp.sum(hit[:, :, None] * fill_one[index_hi, front_lo][None, :, :], axis=1)
    tab_one = jnp.concatenate(
        [side_lo[None], live_first[None], local, fill_first.reshape(-1), slots(keys), slots(far_keys)]
    ).astype(jnp.int32)
    map_far = map_two[far_hi, front_lo]
    _, hit_far = local_order(map_far, side_lo)
    direct, turned = targets(jnp.sum(hit * second_map[None, :], axis=1), quarter)
    direct_far, turned_far = targets(jnp.sum(hit_far * map_far[None, :], axis=1), quarter)
    fill_second = fill_two[front_hi, front_lo].reshape(-1)
    quarters = jnp.stack(
        [quarter, 2 * side_hi + 1 - side_lo, 2 * (1 - side_hi) + side_lo, 2 * (1 - side_hi) + 1 - side_lo]
    )
    tab_two = jnp.concatenate(
        [
            live_two[front_hi, front_lo][None], quarters, fill_second,
            direct, direct_far, turned, turned_far,
        ]
    ).astype(jnp.int32)
    coup = after(coup, got_first, two_hi, units_hi, tab_one, tab_two)
    got_coup = swap(coup, "lo")

    half_rows = HALF_U * TILE
    lower_one, inv_one, panel_own, panel_one, s_own, far_part = call(
        first_kernel,
        "first_front_own",
        [
            dense(PIVOT // 2, PIVOT), dense(PIVOT, PIVOT), dense(half_rows, PIVOT),
            dense(half_rows, PIVOT), tiles(N_TRI), tiles(N_FRONT - S_FAR),
        ],
        [SMEM] + [VMEM] * 6,
        [VMEM] * 5 + [HBM],
        [
            pltpu.VMEM((N_FRONT, TILE, TILE), F32),
            pltpu.VMEM((PIVOT, PIVOT), F32),
            pltpu.VMEM((PIVOT, PIVOT), F32),
            pltpu.SemaphoreType.DMA,
        ],
    )(tab_one, kept, got_first, coup, own, cross, off)
    s_own_far = swap(s_own, "hi")
    own_sent = after(own_sent, got_coup, panel_own)
    got_own = swap(own_sent, "lo")

    cross_a, cross_b, s_part = call(
        second_kernel,
        "first_front_other",
        [tiles(N_CROSS_A), tiles(N_CROSS - N_CROSS_A), tiles(N_TRI)],
        [SMEM] + [VMEM] * 4,
        [VMEM] * 3,
        [pltpu.VMEM((half_rows, PIVOT), F32)],
        waits=(s_own_far, own_sent),
    )(tab_one, far_part, got_coup, inv_one, panel_own)
    cross_a_far, cross_b_far = swap(cross_a, "hi"), swap(cross_b, "hi")
    part = call(third_kernel, "second_front_part", tiles(G_NONE), [SMEM] + [VMEM] * 7, VMEM)(
        tab_two, s_own, cross_a, cross_b, s_own_far, units, units_hi, rows_second
    )
    got_units = swap(after(units_sent, got_own, part), "lo")
    s_oth, s_oth_sent = call(
        add_kernel,
        "first_front_last",
        [tiles(N_TRI), dense(N_OWN * TILE + ROWS, TILE)],
        [VMEM] * 2,
        [VMEM] * 2,
        waits=(part,),
    )(s_part, got_own)
    s_oth_far = swap(s_oth_sent, "hi")
    units_both = swap(got_units, "hi")
    got_two_a = swap(after(two_a, got_units, s_oth, cross_a_far, cross_b_far), "lo")
    part = call(
        more_kernel,
        "second_front_more",
        tiles(G_NONE),
        [SMEM, HBM] + [VMEM] * 4,
        VMEM,
        [pltpu.SemaphoreType.DMA],
    )(tab_two, part, cross_a_far, cross_b_far, s_oth, got_units)
    got_two_b = swap(after(two_b, got_two_a, units_both, s_oth_far, part), "lo")
    square = dense(SECOND, SECOND)
    a, low, inv_a = call(
        pivot_kernel,
        "second_front_pivot",
        [square] * 3,
        [SMEM, HBM] + [VMEM] * 2,
        [VMEM] * 3,
        [
            pltpu.VMEM((G_COUP, TILE, TILE), F32),
            pltpu.VMEM((N_TRI, TILE, TILE), F32),
            pltpu.SemaphoreType.DMA,
        ],
    )(tab_two, part, s_oth_far, units_both)
    two_a_both = swap(got_two_a, "hi")
    lower_two, inv_two = call(
        pivot_rest_kernel,
        "second_front_pivot_rest",
        [dense(SECOND // 4, SECOND), square],
        [SMEM] + [VMEM] * 3,
        [VMEM] * 2,
        [pltpu.VMEM((SECOND, SECOND), F32)] * 2,
        waits=(got_two_a,),
    )(tab_two, a, low, inv_a)
    got_two_b = after(got_two_b, inv_two)
    two_b_both = swap(got_two_b, "hi")
    panel_two, schur, rest = call(
        rows_kernel,
        "second_front_rows",
        [dense(WIDE, SECOND), dense(WIDE, U2T * TILE), dense(WIDE, SECOND)],
        [SMEM, HBM] + [VMEM] * 6,
        [VMEM] * 3,
        [
            pltpu.VMEM((G_NONE - G_COUP, TILE, TILE), F32),
            pltpu.VMEM((N_TRI, TILE, TILE), F32),
            pltpu.VMEM((3, WIDE, SECOND), F32),
            pltpu.SemaphoreType.DMA,
        ],
    )(tab_two, part, s_oth_far, inv_two, two, got_two_a, got_two_b, two_hi)
    schur_two = call(
        last_kernel,
        "second_front_last",
        dense(WIDE, U2T * TILE),
        [SMEM, HBM] + [VMEM] * 5,
        HBM,
        [pltpu.VMEM((WIDE, WIDE), F32), pltpu.SemaphoreType.DMA],
        input_output_aliases={1: 0},
    )(tab_two, schur, rest, panel_two, inv_two, two_a_both, two_b_both)
    return (
        lower_one[None, None],
        panel_one[None, None],
        lower_two[None, None],
        panel_two[None, None],
        schur_two[None, None],
    )


def solution(mesh):
    split_both = P("hi", "lo", None, None)
    return jax.shard_map(
        body,
        mesh=mesh,
        in_specs=(split_both,) * 5 + (P(),) * 6,
        out_specs=(split_both,) * 5,
        check_vma=False,
    )
```

```python
import jax
import jax.numpy as jnp
import numpy as np
from jax import lax
from jax.experimental import pallas as pl
from jax.experimental.pallas import tpu as pltpu
from jax.sharding import PartitionSpec as P

TILE = 128
HALF = TILE // 2
CT = 8
P1T = 6
U1T = 12
P2T = 6
U2T = 12
ROWS = 8

HALF_U = U1T // 2
QUARTER = U2T // 4
PIVOT = P1T * TILE
SECOND = P2T * TILE

TRI_C = [(a, b) for a in range(CT) for b in range(a + 1)]
TRI_U = [(a, b) for a in range(HALF_U) for b in range(a + 1)]
TRI_P = [(a, b) for a in range(P1T // 2) for b in range(a + 1)]
BELOW_C = [(a, b) for a, b in TRI_C if a != b]
BELOW_U = [(a, b) for a, b in TRI_U if a != b]
BELOW_P = [(a, b) for a, b in TRI_P if a != b]
DIAG_FIRST = CT + P1T // 2
N_FIRST = len(BELOW_C) + len(BELOW_P) + (DIAG_FIRST + 1) // 2
N_OWN = len(BELOW_U) + (HALF_U + 1) // 2
UNITS = SECOND // HALF
OWN_UNITS = UNITS // 4
REACH = UNITS // 2 + 1
N_UNIT = OWN_UNITS * REACH
N_WIDE = (N_UNIT + 1) // 2
N_TWO = QUARTER * P2T
N_MAIN = 30
N_TWO_A = 8
N_TWO_B = 8
N_OFF = (P1T // 2) ** 2
N_PIV = P1T * P1T
N_COUP = HALF_U * P1T
N_TRI = len(TRI_U)
N_CROSS = HALF_U * HALF_U
N_CROSS_A = N_CROSS // 2
N_OVER = N_COUP - N_MAIN + N_TWO - N_TWO_A - N_TWO_B
S_COUP = N_PIV
S_OWN = S_COUP + N_COUP
S_FAR = S_OWN + N_TRI
S_CROSS = S_FAR + N_COUP
S_OTH = S_CROSS + N_CROSS
N_FRONT = S_OTH + N_TRI
G_COUP = P2T * P2T
G_TRAIL = G_COUP + U2T * P2T
G_NONE = G_TRAIL + QUARTER * U2T

NT = (((1,), (1,)), ((), ()))
NN = (((1,), (0,)), ((), ()))
F32 = jnp.float32


def split(x):
    high = x.astype(jnp.bfloat16)
    return high, (x - high.astype(F32)).astype(jnp.bfloat16)


def dot3(a, b, dims):
    def one(p, q):
        return lax.dot_general(p, q, dims, preferred_element_type=F32)

    return one(a[0], b[0]) + (one(a[0], b[1]) + one(a[1], b[0]))


def times_inverse(block, parts):
    wide = 2 * TILE
    size = parts[0].shape[0]
    block = split(block)
    return jnp.concatenate(
        [
            dot3([p[:, : c + wide] for p in block], [q[c : c + wide, : c + wide] for q in parts], NT)
            for c in range(0, size, wide)
        ],
        axis=1,
    )


def mul(a, b, dims):
    return dot3(split(a), split(b), dims)


def factor_half(block, width):
    groups = HALF // ROWS
    sub = lax.broadcasted_iota(jnp.int32, (ROWS, TILE), 0)
    lane = lax.broadcasted_iota(jnp.int32, (ROWS, TILE), 1)

    def full(x):
        return jnp.broadcast_to(x, (ROWS, TILE))

    wide = jnp.concatenate([block, jnp.zeros((HALF, HALF), F32)], axis=1)
    a = [
        jnp.where(lane == sub + ROWS * g + HALF, 1.0, wide[ROWS * g : ROWS * g + ROWS])
        for g in range(groups)
    ]
    rows = [None] * HALF
    for j in range(0, HALF, width):
        gj, o = j // ROWS, j % ROWS
        cols = {g: [full(a[g][:, j + i : j + i + 1]) for i in range(width)] for g in range(gj, groups)}
        s = [
            [full(cols[gj][k][o + i : o + i + 1, :]) if k <= i else None for k in range(width)]
            for i in range(width)
        ]
        u = [full(a[gj][o + i : o + i + 1, :]) for i in range(width)]
        inv = [None] * width
        low = [[None] * width for _ in range(width)]
        for k in range(width):
            inv[k] = 1.0 / s[k][k]
            for i in range(k + 1, width):
                low[i][k] = s[i][k] * inv[k]
            for i in range(k + 1, width):
                for q in range(k + 1, i + 1):
                    s[i][q] = s[i][q] - low[i][k] * s[q][k]
        for i in range(width):
            for k in range(i):
                u[i] = u[i] - low[i][k] * u[k]
            rows[j + i] = u[i] * lax.rsqrt(s[i][i])
        scaled = [u[i] * inv[i] for i in range(width)]
        for g in range(gj if o + width < ROWS else gj + 1, groups):
            c = cols[g]
            for i in range(width):
                for k in range(i):
                    c[i] = c[i] - c[k] * low[i][k]
            for i in range(width):
                a[g] = a[g] - c[i] * scaled[i]
    out = []
    for g in range(groups):
        v = rows[ROWS * g]
        for i in range(1, ROWS):
            v = jnp.where(sub == i, rows[ROWS * g + i], v)
        out.append(v)
    both = jnp.concatenate(out, axis=0)
    return both[:, :HALF], both[:, HALF:]


def factor(a, low, inv, tiles, width, start=0, stop=None):
    stop = tiles if stop is None else stop
    d = a[start * TILE : (start + 1) * TILE, start * TILE : (start + 1) * TILE]
    zero = jnp.zeros((HALF, HALF), F32)
    ri = lax.broadcasted_iota(jnp.int32, (HALF, HALF), 0)
    ci = lax.broadcasted_iota(jnp.int32, (HALF, HALF), 1)
    for k in range(start, stop):
        k0, k1, k2 = k * TILE, (k + 1) * TILE, (k + 2) * TILE
        u1, w1 = factor_half(d[:HALF, :HALF], width)
        l21 = mul(d[HALF:, :HALF], w1, NT)
        u2, w2 = factor_half(d[HALF:, HALF:] - mul(l21, l21, NT), width)
        w21 = -mul(w2, mul(l21, w1, NN), NN)
        w = jnp.concatenate([jnp.concatenate([w1, zero], 1), jnp.concatenate([w21, w2], 1)], 0)
        ws = split(w)
        inv[k0:k1, k0:k1] = w
        if k + 1 < tiles:
            p = dot3(split(a[k1:k2, k0:k1]), ws, NT)
            low[k1:k2, k0:k1] = p
            ps = split(p)
            d = a[k1:k2, k1:k2] - dot3(ps, ps, NT)
        l1 = jnp.where(ri >= ci, u1.T, 0.0)
        l2 = jnp.where(ri >= ci, u2.T, 0.0)
        low[k0:k1, k0:k1] = jnp.concatenate(
            [jnp.concatenate([l1, zero], 1), jnp.concatenate([l21, l2], 1)], 0
        )
        if k + 2 < tiles:
            low[k2:, k0:k1] = dot3(split(a[k2:, k0:k1]), ws, NT)
            for j in range(k + 1, tiles):
                j0 = j * TILE
                top = max(j0, k2)
                a[top:, j0 : j0 + TILE] = a[top:, j0 : j0 + TILE] - mul(
                    low[top:, k0:k1], low[j0 : j0 + TILE, k0:k1], NT
                )
        if k > 0:
            x = mul(low[k0:k1, 0:k0], inv[0:k0, 0:k0], NN)
            inv[k0:k1, 0:k0] = -dot3(ws, split(x), NN)
        if k + 1 < tiles:
            rest = jnp.zeros((TILE, (tiles - k - 1) * TILE), F32)
            low[k0:k1, k1:] = rest
            inv[k0:k1, k1:] = rest
    if stop < tiles:
        a[k1:k2, k1:k2] = d


def padded(a, tile_of, live, tiles):
    ri = lax.broadcasted_iota(jnp.int32, (TILE, TILE), 0)
    ci = lax.broadcasted_iota(jnp.int32, (TILE, TILE), 1)
    eye = jnp.where(ri == ci, 1.0, 0.0)
    for i in range(tiles):
        kept = (jnp.int32(i) < live).astype(F32)
        for j in range(i + 1):
            value = tile_of(i, j) * kept
            if i == j:
                value = value + eye * (1.0 - kept)
            a[i * TILE : (i + 1) * TILE, j * TILE : (j + 1) * TILE] = value


def copy_all(pairs, sems):
    copies = [pltpu.make_async_copy(src, dst, sems.at[n]) for n, (src, dst) in enumerate(pairs)]
    for c in copies:
        c.start()
    for c in copies:
        c.wait()


def tile_at(ref, row, col):
    return ref.at[
        pl.ds(pl.multiple_of(row * TILE, TILE), TILE), pl.ds(pl.multiple_of(col * TILE, TILE), TILE)
    ]


def square_index():
    return (
        lax.broadcasted_iota(jnp.int32, (TILE, TILE), 0),
        lax.broadcasted_iota(jnp.int32, (TILE, TILE), 1),
    )


def put_pairs(tiles_in, out, first):
    r, c = square_index()
    diagonals = []
    for n in range(0, len(tiles_in), 2):
        mixed = tiles_in[n]
        if n + 1 < len(tiles_in):
            mixed = jnp.where(r >= c, mixed, tiles_in[n + 1])
            diagonals.append(jnp.sum(jnp.where(r == c, tiles_in[n + 1], 0.0), axis=0, keepdims=True))
        out[pl.ds((first + n // 2) * TILE, TILE), :] = mixed
    diagonals += [jnp.zeros((1, TILE), F32)] * (ROWS - len(diagonals))
    out[pl.ds((first + (len(tiles_in) + 1) // 2) * TILE, ROWS), :] = jnp.concatenate(diagonals, axis=0)


def get_pairs(ref, first, count):
    r, c = square_index()
    base = (first + (count + 1) // 2) * TILE
    out = []
    for n in range(0, count, 2):
        mixed = ref[(first + n // 2) * TILE : (first + n // 2 + 1) * TILE, :]
        if n + 1 == count:
            out.append(mixed)
            continue
        other = mixed.T
        out.append(jnp.where(r >= c, mixed, other))
        diagonal = ref[base + n // 2 : base + n // 2 + 1, :]
        out.append(jnp.where(r == c, diagonal, jnp.where(r < c, mixed, other)))
    return out


def message_tile(ref, n):
    return ref[pl.ds(pl.multiple_of(n * TILE, TILE), TILE), :]


def pack_first(tab, block, pivot, out, square, sems):
    side = tab[CT]
    pairs = []
    for n, (a, b) in enumerate(BELOW_C):
        pairs.append((tile_at(block, tab[a], tab[b]), out.at[pl.ds(n * TILE, TILE)]))
    first = len(BELOW_C)
    for n, (a, b) in enumerate(BELOW_P):
        pairs.append(
            (tile_at(pivot, a, side * (P1T // 2) + b), out.at[pl.ds((first + n) * TILE, TILE)])
        )
    for a in range(CT):
        pairs.append((tile_at(block, tab[a], tab[a]), square.at[a]))
    for a in range(P1T // 2):
        pairs.append((tile_at(pivot, a, side * (P1T // 2) + a), square.at[CT + a]))
    copy_all(pairs, sems)
    put_pairs([square[n] for n in range(DIAG_FIRST)], out, first + len(BELOW_P))


def pack_rest(
    tab, block, pivot, rows, pivot_second, second,
    coup, own, kept, cross, off, own_sent, coup_two, units, units_sent, main, two_sent_a, two_sent_b, over,
    strips, sems,
):
    side = tab[CT]
    order = CT + 1
    local = order + CT
    quarter = tab[local + U1T]
    pairs = []
    for r in range(HALF_U):
        row = tab[local + r] - side * HALF_U
        for c in range(P1T):
            pairs.append((tile_at(rows, row, c), coup.at[r * P1T + c]))
    for n, (a, b) in enumerate(TRI_U):
        row = tab[local + a] - side * HALF_U
        pairs.append((tile_at(rows, row, P1T + tab[local + b]), own.at[n]))
    for n, (a, b) in enumerate(TRI_C):
        pairs.append((tile_at(block, tab[order + a], tab[order + b]), kept.at[n]))
    for i in range(HALF_U):
        row = tab[local + i] - side * HALF_U
        for k in range(HALF_U):
            pairs.append(
                (tile_at(rows, row, P1T + tab[local + HALF_U + k]), cross.at[i * HALF_U + k])
            )
    for i in range(P1T // 2):
        for k in range(P1T // 2):
            pairs.append(
                (tile_at(pivot, i, (1 - side) * (P1T // 2) + k), off.at[i * (P1T // 2) + k])
            )
    for n, (i, k) in enumerate(TRI_P):
        pairs.append((tile_at(pivot, i, side * (P1T // 2) + k), off.at[N_OFF + n]))
    for r in range(QUARTER):
        for c in range(P2T):
            pairs.append((tile_at(second, r, c), coup_two.at[r * P2T + c]))
    first = local + U1T + 1
    for p in range(N_COUP):
        n = tab[first + p]
        row = tab[local + n // P1T] - side * HALF_U
        sent = main.at[p] if p < N_MAIN else over.at[p - N_MAIN]
        pairs.append((tile_at(rows, row, n % P1T), sent))
    first += N_COUP
    for p in range(N_TWO):
        n = tab[first + p]
        if p < N_TWO_A:
            sent = two_sent_a.at[p]
        elif p < N_TWO_A + N_TWO_B:
            sent = two_sent_b.at[p - N_TWO_A]
        else:
            sent = over.at[p + N_COUP - N_MAIN - N_TWO_A - N_TWO_B]
        pairs.append((tile_at(second, n // P2T, n % P2T), sent))
    far = []
    for i in range(OWN_UNITS):
        for d in range(REACH):
            col = (quarter * OWN_UNITS + i - d + UNITS) % UNITS
            far.append(col % 2)
            source = pivot_second.at[
                pl.ds(i * HALF, HALF), pl.ds(pl.multiple_of(col // 2 * TILE, TILE), TILE)
            ]
            pairs.append((source, strips.at[i * REACH + d]))
    copy_all(pairs, sems)
    lane = lax.broadcasted_iota(jnp.int32, (HALF, TILE), 1)

    def placed(n, half):
        strip = strips[n]
        return jnp.where(far[n] == half, strip, pltpu.roll(strip, HALF, 1))

    for n in range(N_WIDE):
        strip = placed(2 * n, 0)
        if 2 * n + 1 < N_UNIT:
            strip = jnp.where(lane < HALF, strip, placed(2 * n + 1, 1))
        units[n * HALF : (n + 1) * HALF, :] = strip
        units_sent[n * HALF : (n + 1) * HALF, :] = strip
    put_own([own[n] for n in range(N_TRI)], own_sent)


def after(array, *others):
    def kernel(*refs):
        pass

    return pl.pallas_call(
        kernel,
        out_shape=jax.ShapeDtypeStruct(array.shape, array.dtype),
        in_specs=[HBM] * (1 + len(others)),
        out_specs=HBM,
        input_output_aliases={0: 0},
        name="after",
        cost_estimate=CHEAP,
    )(array, *others)


T_SIDE = 0
T_LIVE = 1
T_LOCAL = 2
T_FILL = T_LOCAL + U1T
T_SLOT = T_FILL + U1T * P1T
T_SLOT_FAR = T_SLOT + CT * CT
T_PLACE = T_SLOT_FAR + CT * CT


def panel_rows(tile_of, count, live, inv, put):
    parts = split(inv)
    for r in range(0, count, 2):
        block = jnp.concatenate(
            [
                jnp.concatenate([tile_of(r + i, c) for c in range(P1T)], axis=1)
                for i in range(2)
            ],
            axis=0,
        )
        lane = lax.broadcasted_iota(jnp.int32, block.shape, 1)
        block = jnp.where(lane < live * TILE, block, 0.0)
        put(r, times_inverse(block, parts))


def first_kernel(
    tab, mine, theirs, coup, own, cross, off,
    lower_out, inv_out, panel_out, rows_out, own_out, far_out,
    front, a, low, sem,
):
    side = tab[T_SIDE]
    live = tab[T_LIVE]
    half = P1T // 2
    square = get_pairs(theirs, len(BELOW_C) + len(BELOW_P), DIAG_FIRST)
    front[0:N_PIV] = jnp.zeros((N_PIV, TILE, TILE), F32)
    for n, (i, k) in enumerate(TRI_P):
        front[(side * half + i) * P1T + side * half + k] = off[N_OFF + n]
        if i == k:
            tile = square[CT + i]
        else:
            tile = message_tile(theirs, len(BELOW_C) + BELOW_P.index((i, k)))
        front[((1 - side) * half + i) * P1T + (1 - side) * half + k] = tile
    for i in range(half):
        for k in range(half):

            @pl.when(side == 0)
            def _():
                front[(half + k) * P1T + i] = off[i * half + k].T

            @pl.when(side != 0)
            def _():
                front[(half + i) * P1T + k] = off[i * half + k]

    def scale(n, carry):
        front[S_COUP + n] = coup[n] * tab[T_FILL + n].astype(F32)
        front[S_FAR + n] = jnp.zeros((TILE, TILE), F32)
        front[S_CROSS + n] = cross[n]
        return carry

    lax.fori_loop(0, N_COUP, scale, 0)

    def copy(n, carry):
        front[S_OWN + n] = own[n]
        front[S_OTH + n] = jnp.zeros((TILE, TILE), F32)
        return carry

    lax.fori_loop(0, N_TRI, copy, 0)
    for i in range(CT):

        def extend(k, carry, i=i):
            here = tab[T_SLOT + i * CT + k]
            front[here] = front[here] + mine[tri(i, 0) + k]
            return carry

        lax.fori_loop(0, i + 1, extend, 0)

        def extend_far(k, carry, i=i):
            there = tab[T_SLOT_FAR + i * CT + k]
            front[there] = front[there] + message_tile(theirs, i * (i - 1) // 2 + k)
            return carry

        lax.fori_loop(0, i, extend_far, 0)
        there = tab[T_SLOT_FAR + i * CT + i]
        front[there] = front[there] + square[i]
    leave = pltpu.make_async_copy(front.at[pl.ds(S_FAR, N_FRONT - S_FAR)], far_out, sem)
    leave.start()
    padded(a, lambda i, j: front[i * P1T + j], live, P1T)
    factor(a, low, inv_out, P1T, 4)
    lower_out[...] = low[pl.ds(pl.multiple_of(side * (PIVOT // 2), TILE), PIVOT // 2), :]

    def put(r, rows):
        panel_out[r * TILE : (r + 2) * TILE, :] = rows
        for i in range(2):
            place = tab[T_LOCAL + r + i] - side * HALF_U
            rows_out[pl.ds(pl.multiple_of(place * TILE, TILE), TILE), :] = rows[
                i * TILE : (i + 1) * TILE
            ]

    panel_rows(lambda r, c: front[S_COUP + r * P1T + c], HALF_U, live, inv_out[...], put)
    for i in range(HALF_U):
        left = split(panel_out[i * TILE : (i + 1) * TILE, :])
        product = dot3(left, split(panel_out[0 : (i + 1) * TILE, :]), NT)
        for k in range(i + 1):
            own_out[tri(i, k)] = front[S_OWN + tri(i, k)] - product[:, k * TILE : (k + 1) * TILE]
    leave.wait()


def choose(at, parts):
    value = None
    base = sum(count for _, _, count in parts)
    for ref, first, count in reversed(parts):
        base -= count
        tile = ref[first + jnp.clip(at - base, 0, count - 1)]
        value = tile if value is None else jnp.where(at < base + count, tile, value)
    return value


def second_kernel(tab, far, main, over, inv, panel, cross_a, cross_b, panel_far):
    live = tab[T_LIVE]

    def tile_of(r, c):
        n = r * P1T + c
        tile = choose(tab[T_PLACE + n], [(main, 0, N_MAIN), (over, 0, N_COUP - N_MAIN)])
        return far[n] + tile * tab[T_FILL + N_COUP + n].astype(F32)

    def put(r, rows):
        panel_far[r * TILE : (r + 2) * TILE, :] = rows

    panel_rows(tile_of, HALF_U, live, inv[...], put)
    right = split(panel_far[...])
    for i in range(0, HALF_U, 2):
        product = dot3(split(panel[i * TILE : (i + 2) * TILE, :]), right, NT)
        for q in range(2):
            for k in range(HALF_U):
                n = (i + q) * HALF_U + k
                out, first = (cross_a, 0) if n < N_CROSS_A else (cross_b, N_CROSS_A)
                out[n - first] = (
                    far[N_COUP + n]
                    - product[q * TILE : (q + 1) * TILE, k * TILE : (k + 1) * TILE]
                )


def other_kernel(far, panel_far, out, part, sem):
    enter = pltpu.make_async_copy(far.at[pl.ds(N_COUP + N_CROSS, N_TRI)], part, sem)
    enter.start()
    enter.wait()
    for i in range(HALF_U):
        left = split(panel_far[i * TILE : (i + 1) * TILE, :])
        product = dot3(left, split(panel_far[0 : (i + 1) * TILE, :]), NT)
        for k in range(i + 1):
            out[tri(i, k)] = part[tri(i, k)] - product[:, k * TILE : (k + 1) * TILE]


def add_kernel(part, got, out, sent):
    square = get_pairs(got, len(BELOW_U), HALF_U)
    for n, (i, k) in enumerate(BELOW_U):
        out[tri(i, k)] = part[tri(i, k)] + message_tile(got, n)
    for i in range(HALF_U):
        out[tri(i, i)] = part[tri(i, i)] + square[i]
    put_own([out[n] for n in range(N_TRI)], sent)


def put_own(block, out):
    for n, (a, b) in enumerate(BELOW_U):
        out[n * TILE : (n + 1) * TILE, :] = block[tri(a, b)]
    put_pairs([block[tri(a, a)] for a in range(HALF_U)], out, len(BELOW_U))


def get_own(ref, out):
    for n, (i, k) in enumerate(BELOW_U):
        out[tri(i, k)] = message_tile(ref, n)
    for i, tile in enumerate(get_pairs(ref, len(BELOW_U), HALF_U)):
        out[tri(i, i)] = tile


Q_LIVE = 0
Q_MINE = 1
Q_FILL = 5
Q_DIRECT = Q_FILL + U2T * P2T
Q_TURNED = Q_DIRECT + 2 * U1T * U1T
Q_PLACE = Q_TURNED + 2 * U1T * U1T


def extend_cross(tab, refs, g, front, low, high):
    for q, ref in enumerate(refs):
        extend_two(tab, ref, g, front, q * HALF_U // 2, HALF_U, False, low, high, HALF_U // 2)


def extend_two(tab, ref, g, front, rows, cols, triangle, low, high, count=HALF_U):
    for i in range(count):

        def one(k, carry, i=i):
            at = front * U1T * U1T + (rows + i) * U1T + cols + k
            n = (tri(i, 0) if triangle else i * HALF_U) + k
            direct = tab[Q_DIRECT + at]
            turned = tab[Q_TURNED + at]

            @pl.when((direct >= low) & (direct < high))
            def _():
                g[direct - low] = g[direct - low] + ref[n]

            @pl.when((turned >= low) & (turned < high))
            def _():
                g[turned - low] = g[turned - low] + ref[n].T

            return carry

        lax.fori_loop(0, i + 1 if triangle else HALF_U, one, 0)


def add_units(tab, g, units, s):
    lane = lax.broadcasted_iota(jnp.int32, (HALF, TILE), 1)
    for i in range(OWN_UNITS):
        row = tab[Q_MINE + s] * OWN_UNITS + i
        for d in range(REACH):
            n = i * REACH + d
            col = (row - d + UNITS) % UNITS
            strip = units[n // 2 * HALF : (n // 2 + 1) * HALF, :]
            here = n % 2

            def add(r, c, block):
                slot = r // 2 * P2T + c // 2
                start = pl.multiple_of(r % 2 * HALF, HALF)
                old = g[slot, pl.ds(start, HALF), :]
                g[slot, pl.ds(start, HALF), :] = old + jnp.where(lane // HALF == c % 2, block, 0.0)

            @pl.when((col <= row) & ((d < REACH - 1) | (row >= UNITS // 2)))
            def _():
                add(row, col, jnp.where(col % 2 == here, strip, pltpu.roll(strip, HALF, 1)))

            if d < REACH - 1 and d > 0:

                @pl.when(col > row)
                def _():
                    turned = strip.T[here * HALF : (here + 1) * HALF, :]
                    add(col, row, jnp.concatenate([turned, turned], axis=1))


def third_kernel(tab, own0, cross0_a, cross0_b, own1, units0, units2, second, g):
    def clear(n, carry):
        g[n] = jnp.zeros((TILE, TILE), F32)
        return carry

    lax.fori_loop(0, G_TRAIL, clear, 0)
    for r in range(QUARTER):
        for c in range(U2T):
            g[G_TRAIL + r * U2T + c] = second[
                r * TILE : (r + 1) * TILE, SECOND + c * TILE : SECOND + (c + 1) * TILE
            ]
    add_units(tab, g, units0, 0)
    add_units(tab, g, units2, 2)
    extend_two(tab, own0, g, 0, 0, 0, True, 0, G_NONE)
    extend_cross(tab, (cross0_a, cross0_b), g, 0, 0, G_NONE)
    extend_two(tab, own1, g, 1, 0, 0, True, 0, G_NONE)


def more_kernel(tab, part, cross1_a, cross1_b, oth0, units1, g, sem):
    enter = pltpu.make_async_copy(part, g, sem)
    enter.start()
    enter.wait()
    add_units(tab, g, units1, 1)
    extend_cross(tab, (cross1_a, cross1_b), g, 1, 0, G_NONE)
    extend_two(tab, oth0, g, 0, HALF_U, HALF_U, True, 0, G_NONE)


def pivot_kernel(tab, part, oth1, units3, lower_out, high_out, rest_out, g, other, a, low, inv, sem):
    enter = pltpu.make_async_copy(part.at[pl.ds(0, G_COUP)], g, sem)
    enter.start()
    get_own(oth1, other)
    enter.wait()
    add_units(tab, g, units3, 3)
    extend_two(tab, other, g, 1, HALF_U, HALF_U, True, 0, G_COUP)
    padded(a, lambda i, j: g[i * P2T + j], tab[Q_LIVE], P2T)
    factor(a, low, inv, P2T, 8)
    start = tab[Q_MINE] * (SECOND // 4)
    lower_out[...] = low[pl.ds(pl.multiple_of(start, HALF), SECOND // 4), :]
    high_out[...], rest_out[...] = split(inv[...])


def quarter_rows_of(tab, g, quarter):
    return jnp.concatenate(
        [
            jnp.concatenate([g[(quarter * QUARTER + r) * P2T + c] for c in range(P2T)], axis=1)
            for r in range(QUARTER)
        ],
        axis=0,
    )


def placed_two(tab, which, first, second, over):
    parts = [
        (first, 0, N_TWO_A),
        (second, 0, N_TWO_B),
        (over, N_COUP - N_MAIN, N_TWO - N_TWO_A - N_TWO_B),
    ]
    return lambda n: choose(tab[Q_PLACE + which * N_TWO + n], parts)


def quarter_panel(tab, block, coup, parts, quarter):
    rows = []
    for r in range(QUARTER):
        fill = Q_FILL + (quarter * QUARTER + r) * P2T
        rows.append(
            jnp.concatenate(
                [coup(r * P2T + c) * tab[fill + c].astype(F32) for c in range(P2T)], axis=1
            )
        )
    block = block + jnp.concatenate(rows, axis=0)
    lane = lax.broadcasted_iota(jnp.int32, block.shape, 1)
    block = jnp.where(lane < tab[Q_LIVE] * TILE, block, 0.0)
    return times_inverse(block, parts)


WIDE = QUARTER * TILE


def rows_kernel(
    tab, part, oth1, high, low, coup0, coup1_a, coup1_b, over, coup2,
    panel_out, schur_out, rest_out,
    g, other, panels, sem,
):
    enter = pltpu.make_async_copy(part.at[pl.ds(G_COUP, G_NONE - G_COUP)], g, sem)
    enter.start()
    get_own(oth1, other)
    enter.wait()
    extend_two(tab, other, g, 1, HALF_U, HALF_U, True, G_COUP, G_NONE)
    parts = high[...], low[...]
    rest_out[...] = quarter_rows_of(tab, g, tab[Q_MINE + 3])
    whole = [lambda n, ref=ref: ref[n] for ref in (coup0, coup2)]
    for s, coup in enumerate((whole[0], placed_two(tab, 0, coup1_a, coup1_b, over), whole[1])):
        quarter = tab[Q_MINE + s]
        panel = quarter_panel(tab, quarter_rows_of(tab, g, quarter), coup, parts, quarter)
        panels[s] = panel
        if s == 0:
            panel_out[...] = panel
    left = split(panel_out[...])
    for s in range(4):
        quarter = tab[Q_MINE + s]
        if s < 3:
            product = dot3(left, split(panels[s]), NT)
        for r in range(QUARTER):
            for c in range(QUARTER):
                tile = g[G_TRAIL - G_COUP + r * U2T + quarter * QUARTER + c]
                if s < 3:
                    tile = tile - product[r * TILE : (r + 1) * TILE, c * TILE : (c + 1) * TILE]
                col = pl.multiple_of((quarter * QUARTER + c) * TILE, TILE)
                schur_out[r * TILE : (r + 1) * TILE, pl.ds(col, TILE)] = tile


def last_kernel(tab, schur, rest, panel, high, low, coup_a, coup_b, over, out, block, sem):
    quarter = tab[Q_MINE + 3]
    col = pl.ds(pl.multiple_of(quarter * WIDE, TILE), WIDE)
    enter = pltpu.make_async_copy(schur.at[:, col], block, sem)
    enter.start()
    coup = placed_two(tab, 1, coup_a, coup_b, over)
    other = quarter_panel(tab, rest[...], coup, (high[...], low[...]), quarter)
    product = dot3(split(panel[...]), split(other), NT)
    enter.wait()
    block[...] = block[...] - product
    leave = pltpu.make_async_copy(block, out.at[:, col], sem)
    leave.start()
    leave.wait()


def swap(array, axis):
    size = lax.axis_size(axis)
    return lax.ppermute(array, axis, [(i, i ^ (size // 2)) for i in range(size)])


def tiles(count):
    return jax.ShapeDtypeStruct((count, TILE, TILE), F32)


def dense(rows, cols):
    return jax.ShapeDtypeStruct((rows, cols), F32)


SMEM = pl.BlockSpec(memory_space=pltpu.SMEM)
VMEM = pl.BlockSpec(memory_space=pltpu.VMEM)
HBM = pl.BlockSpec(memory_space=pl.ANY)
LIMIT = 60 << 20
CHEAP = pl.CostEstimate(flops=1, bytes_accessed=1, transcendentals=0)


def call(kernel, name, out_shape, in_specs, out_specs, scratch=(), waits=(), limit=LIMIT, **options):
    count = len(in_specs)

    def body(*refs):
        kernel(*refs[:count], *refs[count + len(waits) :])

    run = pl.pallas_call(
        body,
        out_shape=out_shape,
        in_specs=in_specs + [HBM] * len(waits),
        out_specs=out_specs,
        scratch_shapes=list(scratch),
        name=name,
        compiler_params=pltpu.CompilerParams(vmem_limit_bytes=limit),
        cost_estimate=CHEAP,
        **options,
    )
    return lambda *args: run(*args, *waits)


def tri(i, k):
    return i * (i + 1) // 2 + k


def local_order(second_map, side):
    unit = jnp.arange(U1T, dtype=jnp.int32)
    rank = second_map + jnp.where(unit // HALF_U == side, 0, P2T + U2T)
    place = jnp.sum((rank[None, :] < rank[:, None]).astype(jnp.int32), axis=1)
    hit = (place[None, :] == unit[:, None]).astype(jnp.int32)
    return place, hit


def place_of(child_map, place):
    unit = jnp.arange(U1T, dtype=jnp.int32)
    hit = (child_map[:, None] - P1T == unit[None, :]).astype(jnp.int32)
    return jnp.where(child_map < P1T, child_map, P1T + jnp.sum(hit * place[None, :], axis=1))


def sort_by(key):
    spot = jnp.sum((key[None, :] < key[:, None]).astype(jnp.int32), axis=1)
    hit = (spot[None, :] == jnp.arange(CT, dtype=jnp.int32)[:, None]).astype(jnp.int32)
    order = jnp.sum(hit * jnp.arange(CT, dtype=jnp.int32)[None, :], axis=1)
    return order, jnp.sum(hit * key[None, :], axis=1)


def turned_key(key):
    return jnp.where(key < P1T, key, P1T + (key - P1T + HALF_U) % U1T)


def slots(keys):
    row = keys[:, None]
    col = keys[None, :]
    own = P1T + HALF_U
    pivot = row * P1T + col
    coup = jnp.where(row >= own, S_COUP + (row - own) * P1T, S_FAR + (row - P1T) * P1T) + col
    near = S_OWN + tri(row - own, col - own)
    cross = S_CROSS + (row - own) * HALF_U + col - P1T
    other = S_OTH + tri(row - P1T, col - P1T)
    rest = jnp.where(row < own, other, jnp.where(col < own, cross, near))
    return jnp.where(row < P1T, pivot, jnp.where(col < P1T, coup, rest)).reshape(-1)


def needed_first(need):
    need = need.reshape(-1)
    count = need.shape[0]
    at = jnp.arange(count, dtype=jnp.int32)
    key = at + jnp.where(need > 0, 0, count)
    place = jnp.sum((key[None, :] < key[:, None]).astype(jnp.int32), axis=1)
    order = jnp.sum((place[None, :] == at[:, None]).astype(jnp.int32) * at[None, :], axis=1)
    return place, order


def needed(fill, live):
    return fill * (jnp.arange(fill.shape[-1], dtype=jnp.int32) < live[..., None, None])


def targets(goal, quarter):
    row = goal[:, None]
    col = goal[None, :]

    def index(r, c):
        mine = (r - P2T) // QUARTER == quarter
        coup = G_COUP + (r - P2T) * P2T + c
        trail = G_TRAIL + (r - P2T - quarter * QUARTER) * U2T + c - P2T
        rest = jnp.where(c < P2T, coup, jnp.where(mine, trail, G_NONE))
        return jnp.where(r < P2T, jnp.where((c < P2T) & (r >= c), r * P2T + c, G_NONE), rest)

    direct = index(row, col)
    turned = jnp.where(row == col, G_NONE, index(col, row))
    return direct.reshape(-1), turned.reshape(-1)


def body(
    contribution,
    pivot_one,
    rows_one,
    pivot_two,
    rows_two,
    map_one,
    map_two,
    fill_one,
    fill_two,
    live_one,
    live_two,
):
    size_lo = lax.axis_size("lo")
    size_hi = lax.axis_size("hi")
    half_lo = size_lo // 2
    half_hi = size_hi // 2
    index_lo = lax.axis_index("lo")
    index_hi = lax.axis_index("hi")
    side_lo = index_lo // half_lo
    side_hi = index_hi // half_hi
    front_lo = index_lo % half_lo
    front_hi = index_hi % half_hi
    far_lo = (index_lo + half_lo) % size_lo
    far_hi = (index_hi + half_hi) % size_hi
    quarter = 2 * side_hi + side_lo
    block, pivot, rows = contribution[0, 0], pivot_one[0, 0], rows_one[0, 0]
    pivot_second, rows_second = pivot_two[0, 0], rows_two[0, 0]

    second_map = map_two[index_hi, front_lo]
    place, hit = local_order(second_map, side_lo)
    key = place_of(map_one[index_hi, index_lo], place)
    order_sent, _ = sort_by(key)
    tab_first = jnp.concatenate([order_sent, side_lo[None]]).astype(jnp.int32)
    sent = call(
        pack_first,
        "pack_first",
        dense(N_FIRST * TILE + ROWS, TILE),
        [SMEM, HBM, HBM],
        VMEM,
        [
            pltpu.VMEM((DIAG_FIRST, TILE, TILE), F32),
            pltpu.SemaphoreType.DMA((len(TRI_C) + len(TRI_P),)),
        ],
    )(tab_first, block, pivot)
    got_first = swap(sent, "lo")

    unit = jnp.arange(U1T, dtype=jnp.int32)
    local = jnp.sum(hit * unit[None, :], axis=1)
    order_kept, keys = sort_by(turned_key(key))
    live_first = live_one[index_hi, front_lo]
    need_first = needed(
        jnp.sum(hit[:, :, None] * fill_one[index_hi, front_lo][None, :, :], axis=1), live_first
    )
    live_second = live_two[front_hi, front_lo]
    need_second = needed(fill_two[front_hi, front_lo], live_second)

    def place_second(which):
        return needed_first(
            lax.dynamic_slice_in_dim(need_second, which * QUARTER, QUARTER, 0)
        )

    _, order_main = needed_first(need_first[:HALF_U])
    _, order_two = place_second(quarter)
    tab_rest = jnp.concatenate(
        [tab_first, order_kept, local, quarter[None], order_main, order_two]
    ).astype(jnp.int32)
    shapes = [
        tiles(N_COUP), tiles(N_TRI), tiles(len(TRI_C)), tiles(N_CROSS), tiles(N_OFF + len(TRI_P)),
        dense(N_OWN * TILE + ROWS, TILE), tiles(N_TWO),
        dense(N_WIDE * HALF, TILE), dense(N_WIDE * HALF, TILE),
        tiles(N_MAIN), tiles(N_TWO_A), tiles(N_TWO_B), tiles(N_OVER),
    ]
    n_rest = 2 * N_COUP + N_TRI + len(TRI_C) + N_CROSS + N_OFF + len(TRI_P) + 2 * N_TWO + N_UNIT
    coup, own, kept, cross, off, own_sent, two, units, units_sent, main, two_a, two_b, over = call(
        pack_rest,
        "pack_rest",
        shapes,
        [SMEM] + [HBM] * 5,
        [VMEM] * len(shapes),
        [pltpu.VMEM((N_UNIT, HALF, TILE), F32), pltpu.SemaphoreType.DMA((n_rest,))],
        waits=(sent,),
    )(tab_rest, block, pivot, rows, pivot_second, rows_second)
    two_hi = swap(two, "hi")
    units_hi = swap(units, "hi")
    far_key = place_of(map_one[index_hi, far_lo], place)
    _, far_keys = sort_by(turned_key(far_key))
    place_main, _ = needed_first(need_first[HALF_U:])
    tab_one = jnp.concatenate(
        [side_lo[None], live_first[None], local, need_first.reshape(-1), slots(keys), slots(far_keys), place_main]
    ).astype(jnp.int32)
    map_far = map_two[far_hi, front_lo]
    _, hit_far = local_order(map_far, side_lo)
    direct, turned = targets(jnp.sum(hit * second_map[None, :], axis=1), quarter)
    direct_far, turned_far = targets(jnp.sum(hit_far * map_far[None, :], axis=1), quarter)
    place_lo, _ = place_second(2 * side_hi + 1 - side_lo)
    place_both, _ = place_second(2 * (1 - side_hi) + 1 - side_lo)
    quarters = jnp.stack(
        [quarter, 2 * side_hi + 1 - side_lo, 2 * (1 - side_hi) + side_lo, 2 * (1 - side_hi) + 1 - side_lo]
    )
    tab_two = jnp.concatenate(
        [
            live_second[None], quarters, need_second.reshape(-1),
            direct, direct_far, turned, turned_far, place_lo, place_both,
        ]
    ).astype(jnp.int32)
    most = jnp.max(jnp.sum(needed(fill_one, live_one).reshape(-1, N_COUP), axis=1))
    most_two = jnp.max(jnp.sum(needed(fill_two, live_two).reshape(-1, N_TWO), axis=1))

    def send_over(array):
        got = swap(array, "lo")
        return got, swap(got, "hi")

    over_got, over_both = lax.cond(
        (most > N_MAIN) | (most_two > N_TWO_A + N_TWO_B),
        send_over,
        lambda array: (array, array),
        over,
    )
    main = after(main, got_first, two_hi, units_hi, tab_one, tab_two, over_got, over_both)
    got_main = swap(main, "lo")

    half_rows = HALF_U * TILE
    lower_one, inv_one, panel_own, panel_one, s_own, far_part = call(
        first_kernel,
        "first_front_own",
        [
            dense(PIVOT // 2, PIVOT), dense(PIVOT, PIVOT), dense(half_rows, PIVOT),
            dense(half_rows, PIVOT), tiles(N_TRI), tiles(N_FRONT - S_FAR),
        ],
        [SMEM] + [VMEM] * 6,
        [VMEM] * 5 + [HBM],
        [
            pltpu.VMEM((N_FRONT, TILE, TILE), F32),
            pltpu.VMEM((PIVOT, PIVOT), F32),
            pltpu.VMEM((PIVOT, PIVOT), F32),
            pltpu.SemaphoreType.DMA,
        ],
    )(tab_one, kept, got_first, coup, own, cross, off)
    s_own_far = swap(s_own, "hi")
    own_sent = after(own_sent, got_main, panel_own)
    got_own = swap(own_sent, "lo")

    cross_a, cross_b, panel_far = call(
        second_kernel,
        "first_front_other",
        [tiles(N_CROSS_A), tiles(N_CROSS - N_CROSS_A), dense(half_rows, PIVOT)],
        [SMEM] + [VMEM] * 5,
        [VMEM] * 3,
        waits=(s_own_far, own_sent),
    )(tab_one, far_part, got_main, over_got, inv_one, panel_own)
    cross_a_far, cross_b_far = swap(cross_a, "hi"), swap(cross_b, "hi")
    s_part = call(
        other_kernel,
        "first_front_block",
        tiles(N_TRI),
        [HBM, VMEM],
        VMEM,
        [pltpu.VMEM((N_TRI, TILE, TILE), F32), pltpu.SemaphoreType.DMA],
    )(far_part, panel_far)
    part = call(third_kernel, "second_front_part", tiles(G_NONE), [SMEM] + [VMEM] * 7, VMEM)(
        tab_two, s_own, cross_a, cross_b, s_own_far, units, units_hi, rows_second
    )
    got_units = swap(after(units_sent, got_own, part), "lo")
    s_oth, s_oth_sent = call(
        add_kernel,
        "first_front_last",
        [tiles(N_TRI), dense(N_OWN * TILE + ROWS, TILE)],
        [VMEM] * 2,
        [VMEM] * 2,
        waits=(part,),
    )(s_part, got_own)
    s_oth_far = swap(s_oth_sent, "hi")
    units_both = swap(got_units, "hi")
    got_two_a = swap(after(two_a, got_units, s_oth, cross_a_far, cross_b_far), "lo")
    part = call(
        more_kernel,
        "second_front_more",
        tiles(G_NONE),
        [SMEM, HBM] + [VMEM] * 4,
        VMEM,
        [pltpu.SemaphoreType.DMA],
    )(tab_two, part, cross_a_far, cross_b_far, s_oth, got_units)
    two_b = after(two_b, got_two_a, units_both, s_oth_far, part)
    got_two_b = swap(two_b, "lo")
    two_a_both = swap(got_two_a, "hi")
    half = jax.ShapeDtypeStruct((SECOND, SECOND), jnp.bfloat16)
    square = pltpu.VMEM((SECOND, SECOND), F32)
    lower_two, inv_high, inv_low = call(
        pivot_kernel,
        "second_front_pivot",
        [dense(SECOND // 4, SECOND), half, half],
        [SMEM, HBM] + [VMEM] * 2,
        [VMEM] * 3,
        [
            pltpu.VMEM((G_COUP, TILE, TILE), F32),
            pltpu.VMEM((N_TRI, TILE, TILE), F32),
            square, square, square,
            pltpu.SemaphoreType.DMA,
        ],
        waits=(two_b,),
    )(tab_two, part, s_oth_far, units_both)
    got_two_b = after(got_two_b, lower_two)
    two_b_both = swap(got_two_b, "hi")
    panel_two, schur, rest = call(
        rows_kernel,
        "second_front_rows",
        [dense(WIDE, SECOND), dense(WIDE, U2T * TILE), dense(WIDE, SECOND)],
        [SMEM, HBM] + [VMEM] * 8,
        [VMEM] * 3,
        [
            pltpu.VMEM((G_NONE - G_COUP, TILE, TILE), F32),
            pltpu.VMEM((N_TRI, TILE, TILE), F32),
            pltpu.VMEM((3, WIDE, SECOND), F32),
            pltpu.SemaphoreType.DMA,
        ],
    )(tab_two, part, s_oth_far, inv_high, inv_low, two, got_two_a, got_two_b, over_got, two_hi)
    schur_two = call(
        last_kernel,
        "second_front_last",
        dense(WIDE, U2T * TILE),
        [SMEM, HBM] + [VMEM] * 7,
        HBM,
        [pltpu.VMEM((WIDE, WIDE), F32), pltpu.SemaphoreType.DMA],
        input_output_aliases={1: 0},
    )(tab_two, schur, rest, panel_two, inv_high, inv_low, two_a_both, two_b_both, over_both)
    return (
        lower_one[None, None],
        panel_one[None, None],
        lower_two[None, None],
        panel_two[None, None],
        schur_two[None, None],
    )


def solution(mesh):
    split_both = P("hi", "lo", None, None)
    return jax.shard_map(
        body,
        mesh=mesh,
        in_specs=(split_both,) * 5 + (P(),) * 6,
        out_specs=(split_both,) * 5,
        check_vma=False,
    )
```

```python
import functools

import jax
import jax.numpy as jnp
import numpy as np
from jax import lax
from jax.experimental import pallas as pl
from jax.experimental.pallas import tpu as pltpu
from jax.sharding import PartitionSpec as P

TILE = 128
HALF = TILE // 2
CT = 8
P1T = 6
U1T = 12
P2T = 6
U2T = 12
ROWS = 8

HALF_U = U1T // 2
QUARTER = U2T // 4
PIVOT = P1T * TILE
SECOND = P2T * TILE

TRI_C = [(a, b) for a in range(CT) for b in range(a + 1)]
TRI_U = [(a, b) for a in range(HALF_U) for b in range(a + 1)]
TRI_P = [(a, b) for a in range(P1T // 2) for b in range(a + 1)]
BELOW_C = [(a, b) for a, b in TRI_C if a != b]
BELOW_U = [(a, b) for a, b in TRI_U if a != b]
BELOW_P = [(a, b) for a, b in TRI_P if a != b]
DIAG_FIRST = CT + P1T // 2
N_FIRST = len(BELOW_C) + len(BELOW_P) + (DIAG_FIRST + 1) // 2
N_OWN = len(BELOW_U) + (HALF_U + 1) // 2
UNITS = SECOND // HALF
OWN_UNITS = UNITS // 4
REACH = UNITS // 2 + 1
N_UNIT = OWN_UNITS * REACH
N_WIDE = (N_UNIT + 1) // 2
N_TWO = QUARTER * P2T
N_MAIN = 30
N_TWO_A = 5
N_TWO_B = 11
N_OFF = (P1T // 2) ** 2
N_PIV = P1T * P1T
N_COUP = HALF_U * P1T
N_TRI = len(TRI_U)
N_CROSS = HALF_U * HALF_U
N_CROSS_A = N_CROSS // 2
N_OVER = N_COUP - N_MAIN + N_TWO - N_TWO_A - N_TWO_B
S_COUP = N_PIV
S_OWN = S_COUP + N_COUP
S_FAR = S_OWN + N_TRI
S_CROSS = S_FAR + N_COUP
S_OTH = S_CROSS + N_CROSS
N_FRONT = S_OTH + N_TRI
G_COUP = P2T * P2T
G_TRAIL = G_COUP + U2T * P2T
G_NONE = G_TRAIL + QUARTER * U2T

NT = (((1,), (1,)), ((), ()))
NN = (((1,), (0,)), ((), ()))
F32 = jnp.float32


def split(x):
    high = x.astype(jnp.bfloat16)
    return high, (x - high.astype(F32)).astype(jnp.bfloat16)


def dot3(a, b, dims):
    def one(p, q):
        return lax.dot_general(p, q, dims, preferred_element_type=F32)

    return one(a[0], b[0]) + (one(a[0], b[1]) + one(a[1], b[0]))


def times_inverse(block, parts):
    wide = 2 * TILE
    size = parts[0].shape[0]
    block = split(block)
    return jnp.concatenate(
        [
            dot3([p[:, : c + wide] for p in block], [q[c : c + wide, : c + wide] for q in parts], NT)
            for c in range(0, size, wide)
        ],
        axis=1,
    )


def mul(a, b, dims):
    return dot3(split(a), split(b), dims)


def factor_half(block, width):
    groups = HALF // ROWS
    sub = lax.broadcasted_iota(jnp.int32, (ROWS, TILE), 0)
    lane = lax.broadcasted_iota(jnp.int32, (ROWS, TILE), 1)

    def full(x):
        return jnp.broadcast_to(x, (ROWS, TILE))

    wide = jnp.concatenate([block, jnp.zeros((HALF, HALF), F32)], axis=1)
    a = [
        jnp.where(lane == sub + ROWS * g + HALF, 1.0, wide[ROWS * g : ROWS * g + ROWS])
        for g in range(groups)
    ]
    rows = [None] * HALF
    for j in range(0, HALF, width):
        gj, o = j // ROWS, j % ROWS
        cols = {g: [full(a[g][:, j + i : j + i + 1]) for i in range(width)] for g in range(gj, groups)}
        s = [
            [full(cols[gj][k][o + i : o + i + 1, :]) if k <= i else None for k in range(width)]
            for i in range(width)
        ]
        u = [full(a[gj][o + i : o + i + 1, :]) for i in range(width)]
        inv = [None] * width
        low = [[None] * width for _ in range(width)]
        for k in range(width):
            inv[k] = lax.rsqrt(s[k][k])
            for i in range(k + 1, width):
                low[i][k] = s[i][k] * inv[k]
            for i in range(k + 1, width):
                for q in range(k + 1, i + 1):
                    s[i][q] = s[i][q] - low[i][k] * low[q][k]
        for i in range(width):
            for k in range(i):
                u[i] = u[i] - low[i][k] * u[k]
            u[i] = u[i] * inv[i]
            rows[j + i] = u[i]
        for g in range(gj if o + width < ROWS else gj + 1, groups):
            c = cols[g]
            for i in range(width):
                for k in range(i):
                    c[i] = c[i] - c[k] * low[i][k]
                c[i] = c[i] * inv[i]
            for i in range(width):
                a[g] = a[g] - c[i] * u[i]
    out = []
    for g in range(groups):
        v = rows[ROWS * g]
        for i in range(1, ROWS):
            v = jnp.where(sub == i, rows[ROWS * g + i], v)
        out.append(v)
    both = jnp.concatenate(out, axis=0)
    return both[:, :HALF], both[:, HALF:]


def factor(a, low, inv, tiles, width, start=0, stop=None):
    stop = tiles if stop is None else stop
    d = a[start * TILE : (start + 1) * TILE, start * TILE : (start + 1) * TILE]
    zero = jnp.zeros((HALF, HALF), F32)
    ri = lax.broadcasted_iota(jnp.int32, (HALF, HALF), 0)
    ci = lax.broadcasted_iota(jnp.int32, (HALF, HALF), 1)
    for k in range(start, stop):
        k0, k1, k2 = k * TILE, (k + 1) * TILE, (k + 2) * TILE
        u1, w1 = factor_half(d[:HALF, :HALF], width)
        l21 = mul(d[HALF:, :HALF], w1, NT)
        u2, w2 = factor_half(d[HALF:, HALF:] - mul(l21, l21, NT), width)
        w21 = -mul(w2, mul(l21, w1, NN), NN)
        w = jnp.concatenate([jnp.concatenate([w1, zero], 1), jnp.concatenate([w21, w2], 1)], 0)
        ws = split(w)
        inv[k0:k1, k0:k1] = w
        if k + 1 < tiles:
            p = dot3(split(a[k1:k2, k0:k1]), ws, NT)
            low[k1:k2, k0:k1] = p
            ps = split(p)
            d = a[k1:k2, k1:k2] - dot3(ps, ps, NT)
        l1 = jnp.where(ri >= ci, u1.T, 0.0)
        l2 = jnp.where(ri >= ci, u2.T, 0.0)
        low[k0:k1, k0:k1] = jnp.concatenate(
            [jnp.concatenate([l1, zero], 1), jnp.concatenate([l21, l2], 1)], 0
        )
        if k + 2 < tiles:
            low[k2:, k0:k1] = dot3(split(a[k2:, k0:k1]), ws, NT)
            for j in range(k + 1, tiles):
                j0 = j * TILE
                top = max(j0, k2)
                a[top:, j0 : j0 + TILE] = a[top:, j0 : j0 + TILE] - mul(
                    low[top:, k0:k1], low[j0 : j0 + TILE, k0:k1], NT
                )
        if k > 0:
            x = mul(low[k0:k1, 0:k0], inv[0:k0, 0:k0], NN)
            inv[k0:k1, 0:k0] = -dot3(ws, split(x), NN)
        if k + 1 < tiles:
            rest = jnp.zeros((TILE, (tiles - k - 1) * TILE), F32)
            low[k0:k1, k1:] = rest
            inv[k0:k1, k1:] = rest
    if stop < tiles:
        a[k1:k2, k1:k2] = d


def padded(a, tile_of, live, tiles):
    ri = lax.broadcasted_iota(jnp.int32, (TILE, TILE), 0)
    ci = lax.broadcasted_iota(jnp.int32, (TILE, TILE), 1)
    eye = jnp.where(ri == ci, 1.0, 0.0)
    for i in range(tiles):
        kept = (jnp.int32(i) < live).astype(F32)
        for j in range(i + 1):
            value = tile_of(i, j) * kept
            if i == j:
                value = value + eye * (1.0 - kept)
            a[i * TILE : (i + 1) * TILE, j * TILE : (j + 1) * TILE] = value


def copy_all(pairs, sems):
    copies = [pltpu.make_async_copy(src, dst, sems.at[n]) for n, (src, dst) in enumerate(pairs)]
    for c in copies:
        c.start()
    for c in copies:
        c.wait()


def tile_at(ref, row, col):
    return ref.at[
        pl.ds(pl.multiple_of(row * TILE, TILE), TILE), pl.ds(pl.multiple_of(col * TILE, TILE), TILE)
    ]


def square_index():
    return (
        lax.broadcasted_iota(jnp.int32, (TILE, TILE), 0),
        lax.broadcasted_iota(jnp.int32, (TILE, TILE), 1),
    )


def put_pairs(tiles_in, out, first):
    r, c = square_index()
    diagonals = []
    for n in range(0, len(tiles_in), 2):
        mixed = tiles_in[n]
        if n + 1 < len(tiles_in):
            mixed = jnp.where(r >= c, mixed, tiles_in[n + 1])
            diagonals.append(jnp.sum(jnp.where(r == c, tiles_in[n + 1], 0.0), axis=0, keepdims=True))
        out[pl.ds((first + n // 2) * TILE, TILE), :] = mixed
    diagonals += [jnp.zeros((1, TILE), F32)] * (ROWS - len(diagonals))
    out[pl.ds((first + (len(tiles_in) + 1) // 2) * TILE, ROWS), :] = jnp.concatenate(diagonals, axis=0)


def get_pairs(ref, first, count):
    r, c = square_index()
    base = (first + (count + 1) // 2) * TILE
    out = []
    for n in range(0, count, 2):
        mixed = ref[(first + n // 2) * TILE : (first + n // 2 + 1) * TILE, :]
        if n + 1 == count:
            out.append(mixed)
            continue
        other = mixed.T
        out.append(jnp.where(r >= c, mixed, other))
        diagonal = ref[base + n // 2 : base + n // 2 + 1, :]
        out.append(jnp.where(r == c, diagonal, jnp.where(r < c, mixed, other)))
    return out


def message_tile(ref, n):
    return ref[pl.ds(pl.multiple_of(n * TILE, TILE), TILE), :]


def pack_first(tab, block, pivot, out, square, sems):
    side = tab[CT]
    pairs = []
    for n, (a, b) in enumerate(BELOW_C):
        pairs.append((tile_at(block, tab[a], tab[b]), out.at[pl.ds(n * TILE, TILE)]))
    first = len(BELOW_C)
    for n, (a, b) in enumerate(BELOW_P):
        pairs.append(
            (tile_at(pivot, a, side * (P1T // 2) + b), out.at[pl.ds((first + n) * TILE, TILE)])
        )
    for a in range(CT):
        pairs.append((tile_at(block, tab[a], tab[a]), square.at[a]))
    for a in range(P1T // 2):
        pairs.append((tile_at(pivot, a, side * (P1T // 2) + a), square.at[CT + a]))
    copy_all(pairs, sems)
    put_pairs([square[n] for n in range(DIAG_FIRST)], out, first + len(BELOW_P))


def pack_rest(
    tab, block, pivot, rows, pivot_second, second,
    coup, own, kept, cross, off, coup_two, units, units_sent, main, two_sent_a, two_sent_b, over,
    strips, sems,
):
    side = tab[CT]
    order = CT + 1
    local = order + CT
    quarter = tab[local + U1T]
    pairs = []
    for r in range(HALF_U):
        row = tab[local + r] - side * HALF_U
        for c in range(P1T):
            pairs.append((tile_at(rows, row, c), coup.at[r * P1T + c]))
    for n, (a, b) in enumerate(TRI_U):
        row = tab[local + a] - side * HALF_U
        pairs.append((tile_at(rows, row, P1T + tab[local + b]), own.at[n]))
    for n, (a, b) in enumerate(TRI_C):
        pairs.append((tile_at(block, tab[order + a], tab[order + b]), kept.at[n]))
    for i in range(HALF_U):
        row = tab[local + i] - side * HALF_U
        for k in range(HALF_U):
            pairs.append(
                (tile_at(rows, row, P1T + tab[local + HALF_U + k]), cross.at[i * HALF_U + k])
            )
    for i in range(P1T // 2):
        for k in range(P1T // 2):
            pairs.append(
                (tile_at(pivot, i, (1 - side) * (P1T // 2) + k), off.at[i * (P1T // 2) + k])
            )
    for n, (i, k) in enumerate(TRI_P):
        pairs.append((tile_at(pivot, i, side * (P1T // 2) + k), off.at[N_OFF + n]))
    for r in range(QUARTER):
        for c in range(P2T):
            pairs.append((tile_at(second, r, c), coup_two.at[r * P2T + c]))
    first = local + U1T + 1
    for p in range(N_COUP):
        n = tab[first + p]
        row = tab[local + n // P1T] - side * HALF_U
        sent = main.at[p] if p < N_MAIN else over.at[p - N_MAIN]
        pairs.append((tile_at(rows, row, n % P1T), sent))
    first += N_COUP
    for p in range(N_TWO):
        n = tab[first + p]
        if p < N_TWO_A:
            sent = two_sent_a.at[p]
        elif p < N_TWO_A + N_TWO_B:
            sent = two_sent_b.at[p - N_TWO_A]
        else:
            sent = over.at[p + N_COUP - N_MAIN - N_TWO_A - N_TWO_B]
        pairs.append((tile_at(second, n // P2T, n % P2T), sent))
    far = []
    for i in range(OWN_UNITS):
        for d in range(REACH):
            col = (quarter * OWN_UNITS + i - d + UNITS) % UNITS
            far.append(col % 2)
            source = pivot_second.at[
                pl.ds(i * HALF, HALF), pl.ds(pl.multiple_of(col // 2 * TILE, TILE), TILE)
            ]
            pairs.append((source, strips.at[i * REACH + d]))
    copy_all(pairs, sems)
    lane = lax.broadcasted_iota(jnp.int32, (HALF, TILE), 1)

    def placed(n, half):
        strip = strips[n]
        return jnp.where(far[n] == half, strip, pltpu.roll(strip, HALF, 1))

    for n in range(N_WIDE):
        strip = placed(2 * n, 0)
        if 2 * n + 1 < N_UNIT:
            strip = jnp.where(lane < HALF, strip, placed(2 * n + 1, 1))
        units[n * HALF : (n + 1) * HALF, :] = strip
        units_sent[n * HALF : (n + 1) * HALF, :] = strip


def after(array, *others):
    def kernel(*refs):
        pass

    return pl.pallas_call(
        kernel,
        out_shape=jax.ShapeDtypeStruct(array.shape, array.dtype),
        in_specs=[HBM] * (1 + len(others)),
        out_specs=HBM,
        input_output_aliases={0: 0},
        name="after",
        cost_estimate=CHEAP,
    )(array, *others)


def part_of(array):
    return array[(0,) * (array.ndim - 2)][:ROWS]


T_SIDE = 0
T_LIVE = 1
T_LOCAL = 2
T_FILL = T_LOCAL + U1T
T_SLOT = T_FILL + U1T * P1T
T_SLOT_FAR = T_SLOT + CT * CT
T_PLACE = T_SLOT_FAR + CT * CT


def panel_rows(tile_of, count, live, parts, put):
    for r in range(0, count, 2):
        block = jnp.concatenate(
            [
                jnp.concatenate([tile_of(r + i, c) for c in range(P1T)], axis=1)
                for i in range(2)
            ],
            axis=0,
        )
        lane = lax.broadcasted_iota(jnp.int32, block.shape, 1)
        block = jnp.where(lane < live * TILE, block, 0.0)
        put(r, times_inverse(block, parts))


def first_kernel(
    tab, mine, theirs, coup, own, cross, off,
    lower_out, inv_high, inv_low, panel_high, panel_low, rows_out, own_out, own_sent, far_out,
    front, a, low, inv, sem,
):
    side = tab[T_SIDE]
    live = tab[T_LIVE]
    half = P1T // 2
    square = get_pairs(theirs, len(BELOW_C) + len(BELOW_P), DIAG_FIRST)
    front[0:N_PIV] = jnp.zeros((N_PIV, TILE, TILE), F32)
    for n, (i, k) in enumerate(TRI_P):
        front[(side * half + i) * P1T + side * half + k] = off[N_OFF + n]
        if i == k:
            tile = square[CT + i]
        else:
            tile = message_tile(theirs, len(BELOW_C) + BELOW_P.index((i, k)))
        front[((1 - side) * half + i) * P1T + (1 - side) * half + k] = tile
    for i in range(half):
        for k in range(half):

            @pl.when(side == 0)
            def _():
                front[(half + k) * P1T + i] = off[i * half + k].T

            @pl.when(side != 0)
            def _():
                front[(half + i) * P1T + k] = off[i * half + k]

    def scale(n, carry):
        front[S_COUP + n] = coup[n] * tab[T_FILL + n].astype(F32)
        front[S_FAR + n] = jnp.zeros((TILE, TILE), F32)
        front[S_CROSS + n] = cross[n]
        return carry

    lax.fori_loop(0, N_COUP, scale, 0)

    def copy(n, carry):
        front[S_OWN + n] = own[n]
        front[S_OTH + n] = jnp.zeros((TILE, TILE), F32)
        return carry

    lax.fori_loop(0, N_TRI, copy, 0)
    for i in range(CT):

        def extend(k, carry, i=i):
            here = tab[T_SLOT + i * CT + k]
            front[here] = front[here] + mine[tri(i, 0) + k]
            return carry

        lax.fori_loop(0, i + 1, extend, 0)

        def extend_far(k, carry, i=i):
            there = tab[T_SLOT_FAR + i * CT + k]
            front[there] = front[there] + message_tile(theirs, i * (i - 1) // 2 + k)
            return carry

        lax.fori_loop(0, i, extend_far, 0)
        there = tab[T_SLOT_FAR + i * CT + i]
        front[there] = front[there] + square[i]
    leave = pltpu.make_async_copy(front.at[pl.ds(S_FAR, S_OTH - S_FAR)], far_out, sem)
    leave.start()
    padded(a, lambda i, j: front[i * P1T + j], live, P1T)
    factor(a, low, inv, P1T, 4)
    inv_high[...], inv_low[...] = split(inv[...])
    lower_out[...] = low[pl.ds(pl.multiple_of(side * (PIVOT // 2), TILE), PIVOT // 2), :]

    def put(r, rows):
        wide = slice(r * TILE, (r + 2) * TILE)
        panel_high[wide, :], panel_low[wide, :] = split(rows)
        for i in range(2):
            place = tab[T_LOCAL + r + i] - side * HALF_U
            rows_out[pl.ds(pl.multiple_of(place * TILE, TILE), TILE), :] = rows[
                i * TILE : (i + 1) * TILE
            ]

    panel_rows(lambda r, c: front[S_COUP + r * P1T + c], HALF_U, live, (inv_high[...], inv_low[...]), put)
    for i in range(HALF_U):
        left = [p[i * TILE : (i + 1) * TILE, :] for p in (panel_high, panel_low)]
        right = [p[0 : (i + 1) * TILE, :] for p in (panel_high, panel_low)]
        product = dot3(left, right, NT)
        for k in range(i + 1):
            n = S_OWN + tri(i, k)
            front[n] = front[n] - product[:, k * TILE : (k + 1) * TILE]
    put_own([front[S_OWN + n] for n in range(N_TRI)], own_out)
    put_own([front[S_OWN + n] for n in range(N_TRI)], own_sent)
    leave.wait()


def choose(at, parts):
    value = None
    base = sum(count for _, _, count in parts)
    for ref, first, count in reversed(parts):
        base -= count
        tile = ref[first + jnp.clip(at - base, 0, count - 1)]
        value = tile if value is None else jnp.where(at < base + count, tile, value)
    return value


def second_kernel(
    which, tab, far, main, over, inv_high, inv_low, panel_high, panel_low, cross,
    rows_far, cross_far, sems,
):
    wide = HALF_U // 2
    copies = [(far.at[pl.ds(which * wide * P1T, wide * P1T)], rows_far)]
    for i in range(HALF_U):
        copies.append(
            (
                far.at[pl.ds(N_COUP + i * HALF_U + which * wide, wide)],
                cross_far.at[pl.ds(i * wide, wide)],
            )
        )
    copies = [pltpu.make_async_copy(src, dst, sems.at[n]) for n, (src, dst) in enumerate(copies)]
    for c in copies:
        c.start()
    live = tab[T_LIVE]
    parts = inv_high[...], inv_low[...]

    def tile_of(r, c):
        n = (which * wide + r) * P1T + c
        tile = choose(tab[T_PLACE + n], [(main, 0, N_MAIN), (over, 0, N_COUP - N_MAIN)])
        return rows_far[r * P1T + c] + tile * tab[T_FILL + N_COUP + n].astype(F32)

    for c in copies:
        c.wait()
    block = jnp.concatenate(
        [jnp.concatenate([tile_of(r, c) for c in range(P1T)], axis=1) for r in range(wide)], axis=0
    )
    lane = lax.broadcasted_iota(jnp.int32, block.shape, 1)
    block = jnp.where(lane < live * TILE, block, 0.0)
    right = split(times_inverse(block, parts))
    for i in range(0, HALF_U, 2):
        left = [p[i * TILE : (i + 2) * TILE, :] for p in (panel_high, panel_low)]
        product = dot3(left, right, NT)
        for q in range(2):
            for k in range(wide):
                n = (i + q) * wide + k
                cross[n] = (
                    cross_far[n] - product[q * TILE : (q + 1) * TILE, k * TILE : (k + 1) * TILE]
                )


def put_own(block, out):
    for n, (a, b) in enumerate(BELOW_U):
        out[n * TILE : (n + 1) * TILE, :] = block[tri(a, b)]
    put_pairs([block[tri(a, a)] for a in range(HALF_U)], out, len(BELOW_U))


def get_own(ref, out):
    for n, (i, k) in enumerate(BELOW_U):
        out[tri(i, k)] = message_tile(ref, n)
    for i, tile in enumerate(get_pairs(ref, len(BELOW_U), HALF_U)):
        out[tri(i, i)] = tile


Q_LIVE = 0
Q_MINE = 1
Q_FILL = 5
Q_DIRECT = Q_FILL + U2T * P2T
Q_TURNED = Q_DIRECT + 2 * U1T * U1T
Q_PLACE = Q_TURNED + 2 * U1T * U1T


def extend_cross(tab, ref, g, front, which):
    wide = HALF_U // 2
    extend_two(tab, ref, g, front, 0, HALF_U + which * wide, False, 0, G_NONE, wide)


def extend_two(tab, ref, g, front, rows, cols, triangle, low, high, wide=HALF_U):
    for i in range(HALF_U):

        def one(k, carry, i=i):
            at = front * U1T * U1T + (rows + i) * U1T + cols + k
            n = (tri(i, 0) if triangle else i * wide) + k
            direct = tab[Q_DIRECT + at]
            turned = tab[Q_TURNED + at]

            @pl.when((direct >= low) & (direct < high))
            def _():
                g[direct - low] = g[direct - low] + ref[n]

            @pl.when((turned >= low) & (turned < high))
            def _():
                g[turned - low] = g[turned - low] + ref[n].T

            return carry

        lax.fori_loop(0, i + 1 if triangle else wide, one, 0)


def add_units(tab, g, units, s):
    lane = lax.broadcasted_iota(jnp.int32, (HALF, TILE), 1)
    for i in range(OWN_UNITS):
        row = tab[Q_MINE + s] * OWN_UNITS + i
        for d in range(REACH):
            n = i * REACH + d
            col = (row - d + UNITS) % UNITS
            strip = units[n // 2 * HALF : (n // 2 + 1) * HALF, :]
            here = n % 2

            def add(r, c, block):
                slot = r // 2 * P2T + c // 2
                start = pl.multiple_of(r % 2 * HALF, HALF)
                old = g[slot, pl.ds(start, HALF), :]
                g[slot, pl.ds(start, HALF), :] = old + jnp.where(lane // HALF == c % 2, block, 0.0)

            @pl.when((col <= row) & ((d < REACH - 1) | (row >= UNITS // 2)))
            def _():
                add(row, col, jnp.where(col % 2 == here, strip, pltpu.roll(strip, HALF, 1)))

            if d < REACH - 1 and d > 0:

                @pl.when(col > row)
                def _():
                    turned = strip.T[here * HALF : (here + 1) * HALF, :]
                    add(col, row, jnp.concatenate([turned, turned], axis=1))


def third_kernel(tab, own0, units0, units2, second, g, block):
    def clear(n, carry):
        g[n] = jnp.zeros((TILE, TILE), F32)
        return carry

    lax.fori_loop(0, G_TRAIL, clear, 0)
    for r in range(QUARTER):
        for c in range(U2T):
            g[G_TRAIL + r * U2T + c] = second[
                r * TILE : (r + 1) * TILE, SECOND + c * TILE : SECOND + (c + 1) * TILE
            ]
    add_units(tab, g, units0, 0)
    add_units(tab, g, units2, 2)
    get_own(own0, block)
    extend_two(tab, block, g, 0, 0, 0, True, 0, G_NONE)


def more_kernel(
    tab, part, own1, cross0_a, cross0_b, cross1_a, cross1_b, oth0, units1, g, block, sem
):
    enter = pltpu.make_async_copy(part, g, sem)
    enter.start()
    get_own(oth0, block)
    enter.wait()
    add_units(tab, g, units1, 1)
    extend_cross(tab, cross0_a, g, 0, 0)
    extend_cross(tab, cross0_b, g, 0, 1)
    extend_cross(tab, cross1_a, g, 1, 0)
    extend_cross(tab, cross1_b, g, 1, 1)
    extend_two(tab, block, g, 0, HALF_U, HALF_U, True, 0, G_NONE)
    get_own(own1, block)
    extend_two(tab, block, g, 1, 0, 0, True, 0, G_NONE)


def pivot_kernel(tab, part, oth1, units3, lower_out, high_out, rest_out, g, other, a, low, inv, sem):
    enter = pltpu.make_async_copy(part.at[pl.ds(0, G_COUP)], g, sem)
    enter.start()
    get_own(oth1, other)
    enter.wait()
    add_units(tab, g, units3, 3)
    extend_two(tab, other, g, 1, HALF_U, HALF_U, True, 0, G_COUP)
    padded(a, lambda i, j: g[i * P2T + j], tab[Q_LIVE], P2T)
    factor(a, low, inv, P2T, 8)
    start = tab[Q_MINE] * (SECOND // 4)
    lower_out[...] = low[pl.ds(pl.multiple_of(start, HALF), SECOND // 4), :]
    high_out[...], rest_out[...] = split(inv[...])


def quarter_rows_of(tab, g, quarter):
    return jnp.concatenate(
        [
            jnp.concatenate([g[(quarter * QUARTER + r) * P2T + c] for c in range(P2T)], axis=1)
            for r in range(QUARTER)
        ],
        axis=0,
    )


def placed_two(tab, which, first, second, over):
    parts = [
        (first, 0, N_TWO_A),
        (second, 0, N_TWO_B),
        (over, N_COUP - N_MAIN, N_TWO - N_TWO_A - N_TWO_B),
    ]
    return lambda n: choose(tab[Q_PLACE + which * N_TWO + n], parts)


def quarter_panel(tab, block, coup, parts, quarter):
    rows = []
    for r in range(QUARTER):
        fill = Q_FILL + (quarter * QUARTER + r) * P2T
        rows.append(
            jnp.concatenate(
                [coup(r * P2T + c) * tab[fill + c].astype(F32) for c in range(P2T)], axis=1
            )
        )
    block = block + jnp.concatenate(rows, axis=0)
    lane = lax.broadcasted_iota(jnp.int32, block.shape, 1)
    block = jnp.where(lane < tab[Q_LIVE] * TILE, block, 0.0)
    return times_inverse(block, parts)


WIDE = QUARTER * TILE


def fetch(pairs, sems):
    copies = [pltpu.make_async_copy(src, dst, sems.at[n]) for n, (src, dst) in enumerate(pairs)]
    for c in copies:
        c.start()
    return copies


def rows_kernel(
    tab, part, oth1, high_in, low_in, coup0_in, coup1_a_in, coup1_b_in, over_in, coup2_in,
    panel_out, schur_out, rest_out,
    g, oth, high, low, coup0, coup1_a, coup1_b, over, coup2, other, panels, sems,
):
    copies = fetch(
        [
            (oth1, oth),
            (part.at[pl.ds(G_COUP, G_NONE - G_COUP)], g),
            (coup0_in, coup0),
            (high_in, high),
            (low_in, low),
            (coup1_a_in, coup1_a),
            (coup1_b_in, coup1_b),
            (over_in, over),
            (coup2_in, coup2),
        ],
        sems,
    )
    copies[0].wait()
    get_own(oth, other)
    copies[1].wait()
    extend_two(tab, other, g, 1, HALF_U, HALF_U, True, G_COUP, G_NONE)
    rest_out[...] = quarter_rows_of(tab, g, tab[Q_MINE + 3])
    for c in copies[2:]:
        c.wait()
    parts = high[...], low[...]
    whole = [lambda n, ref=ref: ref[n] for ref in (coup0, coup2)]
    for s, coup in enumerate((whole[0], placed_two(tab, 0, coup1_a, coup1_b, over), whole[1])):
        quarter = tab[Q_MINE + s]
        panel = quarter_panel(tab, quarter_rows_of(tab, g, quarter), coup, parts, quarter)
        panels[s] = panel
        if s == 0:
            panel_out[...] = panel
    left = split(panel_out[...])
    for s in range(4):
        quarter = tab[Q_MINE + s]
        if s < 3:
            product = dot3(left, split(panels[s]), NT)
        for r in range(QUARTER):
            for c in range(QUARTER):
                tile = g[G_TRAIL - G_COUP + r * U2T + quarter * QUARTER + c]
                if s < 3:
                    tile = tile - product[r * TILE : (r + 1) * TILE, c * TILE : (c + 1) * TILE]
                col = pl.multiple_of((quarter * QUARTER + c) * TILE, TILE)
                schur_out[r * TILE : (r + 1) * TILE, pl.ds(col, TILE)] = tile


def last_kernel(
    tab, schur, rest_in, panel_in, high_in, low_in, coup_a_in, coup_b_in, over_in,
    out,
    block, rest, panel, high, low, coup_a, coup_b, over, sems, sem,
):
    quarter = tab[Q_MINE + 3]
    col = pl.ds(pl.multiple_of(quarter * WIDE, TILE), WIDE)
    copies = fetch(
        [
            (rest_in, rest),
            (coup_a_in, coup_a),
            (coup_b_in, coup_b),
            (over_in, over),
            (high_in, high),
            (low_in, low),
            (panel_in, panel),
            (schur.at[:, col], block),
        ],
        sems,
    )
    for c in copies[:6]:
        c.wait()
    coup = placed_two(tab, 1, coup_a, coup_b, over)
    other = quarter_panel(tab, rest[...], coup, (high[...], low[...]), quarter)
    for c in copies[6:]:
        c.wait()
    block[...] = block[...] - dot3(split(panel[...]), split(other), NT)
    leave = pltpu.make_async_copy(block, out.at[:, col], sem)
    leave.start()
    leave.wait()


def swap(array, axis):
    size = lax.axis_size(axis)
    return lax.ppermute(array, axis, [(i, i ^ (size // 2)) for i in range(size)])


def tiles(count):
    return jax.ShapeDtypeStruct((count, TILE, TILE), F32)


def halved(rows):
    return jax.ShapeDtypeStruct((rows, PIVOT), jnp.bfloat16)


def dense(rows, cols):
    return jax.ShapeDtypeStruct((rows, cols), F32)


SMEM = pl.BlockSpec(memory_space=pltpu.SMEM)
VMEM = pl.BlockSpec(memory_space=pltpu.VMEM)
HBM = pl.BlockSpec(memory_space=pl.ANY)
LIMIT = 60 << 20
CHEAP = pl.CostEstimate(flops=1, bytes_accessed=1, transcendentals=0)


def call(kernel, name, out_shape, in_specs, out_specs, scratch=(), waits=(), limit=LIMIT, **options):
    count = len(in_specs)

    def body(*refs):
        kernel(*refs[:count], *refs[count + len(waits) :])

    run = pl.pallas_call(
        body,
        out_shape=out_shape,
        in_specs=in_specs + [HBM] * len(waits),
        out_specs=out_specs,
        scratch_shapes=list(scratch),
        name=name,
        compiler_params=pltpu.CompilerParams(vmem_limit_bytes=limit),
        cost_estimate=CHEAP,
        **options,
    )
    return lambda *args: run(*args, *waits)


def tri(i, k):
    return i * (i + 1) // 2 + k


def local_order(second_map, side):
    unit = jnp.arange(U1T, dtype=jnp.int32)
    rank = second_map + jnp.where(unit // HALF_U == side, 0, P2T + U2T)
    place = jnp.sum((rank[None, :] < rank[:, None]).astype(jnp.int32), axis=1)
    hit = (place[None, :] == unit[:, None]).astype(jnp.int32)
    return place, hit


def place_of(child_map, place):
    unit = jnp.arange(U1T, dtype=jnp.int32)
    hit = (child_map[:, None] - P1T == unit[None, :]).astype(jnp.int32)
    return jnp.where(child_map < P1T, child_map, P1T + jnp.sum(hit * place[None, :], axis=1))


def sort_by(key):
    spot = jnp.sum((key[None, :] < key[:, None]).astype(jnp.int32), axis=1)
    hit = (spot[None, :] == jnp.arange(CT, dtype=jnp.int32)[:, None]).astype(jnp.int32)
    order = jnp.sum(hit * jnp.arange(CT, dtype=jnp.int32)[None, :], axis=1)
    return order, jnp.sum(hit * key[None, :], axis=1)


def turned_key(key):
    return jnp.where(key < P1T, key, P1T + (key - P1T + HALF_U) % U1T)


def slots(keys):
    row = keys[:, None]
    col = keys[None, :]
    own = P1T + HALF_U
    pivot = row * P1T + col
    coup = jnp.where(row >= own, S_COUP + (row - own) * P1T, S_FAR + (row - P1T) * P1T) + col
    near = S_OWN + tri(row - own, col - own)
    cross = S_CROSS + (row - own) * HALF_U + col - P1T
    other = S_OTH + tri(row - P1T, col - P1T)
    rest = jnp.where(row < own, other, jnp.where(col < own, cross, near))
    return jnp.where(row < P1T, pivot, jnp.where(col < P1T, coup, rest)).reshape(-1)


def needed_first(need):
    need = need.reshape(-1)
    count = need.shape[0]
    at = jnp.arange(count, dtype=jnp.int32)
    key = at + jnp.where(need > 0, 0, count)
    place = jnp.sum((key[None, :] < key[:, None]).astype(jnp.int32), axis=1)
    order = jnp.sum((place[None, :] == at[:, None]).astype(jnp.int32) * at[None, :], axis=1)
    return place, order


def needed(fill, live):
    return fill * (jnp.arange(fill.shape[-1], dtype=jnp.int32) < live[..., None, None])


def targets(goal, quarter):
    row = goal[:, None]
    col = goal[None, :]

    def index(r, c):
        mine = (r - P2T) // QUARTER == quarter
        coup = G_COUP + (r - P2T) * P2T + c
        trail = G_TRAIL + (r - P2T - quarter * QUARTER) * U2T + c - P2T
        rest = jnp.where(c < P2T, coup, jnp.where(mine, trail, G_NONE))
        return jnp.where(r < P2T, jnp.where((c < P2T) & (r >= c), r * P2T + c, G_NONE), rest)

    direct = index(row, col)
    turned = jnp.where(row == col, G_NONE, index(col, row))
    return direct.reshape(-1), turned.reshape(-1)


def body(
    contribution,
    pivot_one,
    rows_one,
    pivot_two,
    rows_two,
    map_one,
    map_two,
    fill_one,
    fill_two,
    live_one,
    live_two,
):
    size_lo = lax.axis_size("lo")
    size_hi = lax.axis_size("hi")
    half_lo = size_lo // 2
    half_hi = size_hi // 2
    index_lo = lax.axis_index("lo")
    index_hi = lax.axis_index("hi")
    side_lo = index_lo // half_lo
    side_hi = index_hi // half_hi
    front_lo = index_lo % half_lo
    front_hi = index_hi % half_hi
    far_lo = (index_lo + half_lo) % size_lo
    far_hi = (index_hi + half_hi) % size_hi
    quarter = 2 * side_hi + side_lo
    block, pivot, rows = contribution[0, 0], pivot_one[0, 0], rows_one[0, 0]
    pivot_second, rows_second = pivot_two[0, 0], rows_two[0, 0]

    second_map = map_two[index_hi, front_lo]
    place, hit = local_order(second_map, side_lo)
    key = place_of(map_one[index_hi, index_lo], place)
    order_sent, _ = sort_by(key)
    tab_first = jnp.concatenate([order_sent, side_lo[None]]).astype(jnp.int32)
    sent = call(
        pack_first,
        "pack_first",
        dense(N_FIRST * TILE + ROWS, TILE),
        [SMEM, HBM, HBM],
        VMEM,
        [
            pltpu.VMEM((DIAG_FIRST, TILE, TILE), F32),
            pltpu.SemaphoreType.DMA((len(TRI_C) + len(TRI_P),)),
        ],
    )(tab_first, block, pivot)
    got_first = swap(sent, "lo")

    unit = jnp.arange(U1T, dtype=jnp.int32)
    local = jnp.sum(hit * unit[None, :], axis=1)
    order_kept, keys = sort_by(turned_key(key))
    live_first = live_one[index_hi, front_lo]
    need_first = needed(
        jnp.sum(hit[:, :, None] * fill_one[index_hi, front_lo][None, :, :], axis=1), live_first
    )
    live_second = live_two[front_hi, front_lo]
    need_second = needed(fill_two[front_hi, front_lo], live_second)

    def place_second(which):
        return needed_first(
            lax.dynamic_slice_in_dim(need_second, which * QUARTER, QUARTER, 0)
        )

    _, order_main = needed_first(need_first[:HALF_U])
    _, order_two = place_second(quarter)
    tab_rest = jnp.concatenate(
        [tab_first, order_kept, local, quarter[None], order_main, order_two]
    ).astype(jnp.int32)
    shapes = [
        tiles(N_COUP), tiles(N_TRI), tiles(len(TRI_C)), tiles(N_CROSS), tiles(N_OFF + len(TRI_P)),
        tiles(N_TWO),
        dense(N_WIDE * HALF, TILE), dense(N_WIDE * HALF, TILE),
        tiles(N_MAIN), tiles(N_TWO_A), tiles(N_TWO_B), tiles(N_OVER),
    ]
    n_rest = 2 * N_COUP + N_TRI + len(TRI_C) + N_CROSS + N_OFF + len(TRI_P) + 2 * N_TWO + N_UNIT
    coup, own, kept, cross, off, two, units, units_sent, main, two_a, two_b, over = call(
        pack_rest,
        "pack_rest",
        shapes,
        [SMEM] + [HBM] * 5,
        [VMEM] * len(shapes),
        [pltpu.VMEM((N_UNIT, HALF, TILE), F32), pltpu.SemaphoreType.DMA((n_rest,))],
        waits=(sent,),
    )(tab_rest, block, pivot, rows, pivot_second, rows_second)
    two_hi = swap(two, "hi")
    units_hi = swap(units, "hi")
    far_key = place_of(map_one[index_hi, far_lo], place)
    _, far_keys = sort_by(turned_key(far_key))
    place_main, _ = needed_first(need_first[HALF_U:])
    tab_one = jnp.concatenate(
        [side_lo[None], live_first[None], local, need_first.reshape(-1), slots(keys), slots(far_keys), place_main]
    ).astype(jnp.int32)
    map_far = map_two[far_hi, front_lo]
    _, hit_far = local_order(map_far, side_lo)
    direct, turned = targets(jnp.sum(hit * second_map[None, :], axis=1), quarter)
    direct_far, turned_far = targets(jnp.sum(hit_far * map_far[None, :], axis=1), quarter)
    place_lo, _ = place_second(2 * side_hi + 1 - side_lo)
    place_both, _ = place_second(2 * (1 - side_hi) + 1 - side_lo)
    quarters = jnp.stack(
        [quarter, 2 * side_hi + 1 - side_lo, 2 * (1 - side_hi) + side_lo, 2 * (1 - side_hi) + 1 - side_lo]
    )
    tab_two = jnp.concatenate(
        [
            live_second[None], quarters, need_second.reshape(-1),
            direct, direct_far, turned, turned_far, place_lo, place_both,
        ]
    ).astype(jnp.int32)
    most = jnp.max(jnp.sum(needed(fill_one, live_one).reshape(-1, N_COUP), axis=1))
    most_two = jnp.max(jnp.sum(needed(fill_two, live_two).reshape(-1, N_TWO), axis=1))

    def send_over(array):
        got = swap(array, "lo")
        return got, swap(got, "hi")

    over_got, over_both = lax.cond(
        (most > N_MAIN) | (most_two > N_TWO_A + N_TWO_B),
        send_over,
        lambda array: (array, array),
        over,
    )
    main = after(main, part_of(got_first), two_hi, units_hi, tab_one, tab_two, over_got, over_both)
    got_main = swap(main, "lo")

    half_rows = HALF_U * TILE
    message = dense(N_OWN * TILE + ROWS, TILE)
    lower_one, inv_a, inv_b, panel_a, panel_b, panel_one, s_own, own_sent, far_part = call(
        first_kernel,
        "first_front_own",
        [
            dense(PIVOT // 2, PIVOT), *[halved(PIVOT)] * 2, *[halved(half_rows)] * 2,
            dense(half_rows, PIVOT), message, message, tiles(N_CROSS + N_COUP),
        ],
        [SMEM] + [VMEM] * 6,
        [VMEM] * 8 + [HBM],
        [
            pltpu.VMEM((N_FRONT, TILE, TILE), F32),
            pltpu.VMEM((PIVOT, PIVOT), F32),
            pltpu.VMEM((PIVOT, PIVOT), F32),
            pltpu.VMEM((PIVOT, PIVOT), F32),
            pltpu.SemaphoreType.DMA,
        ],
    )(tab_one, kept, got_first, coup, own, cross, off)
    s_own_far = swap(s_own, "hi")
    block = pltpu.VMEM((N_TRI, TILE, TILE), F32)
    part = call(third_kernel, "second_front_part", tiles(G_NONE), [SMEM] + [VMEM] * 4, VMEM, [block])(
        tab_two, s_own, units, units_hi, rows_second
    )
    own_sent = after(own_sent, part_of(got_main), part)
    got_own = swap(own_sent, "lo")


    def cross_of(which, *waits):
        return call(
            functools.partial(second_kernel, which),
            "first_front_other",
            tiles(N_CROSS_A),
            [SMEM, HBM] + [VMEM] * 6,
            VMEM,
            [
                pltpu.VMEM((N_COUP // 2, TILE, TILE), F32),
                pltpu.VMEM((N_CROSS_A, TILE, TILE), F32),
                pltpu.SemaphoreType.DMA((1 + HALF_U,)),
            ],
            waits=waits,
        )(tab_one, far_part, got_main, over_got, inv_a, inv_b, panel_a, panel_b)

    cross_a = cross_of(0, s_own_far, own_sent)
    cross_a_far = swap(cross_a, "hi")
    cross_b = cross_of(1, cross_a)
    cross_b_far = swap(cross_b, "hi")
    got_units = swap(after(units_sent, got_own), "lo")
    s_oth_far = swap(got_own, "hi")
    units_both = swap(got_units, "hi")
    got_two_a = swap(after(two_a, got_units, cross_a_far, cross_b_far), "lo")
    part = call(
        more_kernel,
        "second_front_more",
        tiles(G_NONE),
        [SMEM, HBM] + [VMEM] * 7,
        VMEM,
        [block, pltpu.SemaphoreType.DMA],
    )(tab_two, part, s_own_far, cross_a, cross_b, cross_a_far, cross_b_far, got_own, got_units)
    two_b = after(two_b, got_two_a, units_both, s_oth_far, part)
    got_two_b = swap(two_b, "lo")
    two_a_both = swap(got_two_a, "hi")
    half = jax.ShapeDtypeStruct((SECOND, SECOND), jnp.bfloat16)
    square = pltpu.VMEM((SECOND, SECOND), F32)
    lower_two, inv_high, inv_low = call(
        pivot_kernel,
        "second_front_pivot",
        [dense(SECOND // 4, SECOND), half, half],
        [SMEM, HBM] + [VMEM] * 2,
        [VMEM] * 3,
        [
            pltpu.VMEM((G_COUP, TILE, TILE), F32),
            pltpu.VMEM((N_TRI, TILE, TILE), F32),
            square, square, square,
            pltpu.SemaphoreType.DMA,
        ],
        waits=(two_b,),
    )(tab_two, part, s_oth_far, units_both)
    got_two_b = after(got_two_b, lower_two, two_a_both)
    two_b_both = swap(got_two_b, "hi")
    rows_wide = pltpu.VMEM((WIDE, SECOND), F32)
    halves = [pltpu.VMEM((SECOND, SECOND), jnp.bfloat16)] * 2
    sent_two = [pltpu.VMEM((n, TILE, TILE), F32) for n in (N_TWO_A, N_TWO_B, N_OVER)]
    whole_two = pltpu.VMEM((N_TWO, TILE, TILE), F32)
    panel_two, schur, rest = call(
        rows_kernel,
        "second_front_rows",
        [dense(WIDE, SECOND), dense(WIDE, U2T * TILE), dense(WIDE, SECOND)],
        [SMEM] + [HBM] * 9,
        [VMEM] * 3,
        [
            pltpu.VMEM((G_NONE - G_COUP, TILE, TILE), F32),
            pltpu.VMEM((N_OWN * TILE + ROWS, TILE), F32),
            *halves,
            whole_two,
            *sent_two,
            whole_two,
            block,
            pltpu.VMEM((3, WIDE, SECOND), F32),
            pltpu.SemaphoreType.DMA((9,)),
        ],
    )(tab_two, part, s_oth_far, inv_high, inv_low, two, got_two_a, got_two_b, over_got, two_hi)
    schur_two = call(
        last_kernel,
        "second_front_last",
        dense(WIDE, U2T * TILE),
        [SMEM] + [HBM] * 8,
        HBM,
        [
            pltpu.VMEM((WIDE, WIDE), F32),
            rows_wide,
            rows_wide,
            *halves,
            *sent_two,
            pltpu.SemaphoreType.DMA((8,)),
            pltpu.SemaphoreType.DMA,
        ],
        input_output_aliases={1: 0},
    )(tab_two, schur, rest, panel_two, inv_high, inv_low, two_a_both, two_b_both, over_both)
    return (
        lower_one[None, None],
        panel_one[None, None],
        lower_two[None, None],
        panel_two[None, None],
        schur_two[None, None],
    )


def solution(mesh):
    split_both = P("hi", "lo", None, None)
    return jax.shard_map(
        body,
        mesh=mesh,
        in_specs=(split_both,) * 5 + (P(),) * 6,
        out_specs=(split_both,) * 5,
        check_vma=False,
    )
```

```python
import functools

import jax
import jax.numpy as jnp
import numpy as np
from jax import lax
from jax.experimental import pallas as pl
from jax.experimental.pallas import tpu as pltpu
from jax.sharding import PartitionSpec as P

TILE = 128
HALF = TILE // 2
CT = 8
P1T = 6
U1T = 12
P2T = 6
U2T = 12
ROWS = 8

HALF_U = U1T // 2
QUARTER = U2T // 4
PIVOT = P1T * TILE
SECOND = P2T * TILE

TRI_C = [(a, b) for a in range(CT) for b in range(a + 1)]
TRI_U = [(a, b) for a in range(HALF_U) for b in range(a + 1)]
TRI_P = [(a, b) for a in range(P1T // 2) for b in range(a + 1)]
BELOW_C = [(a, b) for a, b in TRI_C if a != b]
BELOW_U = [(a, b) for a, b in TRI_U if a != b]
BELOW_P = [(a, b) for a, b in TRI_P if a != b]
DIAG_FIRST = CT + P1T // 2
N_FIRST = len(BELOW_C) + len(BELOW_P) + (DIAG_FIRST + 1) // 2
N_OWN = len(BELOW_U) + (HALF_U + 1) // 2
UNITS = SECOND // HALF
OWN_UNITS = UNITS // 4
REACH = UNITS // 2 + 1
N_UNIT = OWN_UNITS * REACH
N_WIDE = (N_UNIT + 1) // 2
N_TWO = QUARTER * P2T
N_MAIN = 30
N_TWO_A = 5
N_TWO_B = 11
N_OFF = (P1T // 2) ** 2
N_PIV = P1T * P1T
N_COUP = HALF_U * P1T
N_TRI = len(TRI_U)
N_CROSS = HALF_U * HALF_U
N_CROSS_A = N_CROSS // 2
N_OVER = N_COUP - N_MAIN
N_TWO_OVER = N_TWO - N_TWO_A - N_TWO_B
S_COUP = N_PIV
S_OWN = S_COUP + N_COUP
S_FAR = S_OWN + N_TRI
S_CROSS = S_FAR + N_COUP
S_OTH = S_CROSS + N_CROSS
N_FRONT = S_OTH + N_TRI
G_COUP = P2T * P2T
G_TRAIL = G_COUP + U2T * P2T
G_NONE = G_TRAIL + QUARTER * U2T

NT = (((1,), (1,)), ((), ()))
NN = (((1,), (0,)), ((), ()))
F32 = jnp.float32


def split(x):
    high = x.astype(jnp.bfloat16)
    return high, (x - high.astype(F32)).astype(jnp.bfloat16)


def dot3(a, b, dims):
    def one(p, q):
        return lax.dot_general(p, q, dims, preferred_element_type=F32)

    return one(a[0], b[0]) + (one(a[0], b[1]) + one(a[1], b[0]))


def times_inverse(block, parts):
    wide = 2 * TILE
    size = parts[0].shape[0]
    block = split(block)
    return jnp.concatenate(
        [
            dot3([p[:, : c + wide] for p in block], [q[c : c + wide, : c + wide] for q in parts], NT)
            for c in range(0, size, wide)
        ],
        axis=1,
    )


def mul(a, b, dims):
    return dot3(split(a), split(b), dims)


def factor_half(block, width):
    groups = HALF // ROWS
    sub = lax.broadcasted_iota(jnp.int32, (ROWS, TILE), 0)
    lane = lax.broadcasted_iota(jnp.int32, (ROWS, TILE), 1)

    def full(x):
        return jnp.broadcast_to(x, (ROWS, TILE))

    wide = jnp.concatenate([block, jnp.zeros((HALF, HALF), F32)], axis=1)
    a = [
        jnp.where(lane == sub + ROWS * g + HALF, 1.0, wide[ROWS * g : ROWS * g + ROWS])
        for g in range(groups)
    ]
    rows = [None] * HALF
    for j in range(0, HALF, width):
        gj, o = j // ROWS, j % ROWS
        cols = {g: [full(a[g][:, j + i : j + i + 1]) for i in range(width)] for g in range(gj, groups)}
        s = [
            [full(cols[gj][k][o + i : o + i + 1, :]) if k <= i else None for k in range(width)]
            for i in range(width)
        ]
        u = [full(a[gj][o + i : o + i + 1, :]) for i in range(width)]
        inv = [None] * width
        low = [[None] * width for _ in range(width)]
        for k in range(width):
            inv[k] = lax.rsqrt(s[k][k])
            for i in range(k + 1, width):
                low[i][k] = s[i][k] * inv[k]
            for i in range(k + 1, width):
                for q in range(k + 1, i + 1):
                    s[i][q] = s[i][q] - low[i][k] * low[q][k]
        for i in range(width):
            for k in range(i):
                u[i] = u[i] - low[i][k] * u[k]
            u[i] = u[i] * inv[i]
            rows[j + i] = u[i]
        for g in range(gj if o + width < ROWS else gj + 1, groups):
            c = cols[g]
            for i in range(width):
                for k in range(i):
                    c[i] = c[i] - c[k] * low[i][k]
                c[i] = c[i] * inv[i]
            for i in range(width):
                a[g] = a[g] - c[i] * u[i]
    out = []
    for g in range(groups):
        v = rows[ROWS * g]
        for i in range(1, ROWS):
            v = jnp.where(sub == i, rows[ROWS * g + i], v)
        out.append(v)
    both = jnp.concatenate(out, axis=0)
    return both[:, :HALF], both[:, HALF:]


def factor(a, low, inv, tiles, width, start=0, stop=None):
    stop = tiles if stop is None else stop
    d = a[start * TILE : (start + 1) * TILE, start * TILE : (start + 1) * TILE]
    zero = jnp.zeros((HALF, HALF), F32)
    ri = lax.broadcasted_iota(jnp.int32, (HALF, HALF), 0)
    ci = lax.broadcasted_iota(jnp.int32, (HALF, HALF), 1)
    for k in range(start, stop):
        k0, k1, k2 = k * TILE, (k + 1) * TILE, (k + 2) * TILE
        u1, w1 = factor_half(d[:HALF, :HALF], width)
        l21 = mul(d[HALF:, :HALF], w1, NT)
        u2, w2 = factor_half(d[HALF:, HALF:] - mul(l21, l21, NT), width)
        w21 = -mul(w2, mul(l21, w1, NN), NN)
        w = jnp.concatenate([jnp.concatenate([w1, zero], 1), jnp.concatenate([w21, w2], 1)], 0)
        ws = split(w)
        inv[k0:k1, k0:k1] = w
        if k + 1 < tiles:
            p = dot3(split(a[k1:k2, k0:k1]), ws, NT)
            low[k1:k2, k0:k1] = p
            ps = split(p)
            d = a[k1:k2, k1:k2] - dot3(ps, ps, NT)
        l1 = jnp.where(ri >= ci, u1.T, 0.0)
        l2 = jnp.where(ri >= ci, u2.T, 0.0)
        low[k0:k1, k0:k1] = jnp.concatenate(
            [jnp.concatenate([l1, zero], 1), jnp.concatenate([l21, l2], 1)], 0
        )
        if k + 2 < tiles:
            low[k2:, k0:k1] = dot3(split(a[k2:, k0:k1]), ws, NT)
            for j in range(k + 1, tiles):
                j0 = j * TILE
                top = max(j0, k2)
                a[top:, j0 : j0 + TILE] = a[top:, j0 : j0 + TILE] - mul(
                    low[top:, k0:k1], low[j0 : j0 + TILE, k0:k1], NT
                )
        if k > 0:
            x = mul(low[k0:k1, 0:k0], inv[0:k0, 0:k0], NN)
            inv[k0:k1, 0:k0] = -dot3(ws, split(x), NN)
        if k + 1 < tiles:
            rest = jnp.zeros((TILE, (tiles - k - 1) * TILE), F32)
            low[k0:k1, k1:] = rest
            inv[k0:k1, k1:] = rest
    if stop < tiles:
        a[k1:k2, k1:k2] = d


def padded(a, tile_of, live, tiles):
    ri = lax.broadcasted_iota(jnp.int32, (TILE, TILE), 0)
    ci = lax.broadcasted_iota(jnp.int32, (TILE, TILE), 1)
    eye = jnp.where(ri == ci, 1.0, 0.0)
    for i in range(tiles):
        kept = (jnp.int32(i) < live).astype(F32)
        for j in range(i + 1):
            value = tile_of(i, j) * kept
            if i == j:
                value = value + eye * (1.0 - kept)
            a[i * TILE : (i + 1) * TILE, j * TILE : (j + 1) * TILE] = value


def copy_all(pairs, sems):
    copies = [pltpu.make_async_copy(src, dst, sems.at[n]) for n, (src, dst) in enumerate(pairs)]
    for c in copies:
        c.start()
    for c in copies:
        c.wait()


def tile_at(ref, row, col):
    return ref.at[
        pl.ds(pl.multiple_of(row * TILE, TILE), TILE), pl.ds(pl.multiple_of(col * TILE, TILE), TILE)
    ]


def square_index():
    return (
        lax.broadcasted_iota(jnp.int32, (TILE, TILE), 0),
        lax.broadcasted_iota(jnp.int32, (TILE, TILE), 1),
    )


def put_pairs(tiles_in, out, first):
    r, c = square_index()
    diagonals = []
    for n in range(0, len(tiles_in), 2):
        mixed = tiles_in[n]
        if n + 1 < len(tiles_in):
            mixed = jnp.where(r >= c, mixed, tiles_in[n + 1])
            diagonals.append(jnp.sum(jnp.where(r == c, tiles_in[n + 1], 0.0), axis=0, keepdims=True))
        out[pl.ds((first + n // 2) * TILE, TILE), :] = mixed
    diagonals += [jnp.zeros((1, TILE), F32)] * (ROWS - len(diagonals))
    out[pl.ds((first + (len(tiles_in) + 1) // 2) * TILE, ROWS), :] = jnp.concatenate(diagonals, axis=0)


def get_pairs(ref, first, count):
    r, c = square_index()
    base = (first + (count + 1) // 2) * TILE
    out = []
    for n in range(0, count, 2):
        mixed = ref[(first + n // 2) * TILE : (first + n // 2 + 1) * TILE, :]
        if n + 1 == count:
            out.append(mixed)
            continue
        other = mixed.T
        out.append(jnp.where(r >= c, mixed, other))
        diagonal = ref[base + n // 2 : base + n // 2 + 1, :]
        out.append(jnp.where(r == c, diagonal, jnp.where(r < c, mixed, other)))
    return out


def message_tile(ref, n):
    return ref[pl.ds(pl.multiple_of(n * TILE, TILE), TILE), :]


def pack_first(tab, block, pivot, out, square, sems):
    side = tab[CT]
    pairs = []
    for n, (a, b) in enumerate(BELOW_C):
        pairs.append((tile_at(block, tab[a], tab[b]), out.at[pl.ds(n * TILE, TILE)]))
    first = len(BELOW_C)
    for n, (a, b) in enumerate(BELOW_P):
        pairs.append(
            (tile_at(pivot, a, side * (P1T // 2) + b), out.at[pl.ds((first + n) * TILE, TILE)])
        )
    for a in range(CT):
        pairs.append((tile_at(block, tab[a], tab[a]), square.at[a]))
    for a in range(P1T // 2):
        pairs.append((tile_at(pivot, a, side * (P1T // 2) + a), square.at[CT + a]))
    copy_all(pairs, sems)
    put_pairs([square[n] for n in range(DIAG_FIRST)], out, first + len(BELOW_P))


def pack_rest(
    tab, block, pivot, rows, pivot_second, second,
    coup, own, kept, cross, off, coup_two, units, units_sent, main, two_sent_a, two_sent_b, over,
    two_over, strips, sems,
):
    side = tab[CT]
    order = CT + 1
    local = order + CT
    quarter = tab[local + U1T]
    pairs = []
    for r in range(HALF_U):
        row = tab[local + r] - side * HALF_U
        for c in range(P1T):
            pairs.append((tile_at(rows, row, c), coup.at[r * P1T + c]))
    for n, (a, b) in enumerate(TRI_U):
        row = tab[local + a] - side * HALF_U
        pairs.append((tile_at(rows, row, P1T + tab[local + b]), own.at[n]))
    for n, (a, b) in enumerate(TRI_C):
        pairs.append((tile_at(block, tab[order + a], tab[order + b]), kept.at[n]))
    for i in range(HALF_U):
        row = tab[local + i] - side * HALF_U
        for k in range(HALF_U):
            pairs.append(
                (tile_at(rows, row, P1T + tab[local + HALF_U + k]), cross.at[i * HALF_U + k])
            )
    for i in range(P1T // 2):
        for k in range(P1T // 2):
            pairs.append(
                (tile_at(pivot, i, (1 - side) * (P1T // 2) + k), off.at[i * (P1T // 2) + k])
            )
    for n, (i, k) in enumerate(TRI_P):
        pairs.append((tile_at(pivot, i, side * (P1T // 2) + k), off.at[N_OFF + n]))
    for r in range(QUARTER):
        for c in range(P2T):
            pairs.append((tile_at(second, r, c), coup_two.at[r * P2T + c]))
    first = local + U1T + 1
    for p in range(N_COUP):
        n = tab[first + p]
        row = tab[local + n // P1T] - side * HALF_U
        sent = main.at[p] if p < N_MAIN else over.at[p - N_MAIN]
        pairs.append((tile_at(rows, row, n % P1T), sent))
    first += N_COUP
    for p in range(N_TWO):
        n = tab[first + p]
        if p < N_TWO_A:
            sent = two_sent_a.at[p]
        elif p < N_TWO_A + N_TWO_B:
            sent = two_sent_b.at[p - N_TWO_A]
        else:
            sent = two_over.at[p - N_TWO_A - N_TWO_B]
        pairs.append((tile_at(second, n // P2T, n % P2T), sent))
    far = []
    for i in range(OWN_UNITS):
        for d in range(REACH):
            col = (quarter * OWN_UNITS + i - d + UNITS) % UNITS
            far.append(col % 2)
            source = pivot_second.at[
                pl.ds(i * HALF, HALF), pl.ds(pl.multiple_of(col // 2 * TILE, TILE), TILE)
            ]
            pairs.append((source, strips.at[i * REACH + d]))
    copy_all(pairs, sems)
    lane = lax.broadcasted_iota(jnp.int32, (HALF, TILE), 1)

    def placed(n, half):
        strip = strips[n]
        return jnp.where(far[n] == half, strip, pltpu.roll(strip, HALF, 1))

    for n in range(N_WIDE):
        strip = placed(2 * n, 0)
        if 2 * n + 1 < N_UNIT:
            strip = jnp.where(lane < HALF, strip, placed(2 * n + 1, 1))
        units[n * HALF : (n + 1) * HALF, :] = strip
        units_sent[n * HALF : (n + 1) * HALF, :] = strip


def after(array, *others):
    def kernel(*refs):
        pass

    return pl.pallas_call(
        kernel,
        out_shape=jax.ShapeDtypeStruct(array.shape, array.dtype),
        in_specs=[HBM] * (1 + len(others)),
        out_specs=HBM,
        input_output_aliases={0: 0},
        name="after",
        cost_estimate=CHEAP,
    )(array, *others)


def part_of(array):
    return array[(0,) * (array.ndim - 2)][:ROWS]


T_SIDE = 0
T_LIVE = 1
T_LOCAL = 2
T_FILL = T_LOCAL + U1T
T_SLOT = T_FILL + U1T * P1T
T_SLOT_FAR = T_SLOT + CT * CT
T_PLACE = T_SLOT_FAR + CT * CT


def panel_rows(tile_of, count, live, parts, put):
    for r in range(0, count, 2):
        block = jnp.concatenate(
            [
                jnp.concatenate([tile_of(r + i, c) for c in range(P1T)], axis=1)
                for i in range(2)
            ],
            axis=0,
        )
        lane = lax.broadcasted_iota(jnp.int32, block.shape, 1)
        block = jnp.where(lane < live * TILE, block, 0.0)
        put(r, times_inverse(block, parts))


def first_kernel(
    tab, mine, theirs, coup, own, cross, off,
    lower_out, inv_high, inv_low, panel_high, panel_low, rows_out, own_out, own_sent, far_out,
    front, a, low, inv, sem,
):
    side = tab[T_SIDE]
    live = tab[T_LIVE]
    half = P1T // 2
    square = get_pairs(theirs, len(BELOW_C) + len(BELOW_P), DIAG_FIRST)
    front[0:N_PIV] = jnp.zeros((N_PIV, TILE, TILE), F32)
    for n, (i, k) in enumerate(TRI_P):
        front[(side * half + i) * P1T + side * half + k] = off[N_OFF + n]
        if i == k:
            tile = square[CT + i]
        else:
            tile = message_tile(theirs, len(BELOW_C) + BELOW_P.index((i, k)))
        front[((1 - side) * half + i) * P1T + (1 - side) * half + k] = tile
    for i in range(half):
        for k in range(half):

            @pl.when(side == 0)
            def _():
                front[(half + k) * P1T + i] = off[i * half + k].T

            @pl.when(side != 0)
            def _():
                front[(half + i) * P1T + k] = off[i * half + k]

    def scale(n, carry):
        front[S_COUP + n] = coup[n] * tab[T_FILL + n].astype(F32)
        front[S_FAR + n] = jnp.zeros((TILE, TILE), F32)
        front[S_CROSS + n] = cross[n]
        return carry

    lax.fori_loop(0, N_COUP, scale, 0)

    def copy(n, carry):
        front[S_OWN + n] = own[n]
        front[S_OTH + n] = jnp.zeros((TILE, TILE), F32)
        return carry

    lax.fori_loop(0, N_TRI, copy, 0)
    for i in range(CT):

        def extend(k, carry, i=i):
            here = tab[T_SLOT + i * CT + k]
            front[here] = front[here] + mine[tri(i, 0) + k]
            return carry

        lax.fori_loop(0, i + 1, extend, 0)

        def extend_far(k, carry, i=i):
            there = tab[T_SLOT_FAR + i * CT + k]
            front[there] = front[there] + message_tile(theirs, i * (i - 1) // 2 + k)
            return carry

        lax.fori_loop(0, i, extend_far, 0)
        there = tab[T_SLOT_FAR + i * CT + i]
        front[there] = front[there] + square[i]
    leave = pltpu.make_async_copy(front.at[pl.ds(S_FAR, S_OTH - S_FAR)], far_out, sem)
    leave.start()
    padded(a, lambda i, j: front[i * P1T + j], live, P1T)
    factor(a, low, inv, P1T, 4)
    inv_high[...], inv_low[...] = split(inv[...])
    lower_out[...] = low[pl.ds(pl.multiple_of(side * (PIVOT // 2), TILE), PIVOT // 2), :]

    def put(r, rows):
        wide = slice(r * TILE, (r + 2) * TILE)
        panel_high[wide, :], panel_low[wide, :] = split(rows)
        for i in range(2):
            place = tab[T_LOCAL + r + i] - side * HALF_U
            rows_out[pl.ds(pl.multiple_of(place * TILE, TILE), TILE), :] = rows[
                i * TILE : (i + 1) * TILE
            ]

    panel_rows(lambda r, c: front[S_COUP + r * P1T + c], HALF_U, live, (inv_high[...], inv_low[...]), put)
    for i in range(HALF_U):
        left = [p[i * TILE : (i + 1) * TILE, :] for p in (panel_high, panel_low)]
        right = [p[0 : (i + 1) * TILE, :] for p in (panel_high, panel_low)]
        product = dot3(left, right, NT)
        for k in range(i + 1):
            n = S_OWN + tri(i, k)
            front[n] = front[n] - product[:, k * TILE : (k + 1) * TILE]
    put_own([front[S_OWN + n] for n in range(N_TRI)], own_out)
    put_own([front[S_OWN + n] for n in range(N_TRI)], own_sent)
    leave.wait()


def choose(at, parts):
    value = None
    base = sum(count for _, _, count in parts)
    for ref, first, count in reversed(parts):
        base -= count
        tile = ref[first + jnp.clip(at - base, 0, count - 1)]
        value = tile if value is None else jnp.where(at < base + count, tile, value)
    return value


def second_kernel(
    which, tab, far, main, over, inv_high, inv_low, panel_high, panel_low, cross,
    rows_far, cross_far, sems,
):
    wide = HALF_U // 2
    copies = [(far.at[pl.ds(which * wide * P1T, wide * P1T)], rows_far)]
    for i in range(HALF_U):
        copies.append(
            (
                far.at[pl.ds(N_COUP + i * HALF_U + which * wide, wide)],
                cross_far.at[pl.ds(i * wide, wide)],
            )
        )
    copies = [pltpu.make_async_copy(src, dst, sems.at[n]) for n, (src, dst) in enumerate(copies)]
    for c in copies:
        c.start()
    live = tab[T_LIVE]
    parts = inv_high[...], inv_low[...]

    def tile_of(r, c):
        n = (which * wide + r) * P1T + c
        tile = choose(tab[T_PLACE + n], [(main, 0, N_MAIN), (over, 0, N_OVER)])
        return rows_far[r * P1T + c] + tile * tab[T_FILL + N_COUP + n].astype(F32)

    for c in copies:
        c.wait()
    block = jnp.concatenate(
        [jnp.concatenate([tile_of(r, c) for c in range(P1T)], axis=1) for r in range(wide)], axis=0
    )
    lane = lax.broadcasted_iota(jnp.int32, block.shape, 1)
    block = jnp.where(lane < live * TILE, block, 0.0)
    right = split(times_inverse(block, parts))
    for i in range(0, HALF_U, 2):
        left = [p[i * TILE : (i + 2) * TILE, :] for p in (panel_high, panel_low)]
        product = dot3(left, right, NT)
        for q in range(2):
            for k in range(wide):
                n = (i + q) * wide + k
                cross[n] = (
                    cross_far[n] - product[q * TILE : (q + 1) * TILE, k * TILE : (k + 1) * TILE]
                )


def put_own(block, out):
    for n, (a, b) in enumerate(BELOW_U):
        out[n * TILE : (n + 1) * TILE, :] = block[tri(a, b)]
    put_pairs([block[tri(a, a)] for a in range(HALF_U)], out, len(BELOW_U))


def get_own(ref, out):
    for n, (i, k) in enumerate(BELOW_U):
        out[tri(i, k)] = message_tile(ref, n)
    for i, tile in enumerate(get_pairs(ref, len(BELOW_U), HALF_U)):
        out[tri(i, i)] = tile


Q_LIVE = 0
Q_MINE = 1
Q_FILL = 5
Q_DIRECT = Q_FILL + U2T * P2T
Q_TURNED = Q_DIRECT + 2 * U1T * U1T
Q_PLACE = Q_TURNED + 2 * U1T * U1T


def extend_cross(tab, ref, g, front, which):
    wide = HALF_U // 2
    extend_two(tab, ref, g, front, 0, HALF_U + which * wide, False, 0, G_NONE, wide)


def extend_two(tab, ref, g, front, rows, cols, triangle, low, high, wide=HALF_U):
    for i in range(HALF_U):

        def one(k, carry, i=i):
            at = front * U1T * U1T + (rows + i) * U1T + cols + k
            n = (tri(i, 0) if triangle else i * wide) + k
            direct = tab[Q_DIRECT + at]
            turned = tab[Q_TURNED + at]

            @pl.when((direct >= low) & (direct < high))
            def _():
                g[direct - low] = g[direct - low] + ref[n]

            @pl.when((turned >= low) & (turned < high))
            def _():
                g[turned - low] = g[turned - low] + ref[n].T

            return carry

        lax.fori_loop(0, i + 1 if triangle else wide, one, 0)


def add_units(tab, g, units, s):
    lane = lax.broadcasted_iota(jnp.int32, (HALF, TILE), 1)
    for i in range(OWN_UNITS):
        row = tab[Q_MINE + s] * OWN_UNITS + i
        for d in range(REACH):
            n = i * REACH + d
            col = (row - d + UNITS) % UNITS
            strip = units[n // 2 * HALF : (n // 2 + 1) * HALF, :]
            here = n % 2

            def add(r, c, block):
                slot = r // 2 * P2T + c // 2
                start = pl.multiple_of(r % 2 * HALF, HALF)
                old = g[slot, pl.ds(start, HALF), :]
                g[slot, pl.ds(start, HALF), :] = old + jnp.where(lane // HALF == c % 2, block, 0.0)

            @pl.when((col <= row) & ((d < REACH - 1) | (row >= UNITS // 2)))
            def _():
                add(row, col, jnp.where(col % 2 == here, strip, pltpu.roll(strip, HALF, 1)))

            if d < REACH - 1 and d > 0:

                @pl.when(col > row)
                def _():
                    turned = strip.T[here * HALF : (here + 1) * HALF, :]
                    add(col, row, jnp.concatenate([turned, turned], axis=1))


def third_kernel(tab, own0, units0, units2, second, g, block):
    def clear(n, carry):
        g[n] = jnp.zeros((TILE, TILE), F32)
        return carry

    lax.fori_loop(0, G_TRAIL, clear, 0)
    for r in range(QUARTER):
        for c in range(U2T):
            g[G_TRAIL + r * U2T + c] = second[
                r * TILE : (r + 1) * TILE, SECOND + c * TILE : SECOND + (c + 1) * TILE
            ]
    add_units(tab, g, units0, 0)
    add_units(tab, g, units2, 2)
    get_own(own0, block)
    extend_two(tab, block, g, 0, 0, 0, True, 0, G_NONE)


def more_kernel(
    tab, part, own1, cross0_a, cross0_b, cross1_a, cross1_b, oth0, units1, g, block, sem
):
    enter = pltpu.make_async_copy(part, g, sem)
    enter.start()
    get_own(oth0, block)
    enter.wait()
    add_units(tab, g, units1, 1)
    extend_cross(tab, cross0_a, g, 0, 0)
    extend_cross(tab, cross0_b, g, 0, 1)
    extend_cross(tab, cross1_a, g, 1, 0)
    extend_cross(tab, cross1_b, g, 1, 1)
    extend_two(tab, block, g, 0, HALF_U, HALF_U, True, 0, G_NONE)
    get_own(own1, block)
    extend_two(tab, block, g, 1, 0, 0, True, 0, G_NONE)


def pivot_kernel(tab, part, oth1, units3, lower_out, high_out, rest_out, g, other, a, low, inv, sem):
    enter = pltpu.make_async_copy(part.at[pl.ds(0, G_COUP)], g, sem)
    enter.start()
    get_own(oth1, other)
    enter.wait()
    add_units(tab, g, units3, 3)
    extend_two(tab, other, g, 1, HALF_U, HALF_U, True, 0, G_COUP)
    padded(a, lambda i, j: g[i * P2T + j], tab[Q_LIVE], P2T)
    factor(a, low, inv, P2T, 8)
    start = tab[Q_MINE] * (SECOND // 4)
    lower_out[...] = low[pl.ds(pl.multiple_of(start, HALF), SECOND // 4), :]
    high_out[...], rest_out[...] = split(inv[...])


def quarter_rows_of(tab, g, quarter):
    return jnp.concatenate(
        [
            jnp.concatenate([g[(quarter * QUARTER + r) * P2T + c] for c in range(P2T)], axis=1)
            for r in range(QUARTER)
        ],
        axis=0,
    )


def placed_two(tab, which, first, second, over):
    parts = [
        (first, 0, N_TWO_A),
        (second, 0, N_TWO_B),
        (over, 0, N_TWO_OVER),
    ]
    return lambda n: choose(tab[Q_PLACE + which * N_TWO + n], parts)


def quarter_panel(tab, block, coup, parts, quarter):
    rows = []
    for r in range(QUARTER):
        fill = Q_FILL + (quarter * QUARTER + r) * P2T
        rows.append(
            jnp.concatenate(
                [coup(r * P2T + c) * tab[fill + c].astype(F32) for c in range(P2T)], axis=1
            )
        )
    block = block + jnp.concatenate(rows, axis=0)
    lane = lax.broadcasted_iota(jnp.int32, block.shape, 1)
    block = jnp.where(lane < tab[Q_LIVE] * TILE, block, 0.0)
    return times_inverse(block, parts)


WIDE = QUARTER * TILE


def fetch(pairs, sems):
    copies = [pltpu.make_async_copy(src, dst, sems.at[n]) for n, (src, dst) in enumerate(pairs)]
    for c in copies:
        c.start()
    return copies


def rows_kernel(
    tab, part, oth1, high_in, low_in, coup0_in, coup1_a_in, coup1_b_in, over_in, coup2_in,
    panel_out, schur_out, rest_out,
    g, oth, high, low, coup0, coup1_a, coup1_b, over, coup2, other, panels, sems,
):
    copies = fetch(
        [
            (oth1, oth),
            (part.at[pl.ds(G_COUP, G_NONE - G_COUP)], g),
            (coup0_in, coup0),
            (high_in, high),
            (low_in, low),
            (coup1_a_in, coup1_a),
            (coup1_b_in, coup1_b),
            (over_in, over),
            (coup2_in, coup2),
        ],
        sems,
    )
    copies[0].wait()
    get_own(oth, other)
    copies[1].wait()
    extend_two(tab, other, g, 1, HALF_U, HALF_U, True, G_COUP, G_NONE)
    rest_out[...] = quarter_rows_of(tab, g, tab[Q_MINE + 3])
    for c in copies[2:]:
        c.wait()
    parts = high[...], low[...]
    whole = [lambda n, ref=ref: ref[n] for ref in (coup0, coup2)]
    for s, coup in enumerate((whole[0], placed_two(tab, 0, coup1_a, coup1_b, over), whole[1])):
        quarter = tab[Q_MINE + s]
        panel = quarter_panel(tab, quarter_rows_of(tab, g, quarter), coup, parts, quarter)
        panels[s] = panel
        if s == 0:
            panel_out[...] = panel
    left = split(panel_out[...])
    for s in range(4):
        quarter = tab[Q_MINE + s]
        if s < 3:
            product = dot3(left, split(panels[s]), NT)
        for r in range(QUARTER):
            for c in range(QUARTER):
                tile = g[G_TRAIL - G_COUP + r * U2T + quarter * QUARTER + c]
                if s < 3:
                    tile = tile - product[r * TILE : (r + 1) * TILE, c * TILE : (c + 1) * TILE]
                col = pl.multiple_of((quarter * QUARTER + c) * TILE, TILE)
                schur_out[r * TILE : (r + 1) * TILE, pl.ds(col, TILE)] = tile


def last_kernel(
    tab, schur, rest_in, panel_in, high_in, low_in, coup_a_in, coup_b_in, over_in,
    out,
    block, rest, panel, high, low, coup_a, coup_b, over, sems, sem,
):
    quarter = tab[Q_MINE + 3]
    col = pl.ds(pl.multiple_of(quarter * WIDE, TILE), WIDE)
    copies = fetch(
        [
            (rest_in, rest),
            (coup_a_in, coup_a),
            (coup_b_in, coup_b),
            (over_in, over),
            (high_in, high),
            (low_in, low),
            (panel_in, panel),
            (schur.at[:, col], block),
        ],
        sems,
    )
    for c in copies[:6]:
        c.wait()
    coup = placed_two(tab, 1, coup_a, coup_b, over)
    other = quarter_panel(tab, rest[...], coup, (high[...], low[...]), quarter)
    for c in copies[6:]:
        c.wait()
    block[...] = block[...] - dot3(split(panel[...]), split(other), NT)
    leave = pltpu.make_async_copy(block, out.at[:, col], sem)
    leave.start()
    leave.wait()


def swap(array, axis):
    size = lax.axis_size(axis)
    return lax.ppermute(array, axis, [(i, i ^ (size // 2)) for i in range(size)])


def tiles(count):
    return jax.ShapeDtypeStruct((count, TILE, TILE), F32)


def halved(rows):
    return jax.ShapeDtypeStruct((rows, PIVOT), jnp.bfloat16)


def dense(rows, cols):
    return jax.ShapeDtypeStruct((rows, cols), F32)


SMEM = pl.BlockSpec(memory_space=pltpu.SMEM)
VMEM = pl.BlockSpec(memory_space=pltpu.VMEM)
HBM = pl.BlockSpec(memory_space=pl.ANY)
LIMIT = 60 << 20
CHEAP = pl.CostEstimate(flops=1, bytes_accessed=1, transcendentals=0)


def call(kernel, name, out_shape, in_specs, out_specs, scratch=(), waits=(), limit=LIMIT, **options):
    count = len(in_specs)

    def body(*refs):
        kernel(*refs[:count], *refs[count + len(waits) :])

    run = pl.pallas_call(
        body,
        out_shape=out_shape,
        in_specs=in_specs + [HBM] * len(waits),
        out_specs=out_specs,
        scratch_shapes=list(scratch),
        name=name,
        compiler_params=pltpu.CompilerParams(vmem_limit_bytes=limit),
        cost_estimate=CHEAP,
        **options,
    )
    return lambda *args: run(*args, *waits)


def tri(i, k):
    return i * (i + 1) // 2 + k


def local_order(second_map, side):
    unit = jnp.arange(U1T, dtype=jnp.int32)
    rank = second_map + jnp.where(unit // HALF_U == side, 0, P2T + U2T)
    place = jnp.sum((rank[None, :] < rank[:, None]).astype(jnp.int32), axis=1)
    hit = (place[None, :] == unit[:, None]).astype(jnp.int32)
    return place, hit


def place_of(child_map, place):
    unit = jnp.arange(U1T, dtype=jnp.int32)
    hit = (child_map[:, None] - P1T == unit[None, :]).astype(jnp.int32)
    return jnp.where(child_map < P1T, child_map, P1T + jnp.sum(hit * place[None, :], axis=1))


def sort_by(key):
    spot = jnp.sum((key[None, :] < key[:, None]).astype(jnp.int32), axis=1)
    hit = (spot[None, :] == jnp.arange(CT, dtype=jnp.int32)[:, None]).astype(jnp.int32)
    order = jnp.sum(hit * jnp.arange(CT, dtype=jnp.int32)[None, :], axis=1)
    return order, jnp.sum(hit * key[None, :], axis=1)


def turned_key(key):
    return jnp.where(key < P1T, key, P1T + (key - P1T + HALF_U) % U1T)


def slots(keys):
    row = keys[:, None]
    col = keys[None, :]
    own = P1T + HALF_U
    pivot = row * P1T + col
    coup = jnp.where(row >= own, S_COUP + (row - own) * P1T, S_FAR + (row - P1T) * P1T) + col
    near = S_OWN + tri(row - own, col - own)
    cross = S_CROSS + (row - own) * HALF_U + col - P1T
    other = S_OTH + tri(row - P1T, col - P1T)
    rest = jnp.where(row < own, other, jnp.where(col < own, cross, near))
    return jnp.where(row < P1T, pivot, jnp.where(col < P1T, coup, rest)).reshape(-1)


def needed_first(need):
    need = need.reshape(-1)
    count = need.shape[0]
    at = jnp.arange(count, dtype=jnp.int32)
    key = at + jnp.where(need > 0, 0, count)
    place = jnp.sum((key[None, :] < key[:, None]).astype(jnp.int32), axis=1)
    order = jnp.sum((place[None, :] == at[:, None]).astype(jnp.int32) * at[None, :], axis=1)
    return place, order


def needed(fill, live):
    return fill * (jnp.arange(fill.shape[-1], dtype=jnp.int32) < live[..., None, None])


def targets(goal, quarter):
    row = goal[:, None]
    col = goal[None, :]

    def index(r, c):
        mine = (r - P2T) // QUARTER == quarter
        coup = G_COUP + (r - P2T) * P2T + c
        trail = G_TRAIL + (r - P2T - quarter * QUARTER) * U2T + c - P2T
        rest = jnp.where(c < P2T, coup, jnp.where(mine, trail, G_NONE))
        return jnp.where(r < P2T, jnp.where((c < P2T) & (r >= c), r * P2T + c, G_NONE), rest)

    direct = index(row, col)
    turned = jnp.where(row == col, G_NONE, index(col, row))
    return direct.reshape(-1), turned.reshape(-1)


def body(
    contribution,
    pivot_one,
    rows_one,
    pivot_two,
    rows_two,
    map_one,
    map_two,
    fill_one,
    fill_two,
    live_one,
    live_two,
):
    size_lo = lax.axis_size("lo")
    size_hi = lax.axis_size("hi")
    half_lo = size_lo // 2
    half_hi = size_hi // 2
    index_lo = lax.axis_index("lo")
    index_hi = lax.axis_index("hi")
    side_lo = index_lo // half_lo
    side_hi = index_hi // half_hi
    front_lo = index_lo % half_lo
    front_hi = index_hi % half_hi
    far_lo = (index_lo + half_lo) % size_lo
    far_hi = (index_hi + half_hi) % size_hi
    quarter = 2 * side_hi + side_lo
    block, pivot, rows = contribution[0, 0], pivot_one[0, 0], rows_one[0, 0]
    pivot_second, rows_second = pivot_two[0, 0], rows_two[0, 0]

    second_map = map_two[index_hi, front_lo]
    place, hit = local_order(second_map, side_lo)
    key = place_of(map_one[index_hi, index_lo], place)
    order_sent, _ = sort_by(key)
    tab_first = jnp.concatenate([order_sent, side_lo[None]]).astype(jnp.int32)
    sent = call(
        pack_first,
        "pack_first",
        dense(N_FIRST * TILE + ROWS, TILE),
        [SMEM, HBM, HBM],
        VMEM,
        [
            pltpu.VMEM((DIAG_FIRST, TILE, TILE), F32),
            pltpu.SemaphoreType.DMA((len(TRI_C) + len(TRI_P),)),
        ],
    )(tab_first, block, pivot)
    got_first = swap(sent, "lo")

    unit = jnp.arange(U1T, dtype=jnp.int32)
    local = jnp.sum(hit * unit[None, :], axis=1)
    order_kept, keys = sort_by(turned_key(key))
    live_first = live_one[index_hi, front_lo]
    need_first = needed(
        jnp.sum(hit[:, :, None] * fill_one[index_hi, front_lo][None, :, :], axis=1), live_first
    )
    live_second = live_two[front_hi, front_lo]
    need_second = needed(fill_two[front_hi, front_lo], live_second)

    def place_second(which):
        return needed_first(
            lax.dynamic_slice_in_dim(need_second, which * QUARTER, QUARTER, 0)
        )

    _, order_main = needed_first(need_first[:HALF_U])
    _, order_two = place_second(quarter)
    tab_rest = jnp.concatenate(
        [tab_first, order_kept, local, quarter[None], order_main, order_two]
    ).astype(jnp.int32)
    shapes = [
        tiles(N_COUP), tiles(N_TRI), tiles(len(TRI_C)), tiles(N_CROSS), tiles(N_OFF + len(TRI_P)),
        tiles(N_TWO),
        dense(N_WIDE * HALF, TILE), dense(N_WIDE * HALF, TILE),
        tiles(N_MAIN), tiles(N_TWO_A), tiles(N_TWO_B), tiles(N_OVER),
        tiles(N_TWO_OVER),
    ]
    n_rest = 2 * N_COUP + N_TRI + len(TRI_C) + N_CROSS + N_OFF + len(TRI_P) + 2 * N_TWO + N_UNIT
    coup, own, kept, cross, off, two, units, units_sent, main, two_a, two_b, over, two_over = call(
        pack_rest,
        "pack_rest",
        shapes,
        [SMEM] + [HBM] * 5,
        [VMEM] * len(shapes),
        [pltpu.VMEM((N_UNIT, HALF, TILE), F32), pltpu.SemaphoreType.DMA((n_rest,))],
        waits=(sent,),
    )(tab_rest, block, pivot, rows, pivot_second, rows_second)
    two_hi = swap(two, "hi")
    units_hi = swap(units, "hi")
    far_key = place_of(map_one[index_hi, far_lo], place)
    _, far_keys = sort_by(turned_key(far_key))
    place_main, _ = needed_first(need_first[HALF_U:])
    tab_one = jnp.concatenate(
        [side_lo[None], live_first[None], local, need_first.reshape(-1), slots(keys), slots(far_keys), place_main]
    ).astype(jnp.int32)
    map_far = map_two[far_hi, front_lo]
    _, hit_far = local_order(map_far, side_lo)
    direct, turned = targets(jnp.sum(hit * second_map[None, :], axis=1), quarter)
    direct_far, turned_far = targets(jnp.sum(hit_far * map_far[None, :], axis=1), quarter)
    place_lo, _ = place_second(2 * side_hi + 1 - side_lo)
    place_both, _ = place_second(2 * (1 - side_hi) + 1 - side_lo)
    quarters = jnp.stack(
        [quarter, 2 * side_hi + 1 - side_lo, 2 * (1 - side_hi) + side_lo, 2 * (1 - side_hi) + 1 - side_lo]
    )
    tab_two = jnp.concatenate(
        [
            live_second[None], quarters, need_second.reshape(-1),
            direct, direct_far, turned, turned_far, place_lo, place_both,
        ]
    ).astype(jnp.int32)
    most = jnp.max(jnp.sum(needed(fill_one, live_one).reshape(-1, N_COUP), axis=1))
    most_two = jnp.max(jnp.sum(needed(fill_two, live_two).reshape(-1, N_TWO), axis=1))

    limits = jnp.stack([most, most_two])
    main = after(main, part_of(got_first), two_hi, units_hi, tab_one, tab_two, limits)
    got_main = swap(main, "lo")

    half_rows = HALF_U * TILE
    message = dense(N_OWN * TILE + ROWS, TILE)
    lower_one, inv_a, inv_b, panel_a, panel_b, panel_one, s_own, own_sent, far_part = call(
        first_kernel,
        "first_front_own",
        [
            dense(PIVOT // 2, PIVOT), *[halved(PIVOT)] * 2, *[halved(half_rows)] * 2,
            dense(half_rows, PIVOT), message, message, tiles(N_CROSS + N_COUP),
        ],
        [SMEM] + [VMEM] * 6,
        [VMEM] * 8 + [HBM],
        [
            pltpu.VMEM((N_FRONT, TILE, TILE), F32),
            pltpu.VMEM((PIVOT, PIVOT), F32),
            pltpu.VMEM((PIVOT, PIVOT), F32),
            pltpu.VMEM((PIVOT, PIVOT), F32),
            pltpu.SemaphoreType.DMA,
        ],
    )(tab_one, kept, got_first, coup, own, cross, off)
    s_own_far = swap(s_own, "hi")
    block = pltpu.VMEM((N_TRI, TILE, TILE), F32)
    part = call(third_kernel, "second_front_part", tiles(G_NONE), [SMEM] + [VMEM] * 4, VMEM, [block])(
        tab_two, s_own, units, units_hi, rows_second
    )

    def send_two(array):
        got = swap(array, "lo")
        return got, swap(got, "hi")

    over_got = lax.cond(
        limits[0] > N_MAIN, lambda array: swap(array, "lo"), lambda array: array, after(over, part)
    )
    two_over, two_over_both = lax.cond(
        limits[1] > N_TWO_A + N_TWO_B, send_two, lambda array: (array, array), after(two_over, part)
    )
    own_sent = after(own_sent, part_of(got_main), over_got, two_over, two_over_both)
    got_own = swap(own_sent, "lo")


    def cross_of(which, *waits):
        return call(
            functools.partial(second_kernel, which),
            "first_front_other",
            tiles(N_CROSS_A),
            [SMEM, HBM] + [VMEM] * 6,
            VMEM,
            [
                pltpu.VMEM((N_COUP // 2, TILE, TILE), F32),
                pltpu.VMEM((N_CROSS_A, TILE, TILE), F32),
                pltpu.SemaphoreType.DMA((1 + HALF_U,)),
            ],
            waits=waits,
        )(tab_one, far_part, got_main, over_got, inv_a, inv_b, panel_a, panel_b)

    cross_a = cross_of(0, s_own_far, own_sent)
    cross_a_far = swap(cross_a, "hi")
    cross_b = cross_of(1, cross_a)
    cross_b_far = swap(cross_b, "hi")
    got_units = swap(after(units_sent, got_own), "lo")
    s_oth_far = swap(got_own, "hi")
    units_both = swap(got_units, "hi")
    got_two_a = swap(after(two_a, got_units, cross_a_far, cross_b_far), "lo")
    part = call(
        more_kernel,
        "second_front_more",
        tiles(G_NONE),
        [SMEM, HBM] + [VMEM] * 7,
        VMEM,
        [block, pltpu.SemaphoreType.DMA],
    )(tab_two, part, s_own_far, cross_a, cross_b, cross_a_far, cross_b_far, got_own, got_units)
    two_b = after(two_b, got_two_a, units_both, s_oth_far, part)
    got_two_b = swap(two_b, "lo")
    two_a_both = swap(got_two_a, "hi")
    half = jax.ShapeDtypeStruct((SECOND, SECOND), jnp.bfloat16)
    square = pltpu.VMEM((SECOND, SECOND), F32)
    lower_two, inv_high, inv_low = call(
        pivot_kernel,
        "second_front_pivot",
        [dense(SECOND // 4, SECOND), half, half],
        [SMEM, HBM] + [VMEM] * 2,
        [VMEM] * 3,
        [
            pltpu.VMEM((G_COUP, TILE, TILE), F32),
            pltpu.VMEM((N_TRI, TILE, TILE), F32),
            square, square, square,
            pltpu.SemaphoreType.DMA,
        ],
        waits=(two_b,),
    )(tab_two, part, s_oth_far, units_both)
    got_two_b = after(got_two_b, lower_two, two_a_both)
    two_b_both = swap(got_two_b, "hi")
    rows_wide = pltpu.VMEM((WIDE, SECOND), F32)
    halves = [pltpu.VMEM((SECOND, SECOND), jnp.bfloat16)] * 2
    sent_two = [pltpu.VMEM((n, TILE, TILE), F32) for n in (N_TWO_A, N_TWO_B, N_TWO_OVER)]
    whole_two = pltpu.VMEM((N_TWO, TILE, TILE), F32)
    panel_two, schur, rest = call(
        rows_kernel,
        "second_front_rows",
        [dense(WIDE, SECOND), dense(WIDE, U2T * TILE), dense(WIDE, SECOND)],
        [SMEM] + [HBM] * 9,
        [VMEM] * 3,
        [
            pltpu.VMEM((G_NONE - G_COUP, TILE, TILE), F32),
            pltpu.VMEM((N_OWN * TILE + ROWS, TILE), F32),
            *halves,
            whole_two,
            *sent_two,
            whole_two,
            block,
            pltpu.VMEM((3, WIDE, SECOND), F32),
            pltpu.SemaphoreType.DMA((9,)),
        ],
    )(tab_two, part, s_oth_far, inv_high, inv_low, two, got_two_a, got_two_b, two_over, two_hi)
    schur_two = call(
        last_kernel,
        "second_front_last",
        dense(WIDE, U2T * TILE),
        [SMEM] + [HBM] * 8,
        HBM,
        [
            pltpu.VMEM((WIDE, WIDE), F32),
            rows_wide,
            rows_wide,
            *halves,
            *sent_two,
            pltpu.SemaphoreType.DMA((8,)),
            pltpu.SemaphoreType.DMA,
        ],
        input_output_aliases={1: 0},
    )(tab_two, schur, rest, panel_two, inv_high, inv_low, two_a_both, two_b_both, two_over_both)
    return (
        lower_one[None, None],
        panel_one[None, None],
        lower_two[None, None],
        panel_two[None, None],
        schur_two[None, None],
    )


def solution(mesh):
    split_both = P("hi", "lo", None, None)
    return jax.shard_map(
        body,
        mesh=mesh,
        in_specs=(split_both,) * 5 + (P(),) * 6,
        out_specs=(split_both,) * 5,
        check_vma=False,
    )
```
